32 devices in a mesh: fsdp: 16 (over z, y, core), ctx: 2 (over x).
Axes of the slice: x: 2, y: 2, z: 4, core: 2. Of those that a mesh axis runs over, the one named last changes fastest.
Arguments:
- activations: bfloat16 [4096, 1280], P('fsdp', 'ctx'), may hold values from -500 to 500
- norm_gain: float32 [4096], P('fsdp'), may hold values from 0.25 to 1.75
- w_in: bfloat16 [3, 4096, 4096], P(None, 'fsdp'), may hold values from -0.09375 to 0.09375
- w_short: float32 [3, 4096, 3], P(None, 'fsdp'), may hold values from -3.5 to 3.5
- long_filter: bfloat16 [4096, 1280], P('fsdp'), may hold values from -1.1 to 1.1
- skip_gain: float32 [4096], P('fsdp'), may hold values from -4 to 4
- w_out: bfloat16 [4096, 4096], P('fsdp'), may hold values from -0.09375 to 0.09375
Outputs:
- mixer_out: bfloat16 [4096, 1280], P('fsdp', 'ctx')
The draws below stay inside these ranges and needn't reach their ends.
All inputs are finite; a program needn't handle non-finite values.
Results may differ from the reference program's by a relative error of at most 0.035.
Values may be sent and summed in bfloat16 or wider, within the bound.
No kernel may reach another device: no remote copies, remote signals or barrier semaphores. Data moves between devices by JAX's collectives and lax.ppermute only.
A program may use at most 64 MiB of HBM per device.

```python
import jax
import jax.numpy as jnp
from jax import lax

CHANNEL_COUNT = 4096
SHORT = 3
GENOME_LETTERS = 1280


def draw_activations(key, part):
    stochastic_seed_parts = jax.random.split(key, 3)
    row_pos = jnp.arange(CHANNEL_COUNT, dtype=jnp.float32) / max(CHANNEL_COUNT - 1, 1)
    rising = jnp.exp(jnp.log(3.0) * row_pos)
    random_part = jax.random.truncated_normal(stochastic_seed_parts[0], -4.0, 4.0, (CHANNEL_COUNT, GENOME_LETTERS), jnp.float32)
    feature_scale = jnp.exp(jax.random.uniform(stochastic_seed_parts[1], (CHANNEL_COUNT,), jnp.float32, 0.0, jnp.log(10.0)))
    token_scale = jnp.exp(jax.random.uniform(stochastic_seed_parts[2], (GENOME_LETTERS,), jnp.float32, 0.0, jnp.log(10.0)))
    return (random_part * (rising * feature_scale)[:, None] * token_scale[None, :] * 0.25).astype(jnp.bfloat16)


def draw_long_filter(key, part):
    stochastic_seed_parts = jax.random.split(key, 6)
    quick_share = 0.35
    quick_mask = jax.random.bernoulli(stochastic_seed_parts[0], quick_share, (CHANNEL_COUNT,))
    quick_rate = 1.0 / jax.random.uniform(stochastic_seed_parts[1], (CHANNEL_COUNT,), jnp.float32, 30.0, 50.0)
    slow_rate = jnp.exp(jax.random.uniform(stochastic_seed_parts[2], (CHANNEL_COUNT,), jnp.float32, jnp.log(0.2), jnp.log(2.0))) / GENOME_LETTERS
    decay_rate = jnp.where(quick_mask, quick_rate, slow_rate)
    delay_offset_number = jnp.arange(GENOME_LETTERS, dtype=jnp.float32)
    kernel_decay_profile = jnp.exp(-decay_rate[:, None] * delay_offset_number[None, :])
    spike_offset = jax.random.randint(stochastic_seed_parts[3], (CHANNEL_COUNT, 3), 1, GENOME_LETTERS).astype(jnp.float32)
    spike_survives = jax.random.uniform(stochastic_seed_parts[4], (CHANNEL_COUNT, 3), jnp.float32, 0.5, 0.8)
    for spike_segment_number in range(3):
        completed_segments = delay_offset_number[None, :] >= spike_offset[:, spike_segment_number][:, None]
        kernel_decay_profile = kernel_decay_profile * jnp.where(completed_segments, spike_survives[:, spike_segment_number][:, None], 1.0)
    amplitude = jnp.sqrt(2.0 * decay_rate / (1.0 - jnp.exp(-2.0 * decay_rate * GENOME_LETTERS)))
    random_part = jax.random.truncated_normal(stochastic_seed_parts[5], -4.0, 4.0, (CHANNEL_COUNT, GENOME_LETTERS), jnp.float32)
    return (amplitude[:, None] * kernel_decay_profile * random_part).astype(jnp.bfloat16)


def block_levels(own_key, shape, cuts, low, high):
    factor_of, own = 1.0, jax.random.fold_in(own_key, 6)
    for dim, shards_of in cuts:
        draws = jnp.exp(jax.random.uniform(jax.random.fold_in(own, dim), (shards_of,), jnp.float32, low / len(cuts), high / len(cuts)))
        factor_of = factor_of * jnp.repeat(draws, shape[dim] // shards_of).reshape([-1 if axis == dim else 1 for axis in range(len(shape))])
    return factor_of


def centred(stream_key, shape, width, limit, pieces=(), held_as=jnp.bfloat16):
    factor_of = block_levels(stream_key, shape, pieces, -0.22, 0.18) if pieces else 1.0
    result = jax.random.normal(stream_key, shape, jnp.float32) * width * factor_of
    return jnp.minimum(jnp.maximum(result, -limit), limit).astype(held_as)


def setup_inputs(seed: int = 0) -> dict:
    streams_of = jax.random.split(jax.random.key(seed), 8)
    activations = draw_activations(jax.random.fold_in(streams_of[7], 71), 0)
    norm_gain = jnp.clip(1.0 + 0.15 * jax.random.normal(streams_of[1], (CHANNEL_COUNT,), jnp.float32), 0.25, 1.75)
    w_in = centred(streams_of[2], (3, CHANNEL_COUNT, CHANNEL_COUNT), CHANNEL_COUNT ** -0.5, 0.09375, ((1, 16),))
    w_short = centred(streams_of[3], (3, CHANNEL_COUNT, SHORT), SHORT ** -0.5, 3.5, ((1, 16),), jnp.float32)
    long_filter = draw_long_filter(jax.random.fold_in(streams_of[7], 71), 0)
    skip_gain = centred(streams_of[5], (CHANNEL_COUNT,), 1.0, 4.0, ((0, 16),), jnp.float32)
    w_out = centred(streams_of[6], (CHANNEL_COUNT, CHANNEL_COUNT), CHANNEL_COUNT ** -0.5, 0.09375, ((0, 16),))
    return {"activations": activations, "norm_gain": norm_gain, "w_in": w_in, "w_short": w_short, "long_filter": long_filter, "skip_gain": skip_gain, "w_out": w_out}


epsilon = 1e-05

def reference(activations, norm_gain, w_in, w_short, long_filter, skip_gain, w_out):
    wide = activations.astype(jnp.float32)
    factor = lax.rsqrt(lax.optimization_barrier(jnp.mean(wide * wide, axis=0)) + epsilon)
    normed = (wide * factor[None, :] * norm_gain[:, None]).astype(jnp.bfloat16)
    projected = jnp.stack([jnp.dot(w_in[stream], normed, preferred_element_type=jnp.float32) for stream in range(3)]).astype(jnp.bfloat16)
    padded = jnp.pad(projected.astype(jnp.float32), ((0, 0), (0, 0), (SHORT - 1, 0)))
    smoothed = jnp.zeros(projected.shape, jnp.float32)
    for tap_index in range(SHORT):
        begin = SHORT - 1 - tap_index
        smoothed = smoothed + w_short[:, :, tap_index][:, :, None] * padded[:, :, begin:begin + GENOME_LETTERS]
    query = smoothed[0]
    key_part = smoothed[1]
    value = smoothed[2]
    gated = (key_part * value).astype(jnp.bfloat16)
    expanded = long_filter.astype(jnp.float32)
    length = 2 * GENOME_LETTERS
    spectrum = jnp.fft.rfft(gated.astype(jnp.float32), n=length, axis=1) * jnp.fft.rfft(expanded, n=length, axis=1)
    filtered = jnp.fft.irfft(spectrum, n=length, axis=1)[:, :GENOME_LETTERS]
    mixed = (query * (filtered + skip_gain[:, None] * gated.astype(jnp.float32))).astype(jnp.bfloat16)
    return jnp.dot(w_out, mixed, preferred_element_type=jnp.float32).astype(jnp.bfloat16)
```

```python
import math

import jax
import jax.numpy as jnp
import numpy as np
from jax import lax
from jax.experimental import pallas as pl
from jax.experimental.pallas import tpu as pltpu
from jax.sharding import PartitionSpec as P

epsilon = 1e-05
block_len = 128
side_rows = 8
bf16 = jnp.bfloat16
f32 = jnp.float32


def split_table(table):
    high = table.astype(bf16)
    low = (table - high.astype(np.float64)).astype(bf16)
    return np.stack([high, low])


def dft_tables():
    size = 2 * block_len
    freq = np.arange(block_len) + 0.5
    angle = 2.0 * math.pi / size * np.arange(size)[:, None] * freq[None, :]
    forward = np.concatenate([np.cos(angle), -np.sin(angle)], axis=1)
    back = angle[block_len:].T
    inverse = np.concatenate([np.cos(back), -np.sin(back)], axis=0) * (2.0 / size)
    return split_table(forward), split_table(inverse)


def whole(shape):
    return pl.BlockSpec(shape, lambda *_: (0,) * len(shape))


def dot(left, right):
    return jnp.dot(left, right, preferred_element_type=f32)


def prepare_kernel(x_ref, gain_ref, first_ref, second_ref):
    rows = x_ref.shape[0]
    half = rows // 2
    wide = x_ref[...].astype(f32)
    gain = jnp.broadcast_to(gain_ref[...], (8, rows)).T[:, :1]
    scaled = (wide * gain).astype(bf16)
    squares = jnp.sum(wide * wide, axis=0, keepdims=True)
    high = squares.astype(bf16)
    low = (squares - high.astype(f32)).astype(bf16)
    first_ref[:half] = scaled[:half]
    row = lax.broadcasted_iota(jnp.int32, (side_rows, wide.shape[1]), 0)
    side = jnp.where(row == 0, high.astype(f32), jnp.where(row == 1, low.astype(f32), 0.0))
    first_ref[half:] = side.astype(bf16)
    second_ref[...] = scaled[half:]


def prepare(x, gain):
    rows, tokens = x.shape
    half = rows // 2
    return pl.pallas_call(
        prepare_kernel,
        out_shape=(
            jax.ShapeDtypeStruct((half + side_rows, tokens), bf16),
            jax.ShapeDtypeStruct((half, tokens), bf16),
        ),
        name="prepare",
    )(x, gain.reshape(1, rows))


def ring_places(count):
    evens = list(range(0, count, 2))
    odds = list(range(1, count, 2))
    return evens + odds[::-1]


def ring_maps():
    chips = lax.axis_size("fsdp") // 2
    order = ring_places(chips)
    ahead = [
        (order[i] * 2 + core, order[(i + 1) % chips] * 2 + core)
        for i in range(chips)
        for core in range(2)
    ]
    behind = [(b, a) for a, b in ahead]
    return ahead, behind, [(i, i ^ 1) for i in range(2 * chips)]


def ring_ids():
    chips = lax.axis_size("fsdp") // 2
    me = lax.axis_index("fsdp")
    chip, core = me // 2, me % 2
    place = jnp.where(chip % 2 == 0, chip // 2, chips - 1 - chip // 2)
    others = (place - jnp.arange(chips, dtype=jnp.int32) + chips) % chips
    ids = jnp.where(others < (chips + 1) // 2, 2 * others, 2 * (chips - 1 - others) + 1)
    return jnp.concatenate([ids, core[None]]).astype(jnp.int32)


def ring_steps(first, second):
    chips = lax.axis_size("fsdp") // 2
    ahead, behind, _ = ring_maps()
    fa, fb, ba, bb = first, second, first, second
    for step in range(1, chips // 2 + 1):
        fa = lax.ppermute(fa, "fsdp", ahead)
        bb = lax.ppermute(bb, "fsdp", behind)
        if step < chips // 2:
            fb = lax.ppermute(fb, "fsdp", ahead)
            ba = lax.ppermute(ba, "fsdp", behind)
            yield [(step, fa, fb), (chips - step, ba, bb)]
        else:
            yield [(step, fa, bb)]


def other_core(block):
    return lax.ppermute(block, "fsdp", ring_maps()[2])


def product_kernel(slots, parts, rows, first_group, side, finish, extra, *refs):
    ids_ref, refs = refs[0], list(refs[1:])
    mine = refs[: 2 * len(slots)]
    theirs = refs[2 * len(slots) : 4 * len(slots)]
    refs = refs[4 * len(slots) :]
    weights, refs = refs[: len(slots)], refs[len(slots) :]
    total = None
    side_in = None
    if not first_group:
        total, refs = refs[0], refs[1:]
        if side:
            side_in, refs = refs[0], refs[1:]
    extras, refs = refs[:extra], refs[extra:]
    *outs, gathered = refs if not (side and finish) else refs[:-1]
    if side and finish:
        outs, gathered, side_total = refs[:-2], refs[-2], refs[-1]
    half = rows // 2
    step = pl.program_id(0)

    @pl.when(step == 0)
    def _():
        core = ids_ref[ids_ref.shape[0] - 1]
        side_sum = None if side_in is None else side_in[...]
        for k in range(len(slots)):
            base = 2 * k * rows
            own = pl.multiple_of(base + core * rows, half)
            other = pl.multiple_of(base + (1 - core) * rows, half)
            for start, pair in ((own, mine[2 * k : 2 * k + 2]), (other, theirs[2 * k : 2 * k + 2])):
                gathered[pl.ds(start, half)] = pair[0][:half]
                gathered[pl.ds(pl.multiple_of(start + half, half), half)] = pair[1][...]
                if side:
                    more = pair[0][half:].astype(f32)
                    side_sum = more if side_sum is None else side_sum + more
        if side:
            if finish:
                side_total[...] = side_sum
            else:
                outs[1][...] = side_sum

    product = None if first_group else total[0]
    for k in range(len(slots)):
        term = dot(weights[k][0], gathered[2 * k * rows : 2 * (k + 1) * rows])
        product = term if product is None else product + term
    if finish:
        finish(step, product, side_total if side else None, extras, outs)
    else:
        outs[0][0] = product


def products(ids, slots, mine, theirs, weight, running, side, finish=None, extras=(), name="sum"):
    streams, out_rows, features = weight.shape
    rows = features // (2 * (ids.shape[0] - 1))
    tokens = mine[1].shape[1]
    first_group = running is None
    state = () if first_group else running

    def weight_spec(slot):
        return pl.BlockSpec((1, out_rows, 2 * rows), lambda s, ids: (s, 0, ids[slot]))

    in_specs = [whole(a.shape) for a in mine + theirs] + [weight_spec(slot) for slot in slots]
    total_spec = pl.BlockSpec((1, out_rows, tokens), lambda s, ids: (s, 0, 0))
    if not first_group:
        in_specs.append(total_spec)
        if side:
            in_specs.append(whole(state[1].shape))
    in_specs += [whole(a.shape) for a in extras]
    scratch = [pltpu.VMEM((2 * len(slots) * rows, tokens), bf16)]
    if finish is None:
        out_shape = [jax.ShapeDtypeStruct((streams, out_rows, tokens), f32)]
        out_specs = [total_spec]
        if side:
            out_shape.append(jax.ShapeDtypeStruct((side_rows, tokens), f32))
            out_specs.append(whole((side_rows, tokens)))
        body = None
    else:
        body, out_shape, out_specs, more_scratch = finish
        if side:
            scratch.append(pltpu.VMEM((side_rows, tokens), f32))
    kernel = lambda *refs: product_kernel(
        slots, None, rows, first_group, side, body, len(extras), *refs
    )
    return pl.pallas_call(
        kernel,
        grid_spec=pltpu.PrefetchScalarGridSpec(
            num_scalar_prefetch=1,
            grid=(streams,),
            in_specs=in_specs,
            out_specs=out_specs,
            scratch_shapes=scratch,
        ),
        out_shape=out_shape,
        compiler_params=pltpu.CompilerParams(vmem_limit_bytes=48 * 2**20),
        cost_estimate=pl.CostEstimate(
            flops=2 * streams * out_rows * tokens * 2 * rows * len(slots),
            bytes_accessed=streams * out_rows * (4 * rows * len(slots) + 8 * tokens),
            transcendentals=0,
        ),
        name=name,
    )(ids, *mine, *theirs, *[weight] * len(slots), *state, *extras)


def gather_products(ids, first, second, weight, side, finish, extras=(), name="sum"):
    chips = lax.axis_size("fsdp") // 2
    running = None
    pending = [(0, first, second)]
    groups = list(ring_steps(first, second))
    groups[0] = pending + groups[0]
    for number, group in enumerate(groups):
        slots = [g[0] for g in group]
        mine = [half for g in group for half in g[1:]]
        theirs = [other_core(half) for half in mine]
        last = number == len(groups) - 1
        running = products(
            ids,
            slots,
            mine,
            theirs,
            weight,
            running,
            side,
            finish if last else None,
            extras if last else (),
            name=f"{name}_{number}",
        )
    return running


def smooth(projected, taps, halo):
    tokens = projected.shape[1]
    lane = lax.broadcasted_iota(jnp.int32, projected.shape, 1)
    out = taps[:, :1] * projected
    count = taps.shape[1]
    for tap in range(1, count):
        moved = pltpu.roll(projected, tap, 1)
        for place in range(tap):
            if halo is None:
                edge = 0.0
            else:
                at = count - 1 - tap + place
                edge = halo[:, at : at + 1]
            moved = jnp.where(lane == place, edge, moved)
        out = out + taps[:, tap : tap + 1] * moved
    return out


def projection_finish(features):
    def body(step, product, side_total, extras, outs):
        projected_ref, gated_ref = outs
        taps_ref = extras[0]
        mean = jnp.sum(side_total[...], axis=0, keepdims=True) * (1.0 / features)
        factor = lax.rsqrt(mean + epsilon)
        projected_ref[pl.ds(step, 1)] = (product * factor).astype(bf16)[None]

        @pl.when(step == 2)
        def _():
            key = smooth(projected_ref[1].astype(f32), taps_ref[1], None)
            value = smooth(projected_ref[2].astype(f32), taps_ref[2], None)
            gated_ref[...] = (key * value).astype(bf16)

    return body


def spectra_kernel(filter_ref, table_ref, out_ref):
    blocks = filter_ref.shape[1] // block_len
    before = jnp.zeros((filter_ref.shape[0], block_len), bf16)
    for k in range(blocks):
        now = filter_ref[:, k * block_len : (k + 1) * block_len]
        segment = jnp.concatenate([before, now], axis=1)
        out_ref[:, 2 * k * block_len : 2 * (k + 1) * block_len] = dot(
            segment, table_ref[0]
        ) + dot(segment, table_ref[1])
        before = now


def filter_spectra(long_filter, table):
    channels, lags = long_filter.shape
    tile = min(channels, 64)
    return pl.pallas_call(
        spectra_kernel,
        grid=(channels // tile,),
        in_specs=[pl.BlockSpec((tile, lags), lambda i: (i, 0)), whole(table.shape)],
        out_specs=pl.BlockSpec((tile, 2 * lags), lambda i: (i, 0)),
        out_shape=jax.ShapeDtypeStruct((channels, 2 * lags), f32),
        name="filter_spectra",
    )(long_filter, table)


def block_spectra(gated, table, spec_ref):
    for b in range(gated.shape[1] // block_len):
        piece = gated[:, b * block_len : (b + 1) * block_len]
        spec_ref[:, 2 * b * block_len : 2 * (b + 1) * block_len] = dot(
            piece, table[0, :block_len]
        ) + dot(piece, table[1, :block_len])


def multiply_spectra(source, filters, pairs, total_ref, fresh):
    def rows_of(i, carry):
        rows = pl.ds(pl.multiple_of(i * 8, 8), 8)

        def part(ref, k, imaginary):
            start = (2 * k + imaginary) * block_len
            return ref[rows, start : start + block_len]

        for a, terms in enumerate(pairs):
            if fresh:
                real = jnp.zeros((8, block_len), f32)
                imag = jnp.zeros((8, block_len), f32)
            else:
                real, imag = part(total_ref, a, 0), part(total_ref, a, 1)
            for b, d in terms:
                gr, gi = part(source, b, 0), part(source, b, 1)
                hr, hi = part(filters, d, 0), part(filters, d, 1)
                real = real + gr * hr - gi * hi
                imag = imag + gr * hi + gi * hr
            total_ref[rows, 2 * a * block_len : (2 * a + 1) * block_len] = real
            total_ref[rows, (2 * a + 1) * block_len : (2 * a + 2) * block_len] = imag
        return carry

    lax.fori_loop(0, total_ref.shape[0] // 8, rows_of, 0)


def own_kernel(projected_ref, halo_ref, taps_ref, filters_ref, table_ref, *refs):
    query_ref, gated_ref, total_ref, spec_ref = refs
    smoothed = [
        smooth(projected_ref[s].astype(f32), taps_ref[s], halo_ref[s].astype(f32))
        for s in range(3)
    ]
    query_ref[...] = smoothed[0]
    gated_ref[...] = (smoothed[1] * smoothed[2]).astype(bf16)
    block_spectra(gated_ref, table_ref, spec_ref)
    blocks = gated_ref.shape[1] // block_len
    pairs = [[(b, a - b) for b in range(a + 1)] for a in range(blocks)]
    multiply_spectra(spec_ref, filters_ref, pairs, total_ref, True)


def own_part(projected, halo, taps, filters, table):
    _, channels, tokens = projected.shape
    tile = min(channels, 64)
    rows = lambda width: pl.BlockSpec((tile, width), lambda i: (i, 0))
    deep = lambda width: pl.BlockSpec((3, tile, width), lambda i: (0, i, 0))
    return pl.pallas_call(
        own_kernel,
        grid=(channels // tile,),
        in_specs=[
            deep(tokens),
            deep(halo.shape[2]),
            deep(taps.shape[2]),
            rows(2 * tokens),
            whole(table.shape),
        ],
        out_specs=[rows(tokens), rows(tokens), rows(2 * tokens)],
        out_shape=[
            jax.ShapeDtypeStruct((channels, tokens), f32),
            jax.ShapeDtypeStruct((channels, tokens), bf16),
            jax.ShapeDtypeStruct((channels, 2 * tokens), f32),
        ],
        scratch_shapes=[pltpu.VMEM((tile, 2 * tokens), f32)],
        compiler_params=pltpu.CompilerParams(vmem_limit_bytes=48 * 2**20),
        cost_estimate=pl.CostEstimate(flops=6 * 10**8, bytes_accessed=6 * 10**6, transcendentals=0),
        name="own_part",
    )(projected, halo, taps, filters, table)


def far_kernel(turn, last, *refs):
    moved_ref, total_ref, filters_ref, table_ref = refs[:4]
    blocks = moved_ref.shape[1] // block_len
    pairs = [
        [(b, turn * blocks + a - b) for b in range(blocks)] for a in range(blocks)
    ]
    if not last:
        out_ref, spec_ref = refs[4:]
        out_ref[...] = total_ref[...]
        block_spectra(moved_ref, table_ref, spec_ref)
        multiply_spectra(spec_ref, filters_ref, pairs, out_ref, False)
        return
    back_ref, query_ref, gated_ref, skip_ref, out_ref, spec_ref, sum_ref = refs[4:]
    sum_ref[...] = total_ref[...]
    block_spectra(moved_ref, table_ref, spec_ref)
    multiply_spectra(spec_ref, filters_ref, pairs, sum_ref, False)
    rows = out_ref.shape[0]
    skip = jnp.broadcast_to(skip_ref[0], (8, rows)).T[:, :1]
    for a in range(blocks):
        lanes = slice(a * block_len, (a + 1) * block_len)
        spectrum = sum_ref[:, 2 * a * block_len : 2 * (a + 1) * block_len]
        high = spectrum.astype(bf16)
        low = (spectrum - high.astype(f32)).astype(bf16)
        filtered = dot(high, back_ref[0]) + (dot(low, back_ref[0]) + dot(high, back_ref[1]))
        gated = gated_ref[:, lanes].astype(f32)
        out_ref[:, lanes] = (query_ref[:, lanes] * (filtered + skip * gated)).astype(bf16)


def far_part(turn, part, moved, total, filters, table, last):
    rows_n, tokens = moved.shape
    filters_n = filters.shape[1]
    at = lambda width: pl.BlockSpec((rows_n, width), lambda i: (part, 0))
    in_specs = [whole(moved.shape), at(2 * tokens) if total.shape[0] != rows_n else whole(total.shape)]
    in_specs += [at(filters_n), whole(table.shape)]
    scratch = [pltpu.VMEM((rows_n, 2 * tokens), f32)]
    if last is None:
        args = ()
        out_shape = jax.ShapeDtypeStruct((rows_n, 2 * tokens), f32)
    else:
        inverse, query, gated, skip = last
        args = (inverse, query, gated, skip.reshape(2, 1, rows_n))
        in_specs += [whole(inverse.shape), at(tokens), at(tokens)]
        in_specs += [pl.BlockSpec((1, 1, rows_n), lambda i: (part, 0, 0))]
        out_shape = jax.ShapeDtypeStruct((rows_n, tokens), bf16)
        scratch.append(pltpu.VMEM((rows_n, 2 * tokens), f32))
    return pl.pallas_call(
        lambda *refs: far_kernel(turn, last is not None, *refs),
        grid=(1,),
        in_specs=in_specs,
        out_specs=whole(out_shape.shape),
        out_shape=out_shape,
        scratch_shapes=scratch,
        compiler_params=pltpu.CompilerParams(vmem_limit_bytes=48 * 2**20),
        cost_estimate=pl.CostEstimate(flops=4 * 10**8, bytes_accessed=4 * 10**6, transcendentals=0),
        name=f"far_part_{turn}_{part}",
    )(moved, total, filters, table, *args)


def from_before(block):
    count = lax.axis_size("ctx")
    return lax.ppermute(block, "ctx", [(i - 1, i) for i in range(1, count)])


def output_finish(step, product, side_total, extras, outs):
    outs[0][...] = product.astype(bf16)


def shards(activations, norm_gain, w_in, w_short, long_filter, skip_gain, w_out):
    channels, tokens = activations.shape
    features = w_in.shape[2]
    turns = lax.axis_size("ctx")
    half = channels // 2
    forward, inverse = (jnp.asarray(t) for t in dft_tables())
    ids = ring_ids()
    first, second = prepare(activations, norm_gain)
    filters = filter_spectra(long_filter, forward)

    finish = (
        projection_finish(features),
        [
            jax.ShapeDtypeStruct((3, channels, tokens), bf16),
            jax.ShapeDtypeStruct((channels, tokens), bf16),
        ],
        [whole((3, channels, tokens)), whole((channels, tokens))],
        None,
    )
    projected, gated_alone = gather_products(
        ids, first, second, w_in, True, finish, (w_short,), "projection"
    )

    taps = w_short.shape[2]
    halo = from_before(projected[:, :, tokens - (taps - 1) :])
    moving = None
    if turns == 2:
        moving = [gated_alone[:half], gated_alone[half:]]
        moving = [from_before(m) for m in moving]
    query, gated, total = own_part(projected, halo, w_short, filters, forward)
    if moving is None:
        moving = [from_before(m) for m in (gated[:half], gated[half:])]
    totals = [total, total]
    mixed = [None, None]
    for turn in range(1, turns):
        for part in range(2):
            last = None
            if turn == turns - 1:
                last = (inverse, query, gated, skip_gain)
            totals[part] = far_part(turn, part, moving[part], totals[part], filters, forward, last)
            if last is None:
                moving[part] = from_before(moving[part])
    mixed = totals

    out_finish = (
        output_finish,
        [jax.ShapeDtypeStruct((channels, tokens), bf16)],
        [whole((channels, tokens))],
        None,
    )
    (result,) = gather_products(
        ids, mixed[0], mixed[1], w_out[None], False, out_finish, (), "output"
    )
    return result


def solution(mesh):
    placed = (
        P("fsdp", "ctx"),
        P("fsdp"),
        P(None, "fsdp", None),
        P(None, "fsdp", None),
        P("fsdp", None),
        P("fsdp"),
        P("fsdp", None),
    )
    return jax.shard_map(
        shards, mesh=mesh, in_specs=placed, out_specs=P("fsdp", "ctx"), check_vma=False
    )
```

```python
import math

import jax
import jax.numpy as jnp
import numpy as np
from jax import lax
from jax.experimental import pallas as pl
from jax.experimental.pallas import tpu as pltpu
from jax.sharding import PartitionSpec as P

epsilon = 1e-05
block_len = 128
side_rows = 8
bf16 = jnp.bfloat16
f32 = jnp.float32
in_vmem = pl.BlockSpec(memory_space=pltpu.VMEM)
in_smem = pl.BlockSpec(memory_space=pltpu.SMEM)
params = pltpu.CompilerParams(vmem_limit_bytes=20 * 2**20)


def shape_of(shape, dtype):
    return jax.ShapeDtypeStruct(tuple(shape), dtype)


def dot(left, right):
    return jnp.dot(left, right, preferred_element_type=f32)


def column(row):
    return jnp.broadcast_to(row, (8, row.shape[1])).T[:, :1]


def tap_columns(taps):
    return jnp.concatenate([taps, jnp.zeros((8 - taps.shape[0], taps.shape[1]), f32)], axis=0).T


def estimate(flops, size):
    return pl.CostEstimate(flops=int(flops), bytes_accessed=int(size), transcendentals=0)


def prepare_kernel(x_ref, gain_ref, out_ref):
    rows = x_ref.shape[0]
    wide = x_ref[...].astype(f32)
    out_ref[:rows] = (wide * column(gain_ref[...])).astype(bf16)
    squares = jnp.sum(wide * wide, axis=0, keepdims=True)
    high = squares.astype(bf16).astype(f32)
    row = lax.broadcasted_iota(jnp.int32, (side_rows, wide.shape[1]), 0)
    side = jnp.where(row == 0, high, jnp.where(row == 1, squares - high, 0.0))
    out_ref[rows:] = side.astype(bf16)


def prepare(x, gain):
    rows, tokens = x.shape
    return pl.pallas_call(
        prepare_kernel,
        in_specs=[in_vmem, in_vmem],
        out_specs=in_vmem,
        out_shape=shape_of((rows + side_rows, tokens), bf16),
        compiler_params=params,
        name="prepare",
    )(x, gain.reshape(1, rows))


def chip_count():
    return lax.axis_size("fsdp") // 2


def ring_order(count):
    return list(range(0, count, 2)) + list(range(1, count, 2))[::-1]


def along_ring(block):
    chips = chip_count()
    order = ring_order(chips)
    pairs = []
    for i in range(chips):
        here, after = order[i], order[(i + 1) % chips]
        pairs += [(2 * here, 2 * after), (2 * after + 1, 2 * here + 1)]
    return lax.ppermute(block, "fsdp", pairs)


def other_core(block):
    return lax.ppermute(block, "fsdp", [(i, i ^ 1) for i in range(2 * chip_count())])


def ring_ids():
    chips = chip_count()
    me = lax.axis_index("fsdp")
    chip, core = me // 2, me % 2
    place = jnp.where(chip % 2 == 0, chip // 2, chips - 1 - chip // 2)
    steps = jnp.arange(chips, dtype=jnp.int32)
    places = (place + jnp.where(core == 0, chips - steps, steps)) % chips
    ids = jnp.where(places < (chips + 1) // 2, 2 * places, 2 * (chips - 1 - places) + 1)
    return jnp.concatenate([ids, core[None]]).astype(jnp.int32)


def gather_in_order(ids_ref, slots, shards, ordered):
    core = ids_ref[ids_ref.shape[0] - 1]
    rows = ordered.shape[0] // (2 * len(slots))
    for k in range(len(slots)):
        for index in range(2):
            place = core if index == 0 else 1 - core
            at = pl.multiple_of((2 * k + place) * rows, rows)
            ordered[pl.ds(at, rows)] = shards[2 * k + index][:rows]


def products(ids, slots, shards, weight, running, side, finish=None, name="sum"):
    streams, out_rows, features = weight.shape
    rows = features // (2 * (ids.shape[0] - 1))
    tokens = shards[0].shape[1]
    count = len(shards)
    first_group = running is None
    state = [] if first_group else list(running)
    body, extras, out_shape = finish if finish else (None, [], None)
    assembled = rows % 128 != 0
    width = 2 * rows if assembled else rows
    scratch_shapes = [pltpu.VMEM((count * rows, tokens), bf16)] if assembled else []

    def kernel(ids_ref, *refs):
        refs = list(refs)
        take = lambda n: [refs.pop(0) for _ in range(n)]
        shard_refs = take(count)
        (weight_ref,) = take(1)
        state_refs = take(len(state))
        extra_refs = take(len(extras))
        outs = take(len(out_shape))
        core = ids_ref[ids_ref.shape[0] - 1]
        if assembled:
            gather_in_order(ids_ref, slots, shard_refs, refs[0])
            right = refs[0][...]
        else:
            right = jnp.concatenate([ref[:rows] for ref in shard_refs], axis=0)
        side_sum = None
        if side:
            parts = [ref[rows:].astype(f32) for ref in shard_refs]
            parts += [] if first_group else [state_refs[1][...]]
            side_sum = sum(parts[1:], parts[0])

        def total(stream):
            left = []
            for k in range(count * rows // width):
                if assembled:
                    block = ids_ref[slots[k]]
                else:
                    block = 2 * ids_ref[slots[k // 2]] + (core if k % 2 == 0 else 1 - core)
                at = pl.ds(pl.multiple_of(block * width, width), width)
                left.append(weight_ref[stream, :, at])
            product = dot(jnp.concatenate(left, axis=1), right)
            return product if first_group else state_refs[0][stream] + product

        if body is not None:
            body(total, side_sum, extra_refs, outs)
            return
        for stream in range(streams):
            outs[0][stream] = total(stream)
        if side:
            outs[1][...] = side_sum

    aliases = {}
    if body is None:
        out_shape = [shape_of((streams, out_rows, tokens), f32)]
        if side:
            out_shape.append(shape_of((side_rows, tokens), f32))
        if not first_group:
            aliases = {1 + count + 1 + i: i for i in range(len(state))}
    return pl.pallas_call(
        kernel,
        in_specs=[in_smem] + [in_vmem] * (count + 1 + len(state) + len(extras)),
        out_specs=[in_vmem] * len(out_shape),
        out_shape=out_shape,
        scratch_shapes=scratch_shapes,
        input_output_aliases=aliases,
        compiler_params=params,
        cost_estimate=estimate(
            2 * streams * out_rows * tokens * rows * count, 2 * streams * out_rows * rows * count
        ),
        name=name,
    )(ids, *shards, weight, *state, *extras)


def gather_products(ids, own, weight, side, finish, name):
    chips = chip_count()
    last_step = chips // 2
    sibling = other_core(own)
    near, far = own, sibling
    running = None
    slots, group = [0], [own, sibling]
    for step in range(1, last_step + 1):
        near = along_ring(near)
        if step < last_step:
            if running is not None:
                far, *running = lax.optimization_barrier((far, *running))
            far = along_ring(far)
        if step > 1:
            running = products(ids, slots, group, weight, running, side, None, f"{name}_{step - 1}")
            slots, group = [], []
        if step < last_step:
            slots = slots + [step, chips - step]
            group = group + [near, far, other_core(far), other_core(near)]
        else:
            slots, group = [step], [near, other_core(near)]
    return products(ids, slots, group, weight, running, side, finish, f"{name}_{last_step}")


def smooth(projected, taps, count, halo):
    lane = lax.broadcasted_iota(jnp.int32, projected.shape, 1)
    out = taps[:, :1] * projected
    for tap in range(1, count):
        moved = pltpu.roll(projected, tap, 1)
        for place in range(tap):
            edge = 0.0
            if halo is not None:
                at = halo.shape[1] - tap + place
                edge = halo[:, at : at + 1]
            moved = jnp.where(lane == place, edge, moved)
        out = out + taps[:, tap : tap + 1] * moved
    return out


def projection_finish(features, w_short, tokens):
    streams, count, channels = w_short.shape

    def body(total, side_sum, extra_refs, outs):
        (taps_ref,) = extra_refs
        projected_ref, gated_ref, halo_ref = outs
        mean = jnp.sum(side_sum, axis=0, keepdims=True) * (1.0 / features)
        factor = lax.rsqrt(mean + epsilon)

        for stream in range(streams):
            projected = (total(stream) * factor).astype(bf16)
            projected_ref[stream] = projected
            tail = projected[:, tokens - block_len :].astype(f32).T
            halo_ref[stream] = tail[block_len - 8 :]

        taps = [tap_columns(taps_ref[stream]) for stream in (1, 2)]
        tile = min(channels, 64)
        for start in range(0, channels, tile):
            rows = slice(start, start + tile)
            key, value = (
                smooth(projected_ref[s, rows].astype(f32), taps[s - 1][rows], count, None)
                for s in (1, 2)
            )
            gated_ref[rows] = (key * value).astype(bf16)

    out_shape = [
        shape_of((streams, channels, tokens), bf16),
        shape_of((channels, tokens), bf16),
        shape_of((streams, 8, channels), f32),
    ]
    return body, [w_short], out_shape


def split_table(table):
    high = table.astype(bf16)
    low = (table - high.astype(np.float64)).astype(bf16)
    return np.stack([high, low])


def dft_tables():
    size = 2 * block_len
    freq = np.arange(block_len) + 0.5
    angle = 2.0 * math.pi / size * np.arange(size)[:, None] * freq[None, :]
    forward = np.concatenate([np.cos(angle), -np.sin(angle)], axis=1)
    back = angle[block_len:].T
    inverse = np.concatenate([np.cos(back), -np.sin(back)], axis=0) * (2.0 / size)
    return split_table(forward), split_table(inverse)


def spectrum_lanes(k):
    return slice(2 * k * block_len, 2 * (k + 1) * block_len)


def block_lanes(k):
    return slice(k * block_len, (k + 1) * block_len)


def spectra_kernel(filter_ref, table_ref, out_ref):
    blocks = filter_ref.shape[1] // block_len
    before = jnp.zeros((filter_ref.shape[0], block_len), bf16)
    for k in range(blocks):
        now = filter_ref[:, block_lanes(k)]
        segment = jnp.concatenate([before, now], axis=1)
        out_ref[:, spectrum_lanes(k)] = dot(segment, table_ref[0]) + dot(segment, table_ref[1])
        before = now


def filter_spectra(long_filter, table):
    channels, lags = long_filter.shape
    return pl.pallas_call(
        spectra_kernel,
        in_specs=[in_vmem, in_vmem],
        out_specs=in_vmem,
        out_shape=shape_of((channels, 2 * lags), f32),
        compiler_params=params,
        cost_estimate=estimate(8 * channels * lags * 2 * block_len, 10 * channels * lags),
        name="filter_spectra",
    )(long_filter, table)


def block_spectra(gated_ref, table_ref, spec_ref):
    for b in range(gated_ref.shape[1] // block_len):
        piece = gated_ref[:, block_lanes(b)]
        spec_ref[:, spectrum_lanes(b)] = dot(piece, table_ref[0, :block_len]) + dot(
            piece, table_ref[1, :block_len]
        )


def multiply_spectra(source_ref, filters_ref, filter_start, pairs, before_ref, total_ref):
    def one_tile(i, carry):
        here = pl.ds(pl.multiple_of(i * 8, 8), 8)
        there = pl.ds(pl.multiple_of(filter_start + i * 8, 8), 8)

        def part(ref, rows, k, imaginary):
            start = (2 * k + imaginary) * block_len
            return ref[rows, start : start + block_len]

        for a, terms in enumerate(pairs):
            real = imag = None
            if before_ref is not None:
                real, imag = part(before_ref, here, a, 0), part(before_ref, here, a, 1)
            for b, d in terms:
                gr, gi = part(source_ref, here, b, 0), part(source_ref, here, b, 1)
                hr, hi = part(filters_ref, there, d, 0), part(filters_ref, there, d, 1)
                more_real, more_imag = gr * hr - gi * hi, gr * hi + gi * hr
                real = more_real if real is None else real + more_real
                imag = more_imag if imag is None else imag + more_imag
            start = 2 * a * block_len
            total_ref[here, start : start + block_len] = real
            total_ref[here, start + block_len : start + 2 * block_len] = imag
        return carry

    lax.fori_loop(0, total_ref.shape[0] // 8, one_tile, 0)


def own_kernel(projected_ref, halo_ref, taps_ref, filters_ref, table_ref, *refs):
    query_ref, gated_ref, first_ref, second_ref, spec_ref, total_ref = refs
    channels, tokens = gated_ref.shape
    half = channels // 2
    count = taps_ref.shape[1]
    halo = [halo_ref[s].T for s in range(3)]
    taps = [tap_columns(taps_ref[s]) for s in range(3)]
    tile = min(channels, 64)
    for start in range(0, channels, tile):
        rows = slice(start, start + tile)
        query, key, value = (
            smooth(projected_ref[s, rows].astype(f32), taps[s][rows], count, halo[s][rows])
            for s in range(3)
        )
        query_ref[rows] = query
        gated_ref[rows] = (key * value).astype(bf16)
    block_spectra(gated_ref, table_ref, spec_ref)
    blocks = tokens // block_len
    pairs = [[(b, a - b) for b in range(a + 1)] for a in range(blocks)]
    multiply_spectra(spec_ref, filters_ref, 0, pairs, None, total_ref)
    first_ref[...] = total_ref[:half]
    second_ref[...] = total_ref[half:]


def own_part(projected, halo, taps, filters, table):
    _, channels, tokens = projected.shape
    return pl.pallas_call(
        own_kernel,
        in_specs=[in_vmem] * 5,
        out_specs=[in_vmem] * 4,
        out_shape=[
            shape_of((channels, tokens), f32),
            shape_of((channels, tokens), bf16),
            shape_of((channels // 2, 2 * tokens), f32),
            shape_of((channels // 2, 2 * tokens), f32),
        ],
        scratch_shapes=[pltpu.VMEM((channels, 2 * tokens), f32)] * 2,
        compiler_params=params,
        cost_estimate=estimate(6 * 10**8, 6 * 10**6),
        name="own_part",
    )(projected, halo, taps, filters, table)


def far_part(turn, part, moved, total, filters, table, last):
    rows, tokens = moved.shape
    blocks = tokens // block_len
    pairs = [[(b, turn * blocks + a - b) for b in range(blocks)] for a in range(blocks)]

    def kernel(moved_ref, total_ref, filters_ref, table_ref, *refs):
        *refs, spec_ref = refs
        block_spectra(moved_ref, table_ref, spec_ref)
        if last is None:
            multiply_spectra(spec_ref, filters_ref, part * rows, pairs, total_ref, refs[0])
            return
        *refs, sum_ref = refs
        back_ref, query_ref, gated_ref, skip_ref = refs[:4]
        out_ref = refs[-1]
        multiply_spectra(spec_ref, filters_ref, part * rows, pairs, total_ref, sum_ref)
        here = slice(part * rows, (part + 1) * rows)
        skip = column(skip_ref[...])[here]
        for a in range(blocks):
            lanes = block_lanes(a)
            spectrum = sum_ref[:, spectrum_lanes(a)]
            high = spectrum.astype(bf16)
            low = (spectrum - high.astype(f32)).astype(bf16)
            filtered = dot(high, back_ref[0]) + (dot(low, back_ref[0]) + dot(high, back_ref[1]))
            gated = gated_ref[here, lanes].astype(f32)
            out_ref[here, lanes] = (query_ref[here, lanes] * (filtered + skip * gated)).astype(bf16)

    args = [moved, total, filters, table]
    aliases = {}
    scratch = [pltpu.VMEM((rows, 2 * tokens), f32)]
    out_shape = shape_of((rows, 2 * tokens), f32)
    if last is not None:
        inverse, query, gated, skip, mixed = last
        args += [inverse, query, gated, skip.reshape(1, 2 * rows)]
        if mixed is not None:
            aliases = {len(args): 0}
            args.append(mixed)
        out_shape = shape_of((2 * rows, tokens), bf16)
        scratch.append(pltpu.VMEM((rows, 2 * tokens), f32))
    return pl.pallas_call(
        kernel,
        in_specs=[in_vmem] * len(args),
        out_specs=in_vmem,
        out_shape=out_shape,
        scratch_shapes=scratch[::-1],
        input_output_aliases=aliases,
        compiler_params=params,
        cost_estimate=estimate(4 * 10**8, 4 * 10**6),
        name=f"far_part_{turn}_{part}",
    )(*args)


def from_before(block):
    count = lax.axis_size("ctx")
    return lax.ppermute(block, "ctx", [(i - 1, i) for i in range(1, count)])


def output_finish(channels, tokens):
    def body(total, side_sum, extra_refs, outs):
        outs[0][...] = total(0).astype(bf16)

    return body, [], [shape_of((channels, tokens), bf16)]


def shards(activations, norm_gain, w_in, w_short, long_filter, skip_gain, w_out):
    channels, tokens = activations.shape
    features = w_in.shape[2]
    w_short = w_short.transpose(0, 2, 1)
    turns = lax.axis_size("ctx")
    half = channels // 2
    forward, inverse = (jnp.asarray(t) for t in dft_tables())
    ids = ring_ids()
    own = prepare(activations, norm_gain)
    filters = filter_spectra(long_filter, forward)

    finish = projection_finish(features, w_short, tokens)
    projected, gated_alone, tail = gather_products(ids, own, w_in, True, finish, "projection")

    halo = from_before(tail)
    moving = None
    if turns == 2:
        moving = [from_before(gated_alone[:half]), from_before(gated_alone[half:])]
    query, gated, *totals = own_part(projected, halo, w_short, filters, forward)
    if moving is None:
        moving = [from_before(gated[:half]), from_before(gated[half:])]
    mixed = None
    for turn in range(1, turns):
        for part in range(2):
            if turn < turns - 1:
                totals[part] = far_part(
                    turn, part, moving[part], totals[part], filters, forward, None
                )
                moving[part] = from_before(moving[part])
            else:
                last = (inverse, query, gated, skip_gain, mixed)
                mixed = far_part(turn, part, moving[part], totals[part], filters, forward, last)

    (result,) = gather_products(
        ids, mixed, w_out[None], False, output_finish(channels, tokens), "output"
    )
    return result


def solution(mesh):
    placed = (
        P("fsdp", "ctx"),
        P("fsdp"),
        P(None, "fsdp", None),
        P(None, "fsdp", None),
        P("fsdp", None),
        P("fsdp"),
        P("fsdp", None),
    )
    return jax.shard_map(
        shards, mesh=mesh, in_specs=placed, out_specs=P("fsdp", "ctx"), check_vma=False
    )
```

```python
import math

import jax
import jax.numpy as jnp
import numpy as np
from jax import lax
from jax.experimental import pallas as pl
from jax.experimental.pallas import tpu as pltpu
from jax.sharding import PartitionSpec as P

epsilon = 1e-05
block_len = 128
STAGGER = 2e9
side_rows = 8
bf16 = jnp.bfloat16
f32 = jnp.float32
in_vmem = pl.BlockSpec(memory_space=pltpu.VMEM)
in_smem = pl.BlockSpec(memory_space=pltpu.SMEM)
params = pltpu.CompilerParams(vmem_limit_bytes=20 * 2**20)


def shape_of(shape, dtype):
    return jax.ShapeDtypeStruct(tuple(shape), dtype)


def dot(left, right):
    return jnp.dot(left, right, preferred_element_type=f32)


def column(row):
    return jnp.broadcast_to(row, (8, row.shape[1])).T[:, :1]


def tap_columns(taps):
    return jnp.concatenate([taps, jnp.zeros((8 - taps.shape[0], taps.shape[1]), f32)], axis=0).T


def estimate(flops, size):
    return pl.CostEstimate(flops=int(flops), bytes_accessed=int(size), transcendentals=0)


def prepare_kernel(ids_ref, x_ref, gain_ref, out_ref):
    rows = x_ref.shape[0]
    wide = x_ref[...].astype(f32)
    out_ref[:rows] = (wide * column(gain_ref[...])).astype(bf16)
    squares = jnp.sum(wide * wide, axis=0, keepdims=True)
    high = squares.astype(bf16).astype(f32)
    row = lax.broadcasted_iota(jnp.int32, (side_rows, wide.shape[1]), 0)
    side = jnp.where(row == 0, high, jnp.where(row == 1, squares - high, 0.0))
    out_ref[rows:] = side.astype(bf16)


def prepare(ids, x, gain):
    rows, tokens = x.shape
    return pl.pallas_call(
        prepare_kernel,
        in_specs=[in_smem, in_vmem, in_vmem],
        out_specs=in_vmem,
        out_shape=shape_of((rows + side_rows, tokens), bf16),
        compiler_params=params,
        name="prepare",
    )(ids, x, gain.reshape(1, rows))


def chip_count():
    return lax.axis_size("fsdp") // 2


def ring_order(count):
    return list(range(0, count, 2)) + list(range(1, count, 2))[::-1]


def along_ring(block):
    chips = chip_count()
    order = ring_order(chips)
    pairs = []
    for i in range(chips):
        here, after = order[i], order[(i + 1) % chips]
        pairs += [(2 * here, 2 * after), (2 * after + 1, 2 * here + 1)]
    return lax.ppermute(block, "fsdp", pairs)


def other_core(block):
    return lax.ppermute(block, "fsdp", [(i, i ^ 1) for i in range(2 * chip_count())])


def ring_ids():
    chips = chip_count()
    me = lax.axis_index("fsdp")
    chip, core = me // 2, me % 2
    place = jnp.where(chip % 2 == 0, chip // 2, chips - 1 - chip // 2)
    steps = jnp.arange(chips, dtype=jnp.int32)
    places = (place + jnp.where(core == 0, chips - steps, steps)) % chips
    ids = jnp.where(places < (chips + 1) // 2, 2 * places, 2 * (chips - 1 - places) + 1)
    return jnp.concatenate([ids, core[None]]).astype(jnp.int32)


def products(ids, items, weight, running, side, finish, cost, name):
    streams, out_rows, features = weight.shape
    rows = features // (2 * (ids.shape[0] - 1))
    shards = [shard for _, _, shard in items]
    tokens = shards[0].shape[1]
    count = len(shards)
    first_group = running is None
    state = [] if first_group else list(running)
    body, extras, out_shape = finish if finish else (None, [], None)
    padded = rows % 128 != 0
    width = 2 * rows if padded else rows
    scratch_shapes = [pltpu.VMEM((count * width, tokens), bf16)] if padded else []

    def kernel(ids_ref, *refs):
        refs = list(refs)
        take = lambda n: [refs.pop(0) for _ in range(n)]
        shard_refs = take(count)
        (weight_ref,) = take(1)
        state_refs = take(len(state))
        extra_refs = take(len(extras))
        outs = take(len(out_shape))
        core = ids_ref[ids_ref.shape[0] - 1]
        if padded:
            (beside_ref,) = refs
            beside_ref[...] = jnp.zeros(beside_ref.shape, bf16)
            for k, (_, other, _) in enumerate(items):
                at = k * width + jnp.where(core == other, 0, rows)
                beside_ref[pl.ds(pl.multiple_of(at, rows), rows)] = shard_refs[k][:rows]
            right = beside_ref[...]
        else:
            right = jnp.concatenate([ref[:rows] for ref in shard_refs], axis=0)
        side_sum = None
        if side:
            parts = [ref[rows:].astype(f32) for ref in shard_refs]
            parts += [] if first_group else [state_refs[1][...]]
            side_sum = sum(parts[1:], parts[0])

        def total(stream):
            left = []
            for slot, other, _ in items:
                block = ids_ref[slot]
                if not padded:
                    block = 2 * block + (1 - core if other else core)
                at = pl.ds(pl.multiple_of(block * width, width), width)
                left.append(weight_ref[stream, :, at])
            product = dot(jnp.concatenate(left, axis=1), right)
            return product if first_group else state_refs[0][stream] + product

        if body is not None:
            body(total, side_sum, extra_refs, outs)
            return
        for stream in range(streams):
            outs[0][stream] = total(stream)
        if side:
            outs[1][...] = side_sum

    aliases = {}
    if body is None:
        out_shape = [shape_of((streams, out_rows, tokens), f32)]
        if side:
            out_shape.append(shape_of((side_rows, tokens), f32))
        if not first_group:
            aliases = {1 + count + 1 + i: i for i in range(len(state))}
    return pl.pallas_call(
        kernel,
        in_specs=[in_smem] + [in_vmem] * (count + 1 + len(state) + len(extras)),
        out_specs=[in_vmem] * len(out_shape),
        out_shape=out_shape,
        scratch_shapes=scratch_shapes,
        input_output_aliases=aliases,
        compiler_params=params,
        cost_estimate=estimate(cost, 0),
        name=name,
    )(ids, *shards, weight, *state, *extras)


def gather_products(ids, own, weight, beside, side, finish, name):
    chips = chip_count()
    last_step = chips // 2

    def send(way, block, scope):
        with jax.named_scope(f"{name}_{scope}"):
            return way(block)

    near, far = own, send(other_core, own, "core_own")
    items = [(0, 0, near), (0, 1, far)]
    running = None
    for step in range(1, last_step + 1):
        near = send(along_ring, near, f"near_{step}")
        arrived = near
        if running is not None:
            arrived, *running = lax.optimization_barrier((near, *running))
        elif beside:
            arrived, *beside = lax.optimization_barrier((near, *beside))
        theirs = send(other_core, arrived, f"core_near_{step}")
        pair = [(step, 0, arrived), (chips - step, 1, theirs)]
        if step < last_step:
            running = products(ids, items + pair, weight, running, side, None, 0, f"{name}_{step}")
            far = send(along_ring, far, f"far_{step}")
            theirs = send(other_core, far, f"core_far_{step}")
            items = [(step, 1, far), (chips - step, 0, theirs)]
        else:
            running = products(ids, items, weight, running, side, None, STAGGER, f"{name}_{step}")
            items = pair
    result = products(ids, items, weight, running, side, finish, 0, f"{name}_last")
    return result, beside


def smooth(projected, taps, count, halo):
    lane = lax.broadcasted_iota(jnp.int32, projected.shape, 1)
    out = taps[:, :1] * projected
    for tap in range(1, count):
        moved = pltpu.roll(projected, tap, 1)
        for place in range(tap):
            edge = 0.0
            if halo is not None:
                at = halo.shape[1] - tap + place
                edge = halo[:, at : at + 1]
            moved = jnp.where(lane == place, edge, moved)
        out = out + taps[:, tap : tap + 1] * moved
    return out


def projection_finish(features, w_short, tokens):
    streams, count, channels = w_short.shape
    half = channels // 2

    def body(total, side_sum, extra_refs, outs):
        (taps_ref,) = extra_refs
        projected_ref, *message_refs = outs
        mean = jnp.sum(side_sum, axis=0, keepdims=True) * (1.0 / features)
        factor = lax.rsqrt(mean + epsilon)
        tails = []
        for stream in range(streams):
            projected = (total(stream) * factor).astype(bf16)
            projected_ref[stream] = projected
            tail = projected[:, tokens - block_len :].astype(f32).T
            tails.append(tail[block_len - count + 1 :])
        taps = [tap_columns(taps_ref[stream]) for stream in (1, 2)]
        tile = min(half, 64)
        for part, message_ref in enumerate(message_refs):
            for start in range(0, half, tile):
                rows = slice(part * half + start, part * half + start + tile)
                key, value = (
                    smooth(projected_ref[s, rows].astype(f32), taps[s - 1][rows], count, None)
                    for s in (1, 2)
                )
                message_ref[start : start + tile] = (key * value).astype(bf16)
            rows = tails + [jnp.zeros((side_rows - streams * (count - 1), channels), f32)]
            side = jnp.concatenate(rows, axis=0)[:, part * half : (part + 1) * half]
            width = min(half, tokens)
            message_ref[half:] = jnp.zeros((side_rows, tokens), bf16)
            message_ref[half:, :width] = side.astype(bf16)

    message = shape_of((half + side_rows, tokens), bf16)
    return body, [w_short], [shape_of((streams, channels, tokens), bf16), message, message]


def halo_columns(message_ref, streams, count):
    half = message_ref.shape[0] - side_rows
    side = message_ref[half:, :half].astype(f32).T
    return [side[:, s * (count - 1) : (s + 1) * (count - 1)] for s in range(streams)]


def split_table(table):
    high = table.astype(bf16)
    low = (table - high.astype(np.float64)).astype(bf16)
    return np.stack([high, low])


def dft_tables():
    size = 2 * block_len
    freq = np.arange(block_len) + 0.5
    angle = 2.0 * math.pi / size * np.arange(size)[:, None] * freq[None, :]
    forward = np.concatenate([np.cos(angle), -np.sin(angle)], axis=1)
    back = angle[block_len:].T
    inverse = np.concatenate([np.cos(back), -np.sin(back)], axis=0) * (2.0 / size)
    return split_table(forward), split_table(inverse)


def spectrum_lanes(k):
    return slice(2 * k * block_len, 2 * (k + 1) * block_len)


def block_lanes(k):
    return slice(k * block_len, (k + 1) * block_len)


def filter_spectra(long_filter, table):
    channels, lags = long_filter.shape

    def kernel(filter_ref, table_ref, spectra_ref):
        before = jnp.zeros((channels, block_len), bf16)
        for k in range(lags // block_len):
            now = filter_ref[:, block_lanes(k)]
            segment = jnp.concatenate([before, now], axis=1)
            spectrum = dot(segment, table_ref[0]) + dot(segment, table_ref[1])
            spectra_ref[:, spectrum_lanes(k)] = spectrum
            before = now

    return pl.pallas_call(
        kernel,
        in_specs=[in_vmem, in_vmem],
        out_specs=in_vmem,
        out_shape=shape_of((channels, 2 * lags), f32),
        compiler_params=params,
        cost_estimate=estimate(8 * channels * lags * 2 * block_len, 10 * channels * lags),
        name="filter_spectra",
    )(long_filter, table)


def block_spectrum(block, table_ref):
    return dot(block, table_ref[0, :block_len]) + dot(block, table_ref[1, :block_len])


def block_spectra(gated_ref, rows, table_ref, spec_ref, first):
    for b in range(first, gated_ref.shape[1] // block_len):
        spec_ref[:, spectrum_lanes(b)] = block_spectrum(gated_ref[:rows, block_lanes(b)], table_ref)


def multiply_spectra(source_ref, filters_ref, filter_start, pairs, before_ref, total_ref):
    def one_tile(i, carry):
        here = pl.ds(pl.multiple_of(i * 8, 8), 8)
        there = pl.ds(pl.multiple_of(filter_start + i * 8, 8), 8)

        def part(ref, rows, k, imaginary):
            start = (2 * k + imaginary) * block_len
            return ref[rows, start : start + block_len]

        for a, terms in enumerate(pairs):
            real = imag = None
            if before_ref is not None:
                real, imag = part(before_ref, here, a, 0), part(before_ref, here, a, 1)
            for b, d in terms:
                gr, gi = part(source_ref, here, b, 0), part(source_ref, here, b, 1)
                hr, hi = part(filters_ref, there, d, 0), part(filters_ref, there, d, 1)
                more_real, more_imag = gr * hr - gi * hi, gr * hi + gi * hr
                real = more_real if real is None else real + more_real
                imag = more_imag if imag is None else imag + more_imag
            if real is None:
                real = imag = jnp.zeros((8, block_len), f32)
            start = 2 * a * block_len
            total_ref[here, start : start + block_len] = real
            total_ref[here, start + block_len : start + 2 * block_len] = imag
        return carry

    lax.fori_loop(0, total_ref.shape[0] // 8, one_tile, 0)


def own_part(projected, messages, moved, taps, filters, table):
    streams, channels, tokens = projected.shape
    half = channels // 2
    count = taps.shape[1]
    blocks = tokens // block_len
    first = 0 if moved else 1
    pairs = [[(b, a - b) for b in range(first, a + 1)] for a in range(blocks)]
    inputs = list(moved or messages)

    def kernel(projected_ref, one_ref, two_ref, taps_ref, filters_ref, table_ref, *refs):
        *refs, spec_ref = refs
        query_refs, total_refs, gated_refs = refs[:2], refs[2:4], refs[4:]
        columns = [tap_columns(taps_ref[s]) for s in range(streams)]
        tile = min(half, 64)
        for part, message_ref in enumerate((one_ref, two_ref)):
            halo = [None] * streams
            if moved:
                halo = halo_columns(message_ref, streams, count)
            for start in range(0, half, tile):
                here = slice(start, start + tile)
                rows = slice(part * half + start, part * half + start + tile)

                def smoothed(s):
                    edge = halo[s][here] if moved else None
                    wide = projected_ref[s, rows].astype(f32)
                    return smooth(wide, columns[s][rows], count, edge)

                query_refs[part][here] = smoothed(0)
                if moved:
                    gated_refs[part][here] = (smoothed(1) * smoothed(2)).astype(bf16)
            source_ref = gated_refs[part] if moved else message_ref
            block_spectra(source_ref, half, table_ref, spec_ref, first)
            multiply_spectra(spec_ref, filters_ref, part * half, pairs, None, total_refs[part])

    out_shape = [shape_of((half, tokens), f32)] * 2 + [shape_of((half, 2 * tokens), f32)] * 2
    if moved:
        out_shape += [shape_of((half, tokens), bf16)] * 2
    outs = pl.pallas_call(
        kernel,
        in_specs=[in_vmem] * 6,
        out_specs=[in_vmem] * len(out_shape),
        out_shape=out_shape,
        scratch_shapes=[pltpu.VMEM((half, 2 * tokens), f32)],
        compiler_params=params,
        cost_estimate=estimate(6 * 10**8, 6 * 10**6),
        name="own_part",
    )(projected, *inputs, taps, filters, table)
    return list(outs[:2]), list(outs[2:4]), list(outs[4:]) if moved else messages


def far_part(turn, part, moved, total, filters, table, last, own):
    rows, tokens = total.shape[0], moved.shape[1]
    blocks = tokens // block_len
    pairs = [[(b, turn * blocks + a - b) for b in range(blocks)] for a in range(blocks)]
    if own:
        pairs = [terms + [(blocks, a)] for a, terms in enumerate(pairs)]
    channels_here = slice(part * rows, (part + 1) * rows)

    def kernel(*refs):
        refs = list(refs)
        take = lambda n: [refs.pop(0) for _ in range(n)]
        moved_ref, total_ref, filters_ref, table_ref = take(4)
        own_refs = take(2) if own else None
        spec_ref = refs.pop()
        if last is None:
            block_spectra(moved_ref, rows, table_ref, spec_ref, 0)
            multiply_spectra(spec_ref, filters_ref, part * rows, pairs, total_ref, refs[0])
            return
        sum_ref = refs.pop()
        back_ref, query_ref, gated_ref, skip_ref = take(4)
        out_ref = refs[-1]
        query, gated = (
            [ref[:rows, block_lanes(a)] for a in range(blocks)] for ref in (query_ref, gated_ref)
        )
        if own:
            projected_ref, taps_ref = own_refs
            streams, count, _ = taps_ref.shape
            halo = halo_columns(moved_ref, streams, count)
            smoothed = []
            for s in range(streams):
                columns = tap_columns(taps_ref[s, :, channels_here])
                wide = projected_ref[s, channels_here, :block_len].astype(f32)
                smoothed.append(smooth(wide, columns, count, halo[s]))
            query[0] = smoothed[0]
            gated[0] = (smoothed[1] * smoothed[2]).astype(bf16)
            spec_ref[:, spectrum_lanes(blocks)] = block_spectrum(gated[0], table_ref)
        block_spectra(moved_ref, rows, table_ref, spec_ref, 0)
        multiply_spectra(spec_ref, filters_ref, part * rows, pairs, total_ref, sum_ref)
        skip = column(skip_ref[...])[channels_here]
        for a in range(blocks):
            spectrum = sum_ref[:, spectrum_lanes(a)]
            high = spectrum.astype(bf16)
            low = (spectrum - high.astype(f32)).astype(bf16)
            filtered = dot(high, back_ref[0]) + (dot(low, back_ref[0]) + dot(high, back_ref[1]))
            mixed = query[a] * (filtered + skip * gated[a].astype(f32))
            out_ref[channels_here, block_lanes(a)] = mixed.astype(bf16)

    args = [moved, total, filters, table]
    if own:
        args += list(own)
    aliases = {}
    scratch = [pltpu.VMEM((rows, 2 * (blocks + 1) * block_len), f32)]
    out_shape = shape_of((rows, 2 * tokens), f32)
    if last is not None:
        inverse, query, gated, skip, mixed = last
        args += [inverse, query, gated, skip.reshape(1, 2 * rows)]
        if mixed is not None:
            aliases = {len(args): 0}
            args.append(mixed)
        out_shape = shape_of((2 * rows, tokens), bf16)
        scratch.append(pltpu.VMEM((rows, 2 * tokens), f32))
    return pl.pallas_call(
        kernel,
        in_specs=[in_vmem] * len(args),
        out_specs=in_vmem,
        out_shape=out_shape,
        scratch_shapes=scratch[::-1],
        input_output_aliases=aliases,
        compiler_params=params,
        cost_estimate=estimate(4 * 10**8, 4 * 10**6),
        name=f"far_part_{turn}_{part}",
    )(*args)


def from_before(block):
    count = lax.axis_size("ctx")
    return lax.ppermute(block, "ctx", [(i - 1, i) for i in range(1, count)])


def output_finish(channels, tokens):
    def body(total, side_sum, extra_refs, outs):
        outs[0][...] = total(0).astype(bf16)

    return body, [], [shape_of((channels, tokens), bf16)]


def shards(activations, norm_gain, w_in, w_short, long_filter, skip_gain, w_out):
    channels, tokens = activations.shape
    features = w_in.shape[2]
    w_short = w_short.transpose(0, 2, 1)
    turns = lax.axis_size("ctx")
    forward, inverse = (jnp.asarray(t) for t in dft_tables())
    ids = ring_ids()
    own = prepare(ids, activations, norm_gain)

    finish = projection_finish(features, w_short, tokens)
    beside = [filter_spectra(long_filter, forward)]
    (projected, *messages), (filters,) = gather_products(
        ids, own, w_in, beside, True, finish, "projection"
    )
    moving = [from_before(message) for message in messages]
    exact = turns > 2
    query, totals, gated = own_part(
        projected, messages, moving if exact else None, w_short, filters, forward
    )
    if exact:
        moving = [from_before(part) for part in gated]
    mixed = None
    for turn in range(1, turns):
        for part in range(2):
            if turn < turns - 1:
                totals[part] = far_part(
                    turn, part, moving[part], totals[part], filters, forward, None, None
                )
                moving[part] = from_before(moving[part])
            else:
                last = (inverse, query[part], gated[part], skip_gain, mixed)
                first_block = None if exact else (projected, w_short)
                mixed = far_part(
                    turn, part, moving[part], totals[part], filters, forward, last, first_block
                )

    finish = output_finish(channels, tokens)
    (result,), _ = gather_products(ids, mixed, w_out[None], [], False, finish, "output")
    return result


def solution(mesh):
    placed = (
        P("fsdp", "ctx"),
        P("fsdp"),
        P(None, "fsdp", None),
        P(None, "fsdp", None),
        P("fsdp", None),
        P("fsdp"),
        P("fsdp", None),
    )
    return jax.shard_map(
        shards, mesh=mesh, in_specs=placed, out_specs=P("fsdp", "ctx"), check_vma=False
    )
```

```python
import math

import jax
import jax.numpy as jnp
import numpy as np
from jax import lax
from jax.experimental import pallas as pl
from jax.experimental.pallas import tpu as pltpu
from jax.sharding import PartitionSpec as P

epsilon = 1e-05
block_len = 128
STAGGER = 2e9
side_rows = 8
bf16 = jnp.bfloat16
f32 = jnp.float32
in_vmem = pl.BlockSpec(memory_space=pltpu.VMEM)
in_smem = pl.BlockSpec(memory_space=pltpu.SMEM)
params = pltpu.CompilerParams(vmem_limit_bytes=12 * 2**20)


def shape_of(shape, dtype):
    return jax.ShapeDtypeStruct(tuple(shape), dtype)


def dot(left, right):
    return jnp.dot(left, right, preferred_element_type=f32)


def column(row):
    return jnp.broadcast_to(row, (8, row.shape[1])).T[:, :1]


def tap_columns(taps):
    return jnp.concatenate([taps, jnp.zeros((8 - taps.shape[0], taps.shape[1]), f32)], axis=0).T


def estimate(flops, size):
    return pl.CostEstimate(flops=int(flops), bytes_accessed=int(size), transcendentals=0)


def prepare_kernel(ids_ref, x_ref, gain_ref, out_ref):
    rows = x_ref.shape[0]
    wide = x_ref[...].astype(f32)
    out_ref[:rows] = (wide * column(gain_ref[...])).astype(bf16)
    squares = jnp.sum(wide * wide, axis=0, keepdims=True)
    high = squares.astype(bf16).astype(f32)
    row = lax.broadcasted_iota(jnp.int32, (side_rows, wide.shape[1]), 0)
    side = jnp.where(row == 0, high, jnp.where(row == 1, squares - high, 0.0))
    out_ref[rows:] = side.astype(bf16)


def prepare(ids, x, gain):
    rows, tokens = x.shape
    return pl.pallas_call(
        prepare_kernel,
        in_specs=[in_smem, in_vmem, in_vmem],
        out_specs=in_vmem,
        out_shape=shape_of((rows + side_rows, tokens), bf16),
        compiler_params=params,
        cost_estimate=estimate(3e9, 0),
        name="prepare",
    )(ids, x, gain.reshape(1, rows))


def chip_count():
    return lax.axis_size("fsdp") // 2


def ring_order(count):
    return list(range(0, count, 2)) + list(range(1, count, 2))[::-1]


def along_ring(block):
    chips = chip_count()
    order = ring_order(chips)
    pairs = []
    for i in range(chips):
        here, after = order[i], order[(i + 1) % chips]
        pairs += [(2 * here, 2 * after), (2 * after + 1, 2 * here + 1)]
    return lax.ppermute(block, "fsdp", pairs)


def other_core(block):
    return lax.ppermute(block, "fsdp", [(i, i ^ 1) for i in range(2 * chip_count())])


def ring_ids():
    chips = chip_count()
    me = lax.axis_index("fsdp")
    chip, core = me // 2, me % 2
    place = jnp.where(chip % 2 == 0, chip // 2, chips - 1 - chip // 2)
    steps = jnp.arange(chips, dtype=jnp.int32)
    places = (place + jnp.where(core == 0, chips - steps, steps)) % chips
    ids = jnp.where(places < (chips + 1) // 2, 2 * places, 2 * (chips - 1 - places) + 1)
    mine = jnp.stack([core, lax.axis_index("ctx")])
    return jnp.concatenate([ids, mine]).astype(jnp.int32)


def core_of(ids_ref):
    return ids_ref[ids_ref.shape[0] - 2]


def turn_of(ids_ref):
    return ids_ref[ids_ref.shape[0] - 1]


def products(ids, items, weight, running, side, finish, cost, name, cut=(0, 1)):
    streams, out_rows, features = weight.shape
    out_rows //= cut[1]
    out_here = slice(cut[0] * out_rows, (cut[0] + 1) * out_rows)
    rows = features // lax.axis_size("fsdp")
    shards = [shard for _, _, shard in items]
    tokens = shards[0].shape[1]
    count = len(shards)
    first_group = running is None
    state = [] if first_group else list(running)
    body, extras, out_shape = finish if finish else (None, [], None)
    padded = rows % 128 != 0
    width = 2 * rows if padded else rows
    scratch_shapes = [pltpu.VMEM((count * width, tokens), bf16)] if padded else []

    def kernel(ids_ref, *refs):
        refs = list(refs)
        take = lambda n: [refs.pop(0) for _ in range(n)]
        shard_refs = take(count)
        (weight_ref,) = take(1)
        state_refs = take(len(state))
        extra_refs = take(len(extras))
        outs = take(len(out_shape))
        core = core_of(ids_ref)
        if padded:
            (beside_ref,) = refs
            beside_ref[...] = jnp.zeros(beside_ref.shape, bf16)
            for k, (_, other, _) in enumerate(items):
                at = k * width + jnp.where(core == other, 0, rows)
                beside_ref[pl.ds(pl.multiple_of(at, rows), rows)] = shard_refs[k][:rows]
            right = beside_ref[...]
        else:
            right = jnp.concatenate([ref[:rows] for ref in shard_refs], axis=0)
        side_sum = None
        if side:
            parts = [ref[rows:].astype(f32) for ref in shard_refs]
            parts += [] if first_group else [state_refs[1][...]]
            side_sum = sum(parts[1:], parts[0])

        def total(stream):
            left = []
            for slot, other, _ in items:
                block = ids_ref[slot]
                if not padded:
                    block = 2 * block + (1 - core if other else core)
                at = pl.ds(pl.multiple_of(block * width, width), width)
                left.append(weight_ref[stream, out_here, at])
            product = dot(jnp.concatenate(left, axis=1), right)
            return product if first_group else state_refs[0][stream, out_here] + product

        if body is not None:
            body(total, side_sum, extra_refs, outs)
            return
        for stream in range(streams):
            outs[0][stream] = total(stream)
        if side:
            outs[1][...] = side_sum

    aliases = {}
    if body is None:
        out_shape = [shape_of((streams, out_rows, tokens), f32)]
        if side:
            out_shape.append(shape_of((side_rows, tokens), f32))
        if not first_group:
            aliases = {1 + count + 1 + i: i for i in range(len(state))}
    return pl.pallas_call(
        kernel,
        in_specs=[in_smem] + [in_vmem] * (count + 1 + len(state) + len(extras)),
        out_specs=[in_vmem] * len(out_shape),
        out_shape=out_shape,
        scratch_shapes=scratch_shapes,
        input_output_aliases=aliases,
        compiler_params=params,
        cost_estimate=estimate(cost, 0),
        name=name,
    )(ids, *shards, weight, *state, *extras)


def gather_products(ids, own, weight, beside, side, finish, name):
    chips = chip_count()
    last_step = chips // 2

    def send(way, block, scope):
        with jax.named_scope(f"{name}_{scope}"):
            return way(block)

    near, far = own, send(other_core, own, "core_own")
    items = [(0, 0, near), (0, 1, far)]
    running = None
    for step in range(1, last_step + 1):
        near = send(along_ring, near, f"near_{step}")
        arrived = near
        if running is not None:
            arrived, *running = lax.optimization_barrier((near, *running))
        elif beside:
            arrived, *beside = lax.optimization_barrier((near, *beside))
        theirs = send(other_core, arrived, f"core_near_{step}")
        pair = [(step, 0, arrived), (chips - step, 1, theirs)]
        if step < last_step:
            running = products(ids, items + pair, weight, running, side, None, 0, f"{name}_{step}")
            far = send(along_ring, far, f"far_{step}")
            theirs = send(other_core, far, f"core_far_{step}")
            items = [(step, 1, far), (chips - step, 0, theirs)]
        else:
            running = products(ids, items, weight, running, side, None, STAGGER, f"{name}_{step}")
            items = pair
    results = [
        products(ids, items, weight, running, side, end, 0, f"{name}_last_{k}", (k, len(finish)))
        for k, end in enumerate(finish)
    ]
    return results, beside


def smooth(projected, taps, count, halo):
    lane = lax.broadcasted_iota(jnp.int32, projected.shape, 1)
    out = taps[:, :1] * projected
    for tap in range(1, count):
        moved = pltpu.roll(projected, tap, 1)
        for place in range(tap):
            edge = 0.0
            if halo is not None:
                at = halo.shape[1] - tap + place
                edge = halo[:, at : at + 1]
            moved = jnp.where(lane == place, edge, moved)
        out = out + taps[:, tap : tap + 1] * moved
    return out


def channel_parts(channels):
    return [(0, channels // 2), (channels // 2, channels // 2)]


def projection_finish(features, w_short, tokens, half_index):
    streams, count, channels = w_short.shape
    half = channels // 2
    begin = half_index * half
    parts = [part for part in channel_parts(channels) if begin <= part[0] < begin + half]

    def body(total, side_sum, extra_refs, outs):
        (taps_ref,) = extra_refs
        projected_ref, *message_refs = outs
        mean = jnp.sum(side_sum, axis=0, keepdims=True) * (1.0 / features)
        factor = lax.rsqrt(mean + epsilon)
        tails = []
        for stream in range(streams):
            projected = (total(stream) * factor).astype(bf16)
            projected_ref[stream] = projected
            tail = projected[:, tokens - block_len :].astype(f32).T
            tails.append(tail[block_len - count + 1 :])
        tails.append(jnp.zeros((side_rows - streams * (count - 1), half), f32))
        side = jnp.concatenate(tails, axis=0)
        taps = [tap_columns(taps_ref[stream]) for stream in (1, 2)]
        for (first, rows), message_ref in zip(parts, message_refs):
            tile = min(rows, 64)
            for start in range(first, first + rows, tile):
                here = slice(start - begin, start - begin + tile)
                key, value = (
                    smooth(
                        projected_ref[s, here].astype(f32),
                        taps[s - 1][start : start + tile],
                        count,
                        None,
                    )
                    for s in (1, 2)
                )
                message_ref[start - first : start - first + tile] = (key * value).astype(bf16)
            message_ref[rows:] = jnp.zeros((side_rows, tokens), bf16)
            here = side[:, first - begin : first - begin + rows]
            message_ref[rows:, :rows] = here.astype(bf16)

    out_shape = [shape_of((streams, half, tokens), bf16)]
    out_shape += [shape_of((rows + side_rows, tokens), bf16) for _, rows in parts]
    return body, [w_short], out_shape


def halo_columns(message_ref, streams, count, inside):
    rows = message_ref.shape[0] - side_rows
    side = jnp.where(inside, message_ref[rows:, :rows].astype(f32), 0.0).T
    return [side[:, s * (count - 1) : (s + 1) * (count - 1)] for s in range(streams)]


def split_table(table):
    high = table.astype(bf16)
    return high, (table - high.astype(np.float64)).astype(bf16)


def dft_tables():
    size = 2 * block_len
    freq = np.arange(block_len) + 0.5
    angle = 2.0 * math.pi / size * np.arange(size)[:, None] * freq[None, :]
    high, low = split_table(np.concatenate([np.cos(angle), -np.sin(angle)], axis=1))
    block = np.concatenate([high[:block_len], low[:block_len]])
    segment = np.concatenate([high, low])
    back = angle[block_len:].T
    inverse = np.concatenate([np.cos(back), -np.sin(back)], axis=0) * (2.0 / size)
    high, low = split_table(inverse)
    return block, segment, np.concatenate([high, low], axis=1)


def spectrum_lanes(k):
    return slice(2 * k * block_len, 2 * (k + 1) * block_len)


def block_lanes(k):
    return slice(k * block_len, (k + 1) * block_len)


def filter_spectra(long_filter, table):
    channels, lags = long_filter.shape

    def kernel(filter_ref, table_ref, spectra_ref):
        before = jnp.zeros((channels, block_len), bf16)
        for k in range(lags // block_len):
            now = filter_ref[:, block_lanes(k)]
            segment = jnp.concatenate([before, now, before, now], axis=1)
            spectra_ref[:, spectrum_lanes(k)] = dot(segment, table_ref[...])
            before = now

    return pl.pallas_call(
        kernel,
        in_specs=[in_vmem, in_vmem],
        out_specs=in_vmem,
        out_shape=shape_of((channels, 2 * lags), f32),
        compiler_params=params,
        cost_estimate=estimate(6e9, 0),
        name="filter_spectra",
    )(long_filter, table)


def block_spectra(pieces, table_ref, spec_ref, first):
    rows = pieces[0].shape[0]
    stacked = jnp.concatenate(pieces, axis=0)
    spectra = dot(jnp.concatenate([stacked, stacked], axis=1), table_ref[...])
    for k in range(len(pieces)):
        spec_ref[:rows, spectrum_lanes(first + k)] = spectra[k * rows : (k + 1) * rows]


def multiply_spectra(source_ref, filters_ref, filter_start, pairs, before_ref, total_ref):
    def one_tile(i, carry):
        here = pl.ds(pl.multiple_of(i * 8, 8), 8)
        there = pl.ds(pl.multiple_of(filter_start + i * 8, 8), 8)

        def parts(ref, rows, k):
            start = 2 * k * block_len
            return (
                ref[rows, start : start + block_len],
                ref[rows, start + block_len : start + 2 * block_len],
            )

        used = [term for terms in pairs for term in terms]
        sources = {b: parts(source_ref, here, b) for b in sorted({b for b, _ in used})}
        filters = {d: parts(filters_ref, there, d) for d in sorted({d for _, d in used})}
        for a, terms in enumerate(pairs):
            real = imag = None
            if before_ref is not None:
                real, imag = parts(before_ref, here, a)
            for b, d in terms:
                gr, gi = sources[b]
                hr, hi = filters[d]
                more_real, more_imag = gr * hr - gi * hi, gr * hi + gi * hr
                real = more_real if real is None else real + more_real
                imag = more_imag if imag is None else imag + more_imag
            if real is None:
                real = imag = jnp.zeros((8, block_len), f32)
            start = 2 * a * block_len
            total_ref[here, start : start + block_len] = real
            total_ref[here, start + block_len : start + 2 * block_len] = imag
        return carry

    lax.fori_loop(0, total_ref.shape[0] // 8, one_tile, 0)


def own_part(ids, projected, messages, moved, taps, filters, table):
    streams, half, tokens = projected[0].shape
    parts = channel_parts(2 * half)
    number = len(parts)
    count = taps.shape[1]
    blocks = tokens // block_len
    first = 0 if moved else 1
    pairs = [[(b, a - b) for b in range(first, a + 1)] for a in range(blocks)]

    def kernel(ids_ref, *refs):
        refs = list(refs)
        take = lambda n: [refs.pop(0) for _ in range(n)]
        projected_refs, message_refs = take(2), take(number)
        taps_ref, filters_ref, table_ref = take(3)
        query_refs, total_refs = take(number), take(number)
        gated_refs = take(number) if moved else None
        (spec_ref,) = refs
        columns = [tap_columns(taps_ref[s]) for s in range(streams)]
        for part, (begin, rows) in enumerate(parts):
            if moved:
                inside = turn_of(ids_ref) > 0
                halo = halo_columns(message_refs[part], streams, count, inside)
            tile = min(rows, 64)
            for start in range(0, rows, tile):
                here = slice(start, start + tile)
                there = slice(begin + start, begin + start + tile)
                in_half = (begin + start) % half
                projected_ref = projected_refs[begin // half]

                def smoothed(s):
                    edge = halo[s][here] if moved else None
                    wide = projected_ref[s, in_half : in_half + tile].astype(f32)
                    return smooth(wide, columns[s][there], count, edge)

                query_refs[part][here] = smoothed(0)
                if moved:
                    gated_refs[part][here] = (smoothed(1) * smoothed(2)).astype(bf16)
            source_ref = gated_refs[part] if moved else message_refs[part]
            pieces = [source_ref[:rows, block_lanes(b)] for b in range(first, blocks)]
            block_spectra(pieces, table_ref, spec_ref, first)
            multiply_spectra(spec_ref, filters_ref, begin, pairs, None, total_refs[part])

    out_shape = [shape_of((rows, tokens), f32) for _, rows in parts]
    out_shape += [shape_of((rows, 2 * tokens), f32) for _, rows in parts]
    if moved:
        out_shape += [shape_of((rows, tokens), bf16) for _, rows in parts]
    inputs = [*projected, *(moved or messages), taps, filters, table]
    outs = pl.pallas_call(
        kernel,
        in_specs=[in_smem] + [in_vmem] * len(inputs),
        out_specs=[in_vmem] * len(out_shape),
        out_shape=out_shape,
        scratch_shapes=[pltpu.VMEM((half, 2 * tokens), f32)],
        compiler_params=params,
        cost_estimate=estimate(0, 0),
        name="own_part",
    )(ids, *inputs)
    gated = list(outs[2 * number :]) if moved else messages
    return list(outs[:number]), list(outs[number : 2 * number]), gated


def far_part(ids, turn, begin, moved, total, filters, table, last, own):
    rows, tokens = total.shape[0], moved.shape[1]
    blocks = tokens // block_len
    pairs = [[(b, turn * blocks + a - b) for b in range(blocks)] for a in range(blocks)]
    if own:
        pairs = [terms + [(blocks, a)] for a, terms in enumerate(pairs)]
    channels_here = slice(begin, begin + rows)

    def kernel(ids_ref, *refs):
        refs = list(refs)
        take = lambda n: [refs.pop(0) for _ in range(n)]
        moved_ref, total_ref, filters_ref, table_ref = take(4)
        own_refs = take(2) if own else None
        spec_ref = refs.pop()
        inside = turn_of(ids_ref) >= turn
        pieces = [
            jnp.where(inside, moved_ref[:rows, block_lanes(b)], jnp.zeros((), bf16))
            for b in range(blocks)
        ]
        if last is None:
            block_spectra(pieces, table_ref, spec_ref, 0)
            multiply_spectra(spec_ref, filters_ref, begin, pairs, total_ref, refs[0])
            return
        sum_ref = refs.pop()
        back_ref, query_ref, gated_ref, skip_ref = take(4)
        out_ref = refs[-1]
        query, gated = (
            [ref[:rows, block_lanes(a)] for a in range(blocks)] for ref in (query_ref, gated_ref)
        )
        if own:
            projected_ref, taps_ref = own_refs
            streams, count, _ = taps_ref.shape
            halo = halo_columns(moved_ref, streams, count, inside)
            in_half = begin % projected_ref.shape[1]
            smoothed = []
            for s in range(streams):
                columns = tap_columns(taps_ref[s])[channels_here]
                wide = projected_ref[s, in_half : in_half + rows, :block_len].astype(f32)
                smoothed.append(smooth(wide, columns, count, halo[s]))
            query[0] = smoothed[0]
            gated[0] = (smoothed[1] * smoothed[2]).astype(bf16)
            pieces.append(gated[0])
        block_spectra(pieces, table_ref, spec_ref, 0)
        multiply_spectra(spec_ref, filters_ref, begin, pairs, total_ref, sum_ref)
        skip = column(skip_ref[...])[channels_here]
        spectra = [sum_ref[:, spectrum_lanes(a)] for a in range(blocks)]
        highs = [spectrum.astype(bf16) for spectrum in spectra]
        lows = [(s - high.astype(f32)).astype(bf16) for s, high in zip(spectra, highs)]
        both = dot(jnp.concatenate(highs, axis=0), back_ref[...])
        small = dot(jnp.concatenate(lows, axis=0), back_ref[:, :block_len])
        filtered = both[:, :block_len] + (both[:, block_len:] + small)
        for a in range(blocks):
            here = filtered[a * rows : (a + 1) * rows]
            mixed = query[a] * (here + skip * gated[a].astype(f32))
            out_ref[channels_here, block_lanes(a)] = mixed.astype(bf16)

    args = [moved, total, filters, table]
    if own:
        args += list(own)
    aliases = {}
    scratch = [pltpu.VMEM((rows, 2 * (blocks + 1) * block_len), f32)]
    out_shape = shape_of((rows, 2 * tokens), f32)
    if last is not None:
        inverse, query, gated, skip, mixed = last
        channels = skip.shape[0]
        args += [inverse, query, gated, skip.reshape(1, channels)]
        if mixed is not None:
            aliases = {1 + len(args): 0}
            args.append(mixed)
        out_shape = shape_of((channels, tokens), bf16)
        scratch.append(pltpu.VMEM((rows, 2 * tokens), f32))
    return pl.pallas_call(
        kernel,
        in_specs=[in_smem] + [in_vmem] * len(args),
        out_specs=in_vmem,
        out_shape=out_shape,
        scratch_shapes=scratch[::-1],
        input_output_aliases=aliases,
        compiler_params=params,
        cost_estimate=estimate(0, 0),
        name=f"far_part_{turn}_{begin}",
    )(ids, *args)


def from_before(block):
    count = lax.axis_size("ctx")
    return lax.ppermute(block, "ctx", [(i, (i + 1) % count) for i in range(count)])


def output_finish(channels, tokens):
    def body(total, side_sum, extra_refs, outs):
        outs[0][...] = total(0).astype(bf16)

    return body, [], [shape_of((channels, tokens), bf16)]


def shards(activations, norm_gain, w_in, w_short, long_filter, skip_gain, w_out):
    channels, tokens = activations.shape
    features = w_in.shape[2]
    w_short = w_short.transpose(0, 2, 1)
    turns = lax.axis_size("ctx")
    parts = channel_parts(channels)
    forward, segments, inverse = (jnp.asarray(t) for t in dft_tables())
    ids = ring_ids()
    own = prepare(ids, activations, norm_gain)

    filters = filter_spectra(long_filter, segments)
    finish = [projection_finish(features, w_short, tokens, k) for k in range(2)]
    results, (filters,) = gather_products(ids, own, w_in, [filters], True, finish, "projection")
    projected = [result[0] for result in results]
    messages = [message for result in results for message in result[1:]]
    moving = [from_before(message) for message in messages]
    exact = turns > 2
    query, totals, gated = own_part(
        ids, projected, messages, moving if exact else None, w_short, filters, forward
    )
    if exact:
        moving = [from_before(part) for part in gated]
    mixed = None
    for turn in range(1, turns):
        for k, (begin, _) in enumerate(parts):
            last = own_block = None
            if turn == turns - 1:
                last = (inverse, query[k], gated[k], skip_gain, mixed)
                if not exact:
                    own_block = (projected[2 * begin // channels], w_short)
            done = far_part(
                ids, turn, begin, moving[k], totals[k], filters, forward, last, own_block
            )
            if last is None:
                totals[k] = done
                moving[k] = from_before(moving[k])
            else:
                mixed = done

    finish = [output_finish(channels, tokens)]
    ((result,),), _ = gather_products(ids, mixed, w_out[None], [], False, finish, "output")
    return result


def solution(mesh):
    placed = (
        P("fsdp", "ctx"),
        P("fsdp"),
        P(None, "fsdp", None),
        P(None, "fsdp", None),
        P("fsdp", None),
        P("fsdp"),
        P("fsdp", None),
    )
    return jax.shard_map(
        shards, mesh=mesh, in_specs=placed, out_specs=P("fsdp", "ctx"), check_vma=False
    )
```

```python
import math

import jax
import jax.numpy as jnp
import numpy as np
from jax import lax
from jax.experimental import pallas as pl
from jax.experimental.pallas import tpu as pltpu
from jax.sharding import PartitionSpec as P

epsilon = 1e-05
block_len = 128
STAGGER = 2e9
side_rows = 8
bf16 = jnp.bfloat16
f32 = jnp.float32
in_vmem = pl.BlockSpec(memory_space=pltpu.VMEM)
in_smem = pl.BlockSpec(memory_space=pltpu.SMEM)
params = pltpu.CompilerParams(vmem_limit_bytes=12 * 2**20)


def shape_of(shape, dtype):
    return jax.ShapeDtypeStruct(tuple(shape), dtype)


def dot(left, right):
    return jnp.dot(left, right, preferred_element_type=f32)


def column(row):
    return jnp.broadcast_to(row, (8, row.shape[1])).T[:, :1]


def tap_columns(taps):
    return jnp.concatenate([taps, jnp.zeros((8 - taps.shape[0], taps.shape[1]), f32)], axis=0).T


def estimate(flops, size):
    return pl.CostEstimate(flops=int(flops), bytes_accessed=int(size), transcendentals=0)


def prepare_kernel(ids_ref, x_ref, gain_ref, out_ref):
    rows = x_ref.shape[0]
    wide = x_ref[...].astype(f32)
    out_ref[:rows] = (wide * column(gain_ref[...])).astype(bf16)
    squares = jnp.sum(wide * wide, axis=0, keepdims=True)
    high = squares.astype(bf16).astype(f32)
    row = lax.broadcasted_iota(jnp.int32, (side_rows, wide.shape[1]), 0)
    side = jnp.where(row == 0, high, jnp.where(row == 1, squares - high, 0.0))
    out_ref[rows:] = side.astype(bf16)


def prepare(ids, x, gain):
    rows, tokens = x.shape
    return pl.pallas_call(
        prepare_kernel,
        in_specs=[in_smem, in_vmem, in_vmem],
        out_specs=in_vmem,
        out_shape=shape_of((rows + side_rows, tokens), bf16),
        compiler_params=params,
        cost_estimate=estimate(3e9, 0),
        name="prepare",
    )(ids, x, gain.reshape(1, rows))


def chip_count():
    return lax.axis_size("fsdp") // 2


def ring_order(count):
    return list(range(0, count, 2)) + list(range(1, count, 2))[::-1]


def along_ring(block):
    chips = chip_count()
    order = ring_order(chips)
    pairs = []
    for i in range(chips):
        here, after = order[i], order[(i + 1) % chips]
        pairs += [(2 * here, 2 * after), (2 * after + 1, 2 * here + 1)]
    return lax.ppermute(block, "fsdp", pairs)


def other_core(block):
    return lax.ppermute(block, "fsdp", [(i, i ^ 1) for i in range(2 * chip_count())])


def ring_ids():
    chips = chip_count()
    me = lax.axis_index("fsdp")
    chip, core = me // 2, me % 2
    place = jnp.where(chip % 2 == 0, chip // 2, chips - 1 - chip // 2)
    steps = jnp.arange(chips, dtype=jnp.int32)
    places = (place + jnp.where(core == 0, chips - steps, steps)) % chips
    ids = jnp.where(places < (chips + 1) // 2, 2 * places, 2 * (chips - 1 - places) + 1)
    mine = jnp.stack([core, lax.axis_index("ctx")])
    return jnp.concatenate([ids, mine]).astype(jnp.int32)


def core_of(ids_ref):
    return ids_ref[ids_ref.shape[0] - 2]


def turn_of(ids_ref):
    return ids_ref[ids_ref.shape[0] - 1]


def take_from(refs, number):
    return [refs.pop(0) for _ in range(number)]


def products(ids, items, weight, running, side, finish, cost, name, cut=(0, 1)):
    streams, out_rows, features = weight.shape
    out_rows //= cut[1]
    out_here = slice(cut[0] * out_rows, (cut[0] + 1) * out_rows)
    rows = features // lax.axis_size("fsdp")
    shards = [piece for _, _, pieces in items for piece in pieces]
    tokens = shards[0].shape[1]
    count = len(shards)
    first_group = running is None
    state = [] if first_group else list(running)
    body, extras, out_shape = finish if finish else (None, [], None)
    padded = rows % 128 != 0
    width = 2 * rows if padded else rows
    scratch_shapes = [pltpu.VMEM((len(items) * width, tokens), bf16)] if padded else []

    def kernel(ids_ref, *refs):
        refs = list(refs)
        take = lambda n: [refs.pop(0) for _ in range(n)]
        shard_refs = take(count)
        (weight_ref,) = take(1)
        state_refs = take(len(state))
        extra_refs = take(len(extras))
        outs = take(len(out_shape))
        core = core_of(ids_ref)
        if padded:
            (beside_ref,) = refs
            beside_ref[...] = jnp.zeros(beside_ref.shape, bf16)
        sides, right = [], []
        for k, (_, other, pieces) in enumerate(items):
            done = 0
            for piece_ref in take_from(shard_refs, len(pieces)):
                more = min(piece_ref.shape[0], rows - done)
                if padded:
                    at = k * width + jnp.where(core == other, 0, rows) + done
                    at = pl.multiple_of(at, math.gcd(rows, done or rows))
                    beside_ref[pl.ds(at, more)] = piece_ref[:more]
                else:
                    right.append(piece_ref[:more])
                if more < piece_ref.shape[0]:
                    sides.append(piece_ref[more:].astype(f32))
                done += more
        right = beside_ref[...] if padded else jnp.concatenate(right, axis=0)
        side_sum = None
        if side:
            parts = sides + ([] if first_group else [state_refs[1][...]])
            side_sum = sum(parts[1:], parts[0])

        def total(stream):
            left = []
            for slot, other, _ in items:
                block = ids_ref[slot]
                if not padded:
                    block = 2 * block + (1 - core if other else core)
                at = pl.ds(pl.multiple_of(block * width, width), width)
                left.append(weight_ref[stream, out_here, at])
            product = dot(jnp.concatenate(left, axis=1), right)
            return product if first_group else state_refs[0][stream, out_here] + product

        if body is not None:
            body(total, side_sum, extra_refs, outs)
            return
        for stream in range(streams):
            outs[0][stream] = total(stream)
        if side:
            outs[1][...] = side_sum

    aliases = {}
    if body is None:
        out_shape = [shape_of((streams, out_rows, tokens), f32)]
        if side:
            out_shape.append(shape_of((side_rows, tokens), f32))
        if not first_group:
            aliases = {1 + count + 1 + i: i for i in range(len(state))}
    return pl.pallas_call(
        kernel,
        in_specs=[in_smem] + [in_vmem] * (count + 1 + len(state) + len(extras)),
        out_specs=[in_vmem] * len(out_shape),
        out_shape=out_shape,
        scratch_shapes=scratch_shapes,
        input_output_aliases=aliases,
        compiler_params=params,
        cost_estimate=estimate(cost, 0),
        name=name,
    )(ids, *shards, weight, *state, *extras)


def gather_products(ids, own, weight, beside, side, finish, name):
    chips = chip_count()
    last_step = chips // 2

    def send(way, pieces, scope):
        sent = []
        for k, piece in enumerate(pieces):
            with jax.named_scope(f"{name}_{scope}_{k}"):
                sent.append(way(piece))
        return sent

    def joined(pieces):
        return [jnp.concatenate(pieces, axis=0)] if len(pieces) > 1 else pieces

    near, far = own, send(other_core, own, "core_own")
    items = [(0, 0, near), (0, 1, far)]
    running = None
    for step in range(1, last_step + 1):
        near = joined(send(along_ring, near, f"near_{step}"))
        arrived = near
        if running is not None:
            arrived, running = lax.optimization_barrier((near, running))
        elif beside:
            arrived, beside = lax.optimization_barrier((near, beside))
        theirs = send(other_core, arrived, f"core_near_{step}")
        pair = [(step, 0, arrived), (chips - step, 1, theirs)]
        if step < last_step:
            running = products(ids, items + pair, weight, running, side, None, 0, f"{name}_{step}")
            far = joined(send(along_ring, far, f"far_{step}"))
            theirs = send(other_core, far, f"core_far_{step}")
            items = [(step, 1, far), (chips - step, 0, theirs)]
        else:
            running = products(ids, items, weight, running, side, None, STAGGER, f"{name}_{step}")
            items = pair
    results = [
        products(ids, items, weight, running, side, end, 0, f"{name}_last_{k}", (k, len(finish)))
        for k, end in enumerate(finish)
    ]
    return results, beside


def smooth(projected, taps, count, halo):
    lane = lax.broadcasted_iota(jnp.int32, projected.shape, 1)
    out = taps[:, :1] * projected
    for tap in range(1, count):
        moved = pltpu.roll(projected, tap, 1)
        for place in range(tap):
            edge = 0.0
            if halo is not None:
                at = halo.shape[1] - tap + place
                edge = halo[:, at : at + 1]
            moved = jnp.where(lane == place, edge, moved)
        out = out + taps[:, tap : tap + 1] * moved
    return out


def channel_parts(channels):
    return [(0, channels // 2), (channels // 2, channels // 2)]


def projection_finish(features, w_short, tokens, half_index):
    streams, count, channels = w_short.shape
    half = channels // 2
    begin = half_index * half
    parts = [part for part in channel_parts(channels) if begin <= part[0] < begin + half]

    def body(total, side_sum, extra_refs, outs):
        (taps_ref,) = extra_refs
        projected_ref, first_ref, *message_refs = outs
        mean = jnp.sum(side_sum, axis=0, keepdims=True) * (1.0 / features)
        factor = lax.rsqrt(mean + epsilon)
        tails = []
        for stream in range(streams):
            projected = (total(stream) * factor).astype(bf16)
            projected_ref[stream] = projected
            tail = projected[:, tokens - block_len :].astype(f32).T
            tails.append(tail[block_len - count + 1 :])
        tails.append(jnp.zeros((side_rows - streams * (count - 1), half), f32))
        side = jnp.concatenate(tails, axis=0)
        taps = [tap_columns(taps_ref[stream]) for stream in (1, 2)]
        for (first, rows), message_ref in zip(parts, message_refs):
            tile = min(rows, 64)
            for start in range(first, first + rows, tile):
                here = slice(start - begin, start - begin + tile)
                key, value = (
                    smooth(
                        projected_ref[s, here].astype(f32),
                        taps[s - 1][start : start + tile],
                        count,
                        None,
                    )
                    for s in (1, 2)
                )
                first_ref[0, here] = key[:, :block_len]
                first_ref[1, here] = value[:, :block_len]
                message_ref[start - first : start - first + tile] = (key * value).astype(bf16)
            message_ref[rows:] = jnp.zeros((side_rows, tokens), bf16)
            here = side[:, first - begin : first - begin + rows]
            message_ref[rows:, :rows] = here.astype(bf16)

    out_shape = [shape_of((streams, half, tokens), bf16), shape_of((2, half, block_len), f32)]
    out_shape += [shape_of((rows + side_rows, tokens), bf16) for _, rows in parts]
    return body, [w_short], out_shape


def halo_columns(message_ref, streams, count, inside):
    rows = message_ref.shape[0] - side_rows
    side = jnp.where(inside, message_ref[rows:, :rows].astype(f32), 0.0).T
    return [side[:, s * (count - 1) : (s + 1) * (count - 1)] for s in range(streams)]


def halo_edges(message_ref, taps, inside):
    streams, count, rows = taps.shape
    side = jnp.where(inside, message_ref[rows:, :rows].astype(f32), 0.0)
    lines = []
    for s in range(streams):
        for token in range(count - 1):
            line = jnp.zeros((1, rows), f32)
            for tap in range(token + 1, count):
                at = s * (count - 1) + count - 1 + token - tap
                line = line + taps[s, tap : tap + 1] * side[at : at + 1]
            lines.append(line)
    lines.append(jnp.zeros((-len(lines) % 8, rows), f32))
    columns = jnp.concatenate(lines, axis=0).T
    lane = lax.broadcasted_iota(jnp.int32, (rows, block_len), 1)
    edges = []
    for s in range(streams):
        edge = jnp.zeros((rows, block_len), f32)
        for token in range(count - 1):
            at = s * (count - 1) + token
            edge = jnp.where(lane == token, columns[:, at : at + 1], edge)
        edges.append(edge)
    return edges


def split_table(table):
    high = table.astype(bf16)
    return high, (table - high.astype(np.float64)).astype(bf16)


def dft_tables():
    size = 2 * block_len
    freq = np.arange(block_len) + 0.5
    angle = 2.0 * math.pi / size * np.arange(size)[:, None] * freq[None, :]
    high, low = split_table(np.concatenate([np.cos(angle), -np.sin(angle)], axis=1))
    block = np.concatenate([high[:block_len], low[:block_len]])
    segment = np.concatenate([high, low])
    back = angle[block_len:].T
    inverse = np.concatenate([np.cos(back), -np.sin(back)], axis=0) * (2.0 / size)
    high, low = split_table(inverse)
    return block, segment, np.concatenate([high, low], axis=1)


def spectrum_lanes(k):
    return slice(2 * k * block_len, 2 * (k + 1) * block_len)


def block_lanes(k):
    return slice(k * block_len, (k + 1) * block_len)


def filter_spectra(long_filter, table):
    channels, lags = long_filter.shape

    def kernel(filter_ref, table_ref, spectra_ref):
        before = jnp.zeros((channels, block_len), bf16)
        for k in range(lags // block_len):
            now = filter_ref[:, block_lanes(k)]
            segment = jnp.concatenate([before, now, before, now], axis=1)
            spectra_ref[:, spectrum_lanes(k)] = dot(segment, table_ref[...])
            before = now

    return pl.pallas_call(
        kernel,
        in_specs=[in_vmem, in_vmem],
        out_specs=in_vmem,
        out_shape=shape_of((channels, 2 * lags), f32),
        compiler_params=params,
        cost_estimate=estimate(6e9, 0),
        name="filter_spectra",
    )(long_filter, table)


def block_spectra(pieces, table_ref, spec_ref, first):
    rows = pieces[0].shape[0]
    stacked = jnp.concatenate(pieces, axis=0)
    spectra = dot(jnp.concatenate([stacked, stacked], axis=1), table_ref[...])
    for k in range(len(pieces)):
        spec_ref[:rows, spectrum_lanes(first + k)] = spectra[k * rows : (k + 1) * rows]


def multiply_spectra(source_ref, filters_ref, filter_start, pairs, before_ref, total_ref):
    used = [term for terms in pairs for term in terms]
    for start in range(0, total_ref.shape[0], 8):
        here = slice(start, start + 8)
        there = slice(filter_start + start, filter_start + start + 8)

        def parts(ref, rows, k):
            return ref[rows, block_lanes(2 * k)], ref[rows, block_lanes(2 * k + 1)]

        sources = {b: parts(source_ref, here, b) for b in sorted({b for b, _ in used})}
        filters = {d: parts(filters_ref, there, d) for d in sorted({d for _, d in used})}
        for a, terms in enumerate(pairs):
            real = imag = None
            if before_ref is not None:
                real, imag = parts(before_ref, here, a)
            for b, d in terms:
                gr, gi = sources[b]
                hr, hi = filters[d]
                more_real, more_imag = gr * hr - gi * hi, gr * hi + gi * hr
                real = more_real if real is None else real + more_real
                imag = more_imag if imag is None else imag + more_imag
            if real is None:
                real = imag = jnp.zeros((8, block_len), f32)
            total_ref[here, block_lanes(2 * a)] = real
            total_ref[here, block_lanes(2 * a + 1)] = imag


def own_part(ids, projected, messages, moved, taps, filters, table):
    streams, half, tokens = projected[0].shape
    parts = channel_parts(2 * half)
    number = len(parts)
    count = taps.shape[1]
    blocks = tokens // block_len
    first = 0 if moved else 1
    pairs = [[(b, a - b) for b in range(first, a + 1)] for a in range(blocks)]

    def kernel(ids_ref, *refs):
        refs = list(refs)
        take = lambda n: [refs.pop(0) for _ in range(n)]
        projected_refs, message_refs = take(2), take(number)
        taps_ref, filters_ref, table_ref = take(3)
        query_refs, total_refs = take(number), take(number)
        gated_refs = take(number) if moved else None
        (spec_ref,) = refs
        columns = [tap_columns(taps_ref[s]) for s in range(streams)]
        for part, (begin, rows) in enumerate(parts):
            if moved:
                inside = turn_of(ids_ref) > 0
                halo = halo_columns(message_refs[part], streams, count, inside)
            tile = min(rows, 64)
            for start in range(0, rows, tile):
                here = slice(start, start + tile)
                there = slice(begin + start, begin + start + tile)
                in_half = (begin + start) % half
                projected_ref = projected_refs[begin // half]

                def smoothed(s):
                    edge = halo[s][here] if moved else None
                    wide = projected_ref[s, in_half : in_half + tile].astype(f32)
                    return smooth(wide, columns[s][there], count, edge)

                query_refs[part][here] = smoothed(0)
                if moved:
                    gated_refs[part][here] = (smoothed(1) * smoothed(2)).astype(bf16)
            source_ref = gated_refs[part] if moved else message_refs[part]
            pieces = [source_ref[:rows, block_lanes(b)] for b in range(first, blocks)]
            block_spectra(pieces, table_ref, spec_ref, first)
            multiply_spectra(spec_ref, filters_ref, begin, pairs, None, total_refs[part])

    out_shape = [shape_of((rows, tokens), f32) for _, rows in parts]
    out_shape += [shape_of((rows, 2 * tokens), f32) for _, rows in parts]
    if moved:
        out_shape += [shape_of((rows, tokens), bf16) for _, rows in parts]
    inputs = [*projected, *(moved or messages), taps, filters, table]
    outs = pl.pallas_call(
        kernel,
        in_specs=[in_smem] + [in_vmem] * len(inputs),
        out_specs=[in_vmem] * len(out_shape),
        out_shape=out_shape,
        scratch_shapes=[pltpu.VMEM((half, 2 * tokens), f32)],
        compiler_params=params,
        cost_estimate=estimate(0, 0),
        name="own_part",
    )(ids, *inputs)
    gated = list(outs[2 * number :]) if moved else messages
    return list(outs[:number]), list(outs[number : 2 * number]), gated


def far_part(ids, turn, begin, moved, total, filters, table, last, own):
    rows, tokens = total.shape[0], moved.shape[1]
    blocks = tokens // block_len
    pairs = [[(b, turn * blocks + a - b) for b in range(blocks)] for a in range(blocks)]
    if own:
        pairs = [terms + [(blocks, a)] for a, terms in enumerate(pairs)]
    channels_here = slice(begin, begin + rows)

    def kernel(ids_ref, *refs):
        refs = list(refs)
        take = lambda n: [refs.pop(0) for _ in range(n)]
        moved_ref, total_ref, filters_ref, table_ref = take(4)
        own_refs = take(2) if own else None
        spec_ref = refs.pop()
        inside = turn_of(ids_ref) >= turn
        pieces = [
            jnp.where(inside, moved_ref[:rows, block_lanes(b)], jnp.zeros((), bf16))
            for b in range(blocks)
        ]
        if last is None:
            block_spectra(pieces, table_ref, spec_ref, 0)
            multiply_spectra(spec_ref, filters_ref, begin, pairs, total_ref, refs[0])
            return
        sum_ref = refs.pop()
        back_ref, query_ref, gated_ref, skip_ref = take(4)
        out_ref = refs[-1]
        query, gated = (
            [ref[:rows, block_lanes(a)] for a in range(blocks)] for ref in (query_ref, gated_ref)
        )
        if own:
            first_ref, taps_ref = own_refs
            in_half = slice(begin % first_ref.shape[1], begin % first_ref.shape[1] + rows)
            edges = halo_edges(moved_ref, taps_ref[:, :, channels_here], inside)
            query[0] = query[0] + edges[0]
            key, value = first_ref[0, in_half] + edges[1], first_ref[1, in_half] + edges[2]
            gated[0] = (key * value).astype(bf16)
            pieces.append(gated[0])
        block_spectra(pieces, table_ref, spec_ref, 0)
        multiply_spectra(spec_ref, filters_ref, begin, pairs, total_ref, sum_ref)
        skip = column(skip_ref[...])[channels_here]
        spectra = [sum_ref[:, spectrum_lanes(a)] for a in range(blocks)]
        highs = [spectrum.astype(bf16) for spectrum in spectra]
        lows = [(s - high.astype(f32)).astype(bf16) for s, high in zip(spectra, highs)]
        both = dot(jnp.concatenate(highs, axis=0), back_ref[...])
        small = dot(jnp.concatenate(lows, axis=0), back_ref[:, :block_len])
        filtered = both[:, :block_len] + (both[:, block_len:] + small)
        for a in range(blocks):
            here = filtered[a * rows : (a + 1) * rows]
            mixed = (query[a] * (here + skip * gated[a].astype(f32))).astype(bf16)
            out_ref[:, block_lanes(a)] = mixed

    args = [moved, total, filters, table]
    if own:
        args += list(own)
    scratch = [pltpu.VMEM((rows, 2 * (blocks + 1) * block_len), f32)]
    out_shape = shape_of((rows, 2 * tokens), f32)
    if last is not None:
        inverse, query, gated, skip = last
        args += [inverse, query, gated, skip.reshape(1, -1)]
        out_shape = shape_of((rows, tokens), bf16)
        scratch.append(pltpu.VMEM((rows, 2 * tokens), f32))
    return pl.pallas_call(
        kernel,
        in_specs=[in_smem] + [in_vmem] * len(args),
        out_specs=in_vmem,
        out_shape=out_shape,
        scratch_shapes=scratch[::-1],
        compiler_params=params,
        cost_estimate=estimate(0, 0),
        name=f"far_part_{turn}_{begin}",
    )(ids, *args)


def from_before(block):
    count = lax.axis_size("ctx")
    return lax.ppermute(block, "ctx", [(i, (i + 1) % count) for i in range(count)])


def output_finish(channels, tokens):
    def body(total, side_sum, extra_refs, outs):
        outs[0][...] = total(0).astype(bf16)

    return body, [], [shape_of((channels, tokens), bf16)]


def shards(activations, norm_gain, w_in, w_short, long_filter, skip_gain, w_out):
    channels, tokens = activations.shape
    features = w_in.shape[2]
    w_short = w_short.transpose(0, 2, 1)
    turns = lax.axis_size("ctx")
    parts = channel_parts(channels)
    forward, segments, inverse = (jnp.asarray(t) for t in dft_tables())
    ids = ring_ids()
    own = prepare(ids, activations, norm_gain)

    filters = filter_spectra(long_filter, segments)
    finish = [projection_finish(features, w_short, tokens, k) for k in range(2)]
    results, (filters,) = gather_products(
        ids, [own], w_in, [filters], True, finish, "projection"
    )
    projected = [result[0] for result in results]
    first_blocks = [result[1] for result in results]
    messages = [message for result in results for message in result[2:]]
    moving = [from_before(message) for message in messages]
    exact = turns > 2
    query, totals, gated = own_part(
        ids, projected, messages, moving if exact else None, w_short, filters, forward
    )
    if exact:
        moving = [from_before(part) for part in gated]
    mixed = []
    for turn in range(1, turns):
        for k, (begin, _) in enumerate(parts):
            last = own_block = None
            if turn == turns - 1:
                last = (inverse, query[k], gated[k], skip_gain)
                if not exact:
                    own_block = (first_blocks[2 * begin // channels], w_short)
            done = far_part(
                ids, turn, begin, moving[k], totals[k], filters, forward, last, own_block
            )
            if last is None:
                totals[k] = done
                moving[k] = from_before(moving[k])
            else:
                mixed.append(done)

    finish = [output_finish(channels, tokens)]
    ((result,),), _ = gather_products(
        ids, mixed, w_out[None], [], False, finish, "output"
    )
    return result


def solution(mesh):
    placed = (
        P("fsdp", "ctx"),
        P("fsdp"),
        P(None, "fsdp", None),
        P(None, "fsdp", None),
        P("fsdp", None),
        P("fsdp"),
        P("fsdp", None),
    )
    return jax.shard_map(
        shards, mesh=mesh, in_specs=placed, out_specs=P("fsdp", "ctx"), check_vma=False
    )
```

```python
import math

import jax
import jax.numpy as jnp
import numpy as np
from jax import lax
from jax.experimental import pallas as pl
from jax.experimental.pallas import tpu as pltpu
from jax.sharding import PartitionSpec as P

epsilon = 1e-05
block_len = 128
STAGGER = 2e9
side_rows = 8
bf16 = jnp.bfloat16
f32 = jnp.float32
in_vmem = pl.BlockSpec(memory_space=pltpu.VMEM)
params = pltpu.CompilerParams(vmem_limit_bytes=12 * 2**20)


def shape_of(shape, dtype):
    return jax.ShapeDtypeStruct(tuple(shape), dtype)


def dot(left, right):
    return jnp.dot(left, right, preferred_element_type=f32)


def column(row):
    return jnp.broadcast_to(row, (8, row.shape[1])).T[:, :1]


def tap_columns(taps):
    return jnp.concatenate([taps, jnp.zeros((8 - taps.shape[0], taps.shape[1]), f32)], axis=0).T


def estimate(flops, size):
    return pl.CostEstimate(flops=int(flops), bytes_accessed=int(size), transcendentals=0)


def prepare_kernel(x_ref, gain_ref, out_ref):
    rows = x_ref.shape[0]
    wide = x_ref[...].astype(f32)
    out_ref[:rows] = (wide * column(gain_ref[...])).astype(bf16)
    squares = jnp.sum(wide * wide, axis=0, keepdims=True)
    high = squares.astype(bf16).astype(f32)
    row = lax.broadcasted_iota(jnp.int32, (side_rows, wide.shape[1]), 0)
    side = jnp.where(row == 0, high, jnp.where(row == 1, squares - high, 0.0))
    out_ref[rows:] = side.astype(bf16)


def prepare(x, gain):
    rows, tokens = x.shape
    return pl.pallas_call(
        prepare_kernel,
        in_specs=[in_vmem, in_vmem],
        out_specs=in_vmem,
        out_shape=shape_of((rows + side_rows, tokens), bf16),
        compiler_params=params,
        cost_estimate=estimate(3e9, 0),
        name="prepare",
    )(x, gain.reshape(1, rows))


def chip_count():
    return lax.axis_size("fsdp") // 2


def ring_order(count):
    return list(range(0, count, 2)) + list(range(1, count, 2))[::-1]


def along_ring(block):
    chips = chip_count()
    order = ring_order(chips)
    pairs = []
    for i in range(chips):
        here, after = order[i], order[(i + 1) % chips]
        pairs += [(2 * here, 2 * after), (2 * after + 1, 2 * here + 1)]
    return lax.ppermute(block, "fsdp", pairs)


def other_core(block):
    return lax.ppermute(block, "fsdp", [(i, i ^ 1) for i in range(2 * chip_count())])


def my_core():
    return lax.axis_index("fsdp") & 1


def source_chip(steps):
    chips = chip_count()
    chip = lax.shift_right_logical(lax.axis_index("fsdp"), 1)
    half = lax.shift_right_logical(chip, 1)
    place = jnp.where(chip & 1 == 0, half, chips - 1 - half)
    place = place + jnp.where(my_core() == 0, chips - steps, steps)
    place = jnp.where(place >= chips, place - chips, place)
    return jnp.where(place < (chips + 1) // 2, 2 * place, 2 * (chips - 1 - place) + 1)


def take_from(refs, number):
    return [refs.pop(0) for _ in range(number)]


def products(items, weight, running, side, finish, cost, name, cut=(0, 1)):
    streams, out_rows, features = weight.shape
    out_rows //= cut[1]
    out_here = slice(cut[0] * out_rows, (cut[0] + 1) * out_rows)
    rows = features // lax.axis_size("fsdp")
    shards = [piece for _, _, pieces in items for piece in pieces]
    tokens = shards[0].shape[1]
    count = len(shards)
    first_group = running is None
    state = [] if first_group else list(running)
    body, extras, out_shape = finish if finish else (None, [], None)
    padded = rows % 128 != 0
    width = 2 * rows if padded else rows
    scratch_shapes = [pltpu.VMEM((len(items) * width, tokens), bf16)] if padded else []

    def kernel(*refs):
        refs = list(refs)
        take = lambda n: take_from(refs, n)
        shard_refs = take(count)
        (weight_ref,) = take(1)
        state_refs = take(len(state))
        extra_refs = take(len(extras))
        outs = take(len(out_shape))
        core = my_core()
        chip_of = {steps: source_chip(steps) for steps in sorted({item[0] for item in items})}
        if padded:
            (beside_ref,) = refs
            beside_ref[...] = jnp.zeros(beside_ref.shape, bf16)
        sides, right = [], []
        for k, (_, other, pieces) in enumerate(items):
            done = 0
            for piece_ref in take_from(shard_refs, len(pieces)):
                more = min(piece_ref.shape[0], rows - done)
                if padded:
                    at = k * width + jnp.where(core == other, 0, rows) + done
                    at = pl.multiple_of(at, math.gcd(rows, done or rows))
                    beside_ref[pl.ds(at, more)] = piece_ref[:more]
                else:
                    right.append(piece_ref[:more])
                if more < piece_ref.shape[0]:
                    sides.append(piece_ref[more:].astype(f32))
                done += more
        right = beside_ref[...] if padded else jnp.concatenate(right, axis=0)
        side_sum = None
        if side:
            parts = sides + ([] if first_group else [state_refs[1][...]])
            side_sum = sum(parts[1:], parts[0])

        def total(stream):
            left = []
            for steps, other, _ in items:
                block = chip_of[steps]
                if not padded:
                    block = 2 * block + (1 - core if other else core)
                at = pl.ds(pl.multiple_of(block * width, width), width)
                left.append(weight_ref[stream, out_here, at])
            product = dot(jnp.concatenate(left, axis=1), right)
            return product if first_group else state_refs[0][stream, out_here] + product

        if body is not None:
            body(total, side_sum, extra_refs, outs)
            return
        for stream in range(streams):
            outs[0][stream] = total(stream)
        if side:
            outs[1][...] = side_sum

    aliases = {}
    if body is None:
        out_shape = [shape_of((streams, out_rows, tokens), f32)]
        if side:
            out_shape.append(shape_of((side_rows, tokens), f32))
        if not first_group:
            aliases = {count + 1 + i: i for i in range(len(state))}
    return pl.pallas_call(
        kernel,
        in_specs=[in_vmem] * (count + 1 + len(state) + len(extras)),
        out_specs=[in_vmem] * len(out_shape),
        out_shape=out_shape,
        scratch_shapes=scratch_shapes,
        input_output_aliases=aliases,
        compiler_params=params,
        cost_estimate=estimate(cost, 0),
        name=name,
    )(*shards, weight, *state, *extras)


def gather_products(own, weight, beside, side, finish, name):
    chips = chip_count()
    last_step = chips // 2

    def send(way, pieces, scope):
        sent = []
        for k, piece in enumerate(pieces):
            with jax.named_scope(f"{name}_{scope}_{k}"):
                sent.append(way(piece))
        return sent

    def joined(pieces):
        return [jnp.concatenate(pieces, axis=0)] if len(pieces) > 1 else pieces

    near, far = own, send(other_core, own, "core_own")
    items = [(0, 0, near), (0, 1, far)]
    running = None
    for step in range(1, last_step + 1):
        near = joined(send(along_ring, near, f"near_{step}"))
        arrived = near
        if running is not None:
            arrived, running = lax.optimization_barrier((near, running))
        elif beside:
            arrived, beside = lax.optimization_barrier((near, beside))
        theirs = send(other_core, arrived, f"core_near_{step}")
        pair = [(step, 0, arrived), (chips - step, 1, theirs)]
        if step < last_step:
            running = products(items + pair, weight, running, side, None, 0, f"{name}_{step}")
            far = joined(send(along_ring, far, f"far_{step}"))
            theirs = send(other_core, far, f"core_far_{step}")
            items = [(step, 1, far), (chips - step, 0, theirs)]
        else:
            running = products(items, weight, running, side, None, STAGGER, f"{name}_{step}")
            items = pair
    results = [
        products(items, weight, running, side, end, 0, f"{name}_last_{k}", (k, len(finish)))
        for k, end in enumerate(finish)
    ]
    return results, beside


def smooth(projected, taps, count, halo):
    lane = lax.broadcasted_iota(jnp.int32, projected.shape, 1)
    out = taps[:, :1] * projected
    for tap in range(1, count):
        moved = pltpu.roll(projected, tap, 1)
        for place in range(tap):
            edge = 0.0
            if halo is not None:
                at = halo.shape[1] - tap + place
                edge = halo[:, at : at + 1]
            moved = jnp.where(lane == place, edge, moved)
        out = out + taps[:, tap : tap + 1] * moved
    return out


def channel_parts(channels):
    return [(0, channels // 2), (channels // 2, channels // 2)]


def projection_finish(features, w_short, tokens, half_index):
    streams, count, channels = w_short.shape
    half = channels // 2
    begin = half_index * half
    parts = [part for part in channel_parts(channels) if begin <= part[0] < begin + half]

    def body(total, side_sum, extra_refs, outs):
        (taps_ref,) = extra_refs
        projected_ref, first_ref, *message_refs = outs
        mean = jnp.sum(side_sum, axis=0, keepdims=True) * (1.0 / features)
        factor = lax.rsqrt(mean + epsilon)
        tails = []
        for stream in range(streams):
            projected = (total(stream) * factor).astype(bf16)
            projected_ref[stream] = projected
            tail = projected[:, tokens - block_len :].astype(f32).T
            tails.append(tail[block_len - count + 1 :])
        tails.append(jnp.zeros((side_rows - streams * (count - 1), half), f32))
        side = jnp.concatenate(tails, axis=0)
        taps = [tap_columns(taps_ref[stream]) for stream in (1, 2)]
        for (first, rows), message_ref in zip(parts, message_refs):
            tile = min(rows, 64)
            for start in range(first, first + rows, tile):
                here = slice(start - begin, start - begin + tile)
                key, value = (
                    smooth(
                        projected_ref[s, here].astype(f32),
                        taps[s - 1][start : start + tile],
                        count,
                        None,
                    )
                    for s in (1, 2)
                )
                first_ref[0, here] = key[:, :block_len]
                first_ref[1, here] = value[:, :block_len]
                message_ref[start - first : start - first + tile] = (key * value).astype(bf16)
            message_ref[rows:] = jnp.zeros((side_rows, tokens), bf16)
            here = side[:, first - begin : first - begin + rows]
            message_ref[rows:, :rows] = here.astype(bf16)

    out_shape = [shape_of((streams, half, tokens), bf16), shape_of((2, half, block_len), f32)]
    out_shape += [shape_of((rows + side_rows, tokens), bf16) for _, rows in parts]
    return body, [w_short], out_shape


def halo_columns(message_ref, streams, count, inside):
    rows = message_ref.shape[0] - side_rows
    side = jnp.where(inside, message_ref[rows:, :rows].astype(f32), 0.0).T
    return [side[:, s * (count - 1) : (s + 1) * (count - 1)] for s in range(streams)]


def halo_edges(message_ref, taps, inside):
    streams, count, rows = taps.shape
    side = jnp.where(inside, message_ref[rows:, :rows].astype(f32), 0.0)
    lines = []
    for s in range(streams):
        for token in range(count - 1):
            line = jnp.zeros((1, rows), f32)
            for tap in range(token + 1, count):
                at = s * (count - 1) + count - 1 + token - tap
                line = line + taps[s, tap : tap + 1] * side[at : at + 1]
            lines.append(line)
    lines.append(jnp.zeros((-len(lines) % 8, rows), f32))
    columns = jnp.concatenate(lines, axis=0).T
    lane = lax.broadcasted_iota(jnp.int32, (rows, block_len), 1)
    edges = []
    for s in range(streams):
        edge = jnp.zeros((rows, block_len), f32)
        for token in range(count - 1):
            at = s * (count - 1) + token
            edge = jnp.where(lane == token, columns[:, at : at + 1], edge)
        edges.append(edge)
    return edges


def split_table(table):
    high = table.astype(bf16)
    return high, (table - high.astype(np.float64)).astype(bf16)


def dft_tables():
    size = 2 * block_len
    freq = np.arange(block_len) + 0.5
    angle = 2.0 * math.pi / size * np.arange(size)[:, None] * freq[None, :]
    high, low = split_table(np.concatenate([np.cos(angle), -np.sin(angle)], axis=1))
    block = np.concatenate([high[:block_len], low[:block_len]])
    segment = np.concatenate([high, low])
    back = angle[block_len:].T
    inverse = np.concatenate([np.cos(back), -np.sin(back)], axis=0) * (2.0 / size)
    high, low = split_table(inverse)
    return block, segment, np.concatenate([high, low], axis=1)


def spectrum_lanes(k):
    return slice(2 * k * block_len, 2 * (k + 1) * block_len)


def block_lanes(k):
    return slice(k * block_len, (k + 1) * block_len)


def filter_spectra(long_filter, table):
    channels, lags = long_filter.shape

    def kernel(filter_ref, table_ref, spectra_ref):
        before = jnp.zeros((channels, block_len), bf16)
        for k in range(lags // block_len):
            now = filter_ref[:, block_lanes(k)]
            segment = jnp.concatenate([before, now, before, now], axis=1)
            spectra_ref[:, spectrum_lanes(k)] = dot(segment, table_ref[...])
            before = now

    return pl.pallas_call(
        kernel,
        in_specs=[in_vmem, in_vmem],
        out_specs=in_vmem,
        out_shape=shape_of((channels, 2 * lags), f32),
        compiler_params=params,
        cost_estimate=estimate(6e9, 0),
        name="filter_spectra",
    )(long_filter, table)


def block_spectra(pieces, table_ref, spec_ref, first):
    rows = pieces[0].shape[0]
    stacked = jnp.concatenate(pieces, axis=0)
    spectra = dot(jnp.concatenate([stacked, stacked], axis=1), table_ref[...])
    for k in range(len(pieces)):
        spec_ref[:rows, spectrum_lanes(first + k)] = spectra[k * rows : (k + 1) * rows]


def multiply_spectra(source_ref, filters_ref, filter_start, pairs, before_ref, total_ref):
    used = [term for terms in pairs for term in terms]
    for start in range(0, total_ref.shape[0], 8):
        here = slice(start, start + 8)
        there = slice(filter_start + start, filter_start + start + 8)

        def parts(ref, rows, k):
            return ref[rows, block_lanes(2 * k)], ref[rows, block_lanes(2 * k + 1)]

        sources = {b: parts(source_ref, here, b) for b in sorted({b for b, _ in used})}
        filters = {d: parts(filters_ref, there, d) for d in sorted({d for _, d in used})}
        for a, terms in enumerate(pairs):
            real = imag = None
            if before_ref is not None:
                real, imag = parts(before_ref, here, a)
            for b, d in terms:
                gr, gi = sources[b]
                hr, hi = filters[d]
                more_real, more_imag = gr * hr - gi * hi, gr * hi + gi * hr
                real = more_real if real is None else real + more_real
                imag = more_imag if imag is None else imag + more_imag
            if real is None:
                real = imag = jnp.zeros((8, block_len), f32)
            total_ref[here, block_lanes(2 * a)] = real
            total_ref[here, block_lanes(2 * a + 1)] = imag


def own_part(projected, messages, moved, taps, filters, table):
    streams, half, tokens = projected[0].shape
    parts = channel_parts(2 * half)
    number = len(parts)
    count = taps.shape[1]
    blocks = tokens // block_len
    first = 0 if moved else 1
    pairs = [[(b, a - b) for b in range(first, a + 1)] for a in range(blocks)]

    def kernel(*refs):
        refs = list(refs)
        take = lambda n: take_from(refs, n)
        projected_refs, message_refs = take(2), take(number)
        taps_ref, filters_ref, table_ref = take(3)
        query_refs, total_refs = take(number), take(number)
        gated_refs = take(number) if moved else None
        (spec_ref,) = refs
        columns = [tap_columns(taps_ref[s]) for s in range(streams)]
        for part, (begin, rows) in enumerate(parts):
            if moved:
                inside = lax.axis_index("ctx") > 0
                halo = halo_columns(message_refs[part], streams, count, inside)
            tile = min(rows, 64)
            for start in range(0, rows, tile):
                here = slice(start, start + tile)
                there = slice(begin + start, begin + start + tile)
                in_half = (begin + start) % half
                projected_ref = projected_refs[begin // half]

                def smoothed(s):
                    edge = halo[s][here] if moved else None
                    wide = projected_ref[s, in_half : in_half + tile].astype(f32)
                    return smooth(wide, columns[s][there], count, edge)

                query_refs[part][here] = smoothed(0)
                if moved:
                    gated_refs[part][here] = (smoothed(1) * smoothed(2)).astype(bf16)
            source_ref = gated_refs[part] if moved else message_refs[part]
            pieces = [source_ref[:rows, block_lanes(b)] for b in range(first, blocks)]
            block_spectra(pieces, table_ref, spec_ref, first)
            multiply_spectra(spec_ref, filters_ref, begin, pairs, None, total_refs[part])

    out_shape = [shape_of((rows, tokens), f32) for _, rows in parts]
    out_shape += [shape_of((rows, 2 * tokens), f32) for _, rows in parts]
    if moved:
        out_shape += [shape_of((rows, tokens), bf16) for _, rows in parts]
    inputs = [*projected, *(moved or messages), taps, filters, table]
    outs = pl.pallas_call(
        kernel,
        in_specs=[in_vmem] * len(inputs),
        out_specs=[in_vmem] * len(out_shape),
        out_shape=out_shape,
        scratch_shapes=[pltpu.VMEM((half, 2 * tokens), f32)],
        compiler_params=params,
        cost_estimate=estimate(0, 0),
        name="own_part",
    )(*inputs)
    gated = list(outs[2 * number :]) if moved else messages
    return list(outs[:number]), list(outs[number : 2 * number]), gated


def far_part(turn, begin, moved, total, filters, table, last, own):
    rows, tokens = total.shape[0], moved.shape[1]
    blocks = tokens // block_len
    pairs = [[(b, turn * blocks + a - b) for b in range(blocks)] for a in range(blocks)]
    if own:
        pairs = [terms + [(blocks, a)] for a, terms in enumerate(pairs)]
    channels_here = slice(begin, begin + rows)

    def kernel(*refs):
        refs = list(refs)
        take = lambda n: take_from(refs, n)
        moved_ref, total_ref, filters_ref, table_ref = take(4)
        own_refs = take(2) if own else None
        spec_ref = refs.pop()
        inside = lax.axis_index("ctx") >= turn
        pieces = [
            jnp.where(inside, moved_ref[:rows, block_lanes(b)], jnp.zeros((), bf16))
            for b in range(blocks)
        ]
        if last is None:
            block_spectra(pieces, table_ref, spec_ref, 0)
            multiply_spectra(spec_ref, filters_ref, begin, pairs, total_ref, refs[0])
            return
        sum_ref = refs.pop()
        back_ref, query_ref, gated_ref, skip_ref = take(4)
        out_ref = refs[-1]
        query, gated = (
            [ref[:rows, block_lanes(a)] for a in range(blocks)] for ref in (query_ref, gated_ref)
        )
        if own:
            first_ref, taps_ref = own_refs
            in_half = slice(begin % first_ref.shape[1], begin % first_ref.shape[1] + rows)
            edges = halo_edges(moved_ref, taps_ref[:, :, channels_here], inside)
            query[0] = query[0] + edges[0]
            key, value = first_ref[0, in_half] + edges[1], first_ref[1, in_half] + edges[2]
            gated[0] = (key * value).astype(bf16)
            pieces.append(gated[0])
        block_spectra(pieces, table_ref, spec_ref, 0)
        multiply_spectra(spec_ref, filters_ref, begin, pairs, total_ref, sum_ref)
        skip = column(skip_ref[...])[channels_here]
        spectra = [sum_ref[:, spectrum_lanes(a)] for a in range(blocks)]
        highs = [spectrum.astype(bf16) for spectrum in spectra]
        lows = [(s - high.astype(f32)).astype(bf16) for s, high in zip(spectra, highs)]
        both = dot(jnp.concatenate(highs, axis=0), back_ref[...])
        small = dot(jnp.concatenate(lows, axis=0), back_ref[:, :block_len])
        filtered = both[:, :block_len] + (both[:, block_len:] + small)
        for a in range(blocks):
            here = filtered[a * rows : (a + 1) * rows]
            mixed = (query[a] * (here + skip * gated[a].astype(f32))).astype(bf16)
            out_ref[:, block_lanes(a)] = mixed

    args = [moved, total, filters, table]
    if own:
        args += list(own)
    scratch = [pltpu.VMEM((rows, 2 * (blocks + 1) * block_len), f32)]
    out_shape = shape_of((rows, 2 * tokens), f32)
    if last is not None:
        inverse, query, gated, skip = last
        args += [inverse, query, gated, skip.reshape(1, -1)]
        out_shape = shape_of((rows, tokens), bf16)
        scratch.append(pltpu.VMEM((rows, 2 * tokens), f32))
    return pl.pallas_call(
        kernel,
        in_specs=[in_vmem] * len(args),
        out_specs=in_vmem,
        out_shape=out_shape,
        scratch_shapes=scratch[::-1],
        compiler_params=params,
        cost_estimate=estimate(0, 0),
        name=f"far_part_{turn}_{begin}",
    )(*args)


def from_before(block):
    count = lax.axis_size("ctx")
    return lax.ppermute(block, "ctx", [(i, (i + 1) % count) for i in range(count)])


def output_finish(channels, tokens):
    def body(total, side_sum, extra_refs, outs):
        outs[0][...] = total(0).astype(bf16)

    return body, [], [shape_of((channels, tokens), bf16)]


def shards(activations, norm_gain, w_in, w_short, long_filter, skip_gain, w_out):
    channels, tokens = activations.shape
    features = w_in.shape[2]
    w_short = w_short.transpose(0, 2, 1)
    turns = lax.axis_size("ctx")
    parts = channel_parts(channels)
    forward, segments, inverse = (jnp.asarray(t) for t in dft_tables())
    own = prepare(activations, norm_gain)

    filters = filter_spectra(long_filter, segments)
    finish = [projection_finish(features, w_short, tokens, k) for k in range(2)]
    results, (filters,) = gather_products(
        [own], w_in, [filters], True, finish, "projection"
    )
    projected = [result[0] for result in results]
    first_blocks = [result[1] for result in results]
    messages = [message for result in results for message in result[2:]]
    moving = [from_before(message) for message in messages]
    exact = turns > 2
    query, totals, gated = own_part(
        projected, messages, moving if exact else None, w_short, filters, forward
    )
    if exact:
        moving = [from_before(part) for part in gated]
    mixed = []
    for turn in range(1, turns):
        for k, (begin, _) in enumerate(parts):
            last = own_block = None
            if turn == turns - 1:
                last = (inverse, query[k], gated[k], skip_gain)
                if not exact:
                    own_block = (first_blocks[2 * begin // channels], w_short)
            done = far_part(
                turn, begin, moving[k], totals[k], filters, forward, last, own_block
            )
            if last is None:
                totals[k] = done
                moving[k] = from_before(moving[k])
            else:
                mixed.append(done)

    finish = [output_finish(channels, tokens)]
    ((result,),), _ = gather_products(
        mixed, w_out[None], [], False, finish, "output"
    )
    return result


def solution(mesh):
    placed = (
        P("fsdp", "ctx"),
        P("fsdp"),
        P(None, "fsdp", None),
        P(None, "fsdp", None),
        P("fsdp", None),
        P("fsdp"),
        P("fsdp", None),
    )
    return jax.shard_map(
        shards, mesh=mesh, in_specs=placed, out_specs=P("fsdp", "ctx"), check_vma=False
    )
```

```python
import math

import jax
import jax.numpy as jnp
import numpy as np
from jax import lax
from jax.experimental import pallas as pl
from jax.experimental.pallas import tpu as pltpu
from jax.sharding import PartitionSpec as P

epsilon = 1e-05
block_len = 128
STAGGER = 2e9
side_rows = 8
bf16 = jnp.bfloat16
f32 = jnp.float32
in_vmem = pl.BlockSpec(memory_space=pltpu.VMEM)
params = pltpu.CompilerParams(vmem_limit_bytes=12 * 2**20)


def shape_of(shape, dtype):
    return jax.ShapeDtypeStruct(tuple(shape), dtype)


def dot(left, right):
    return jnp.dot(left, right, preferred_element_type=f32)


def column(row):
    return jnp.broadcast_to(row, (8, row.shape[1])).T[:, :1]


def tap_columns(taps):
    return jnp.concatenate([taps, jnp.zeros((8 - taps.shape[0], taps.shape[1]), f32)], axis=0).T


def estimate(flops, size):
    return pl.CostEstimate(flops=int(flops), bytes_accessed=int(size), transcendentals=0)


def begin():
    def kernel(out_ref):
        out_ref[...] = jnp.zeros(out_ref.shape, f32)

    return pl.pallas_call(
        kernel,
        out_specs=in_vmem,
        out_shape=shape_of((8, 128), f32),
        compiler_params=params,
        cost_estimate=estimate(3e9, 0),
        name="begin",
    )()


def prepare_kernel(x_ref, gain_ref, begun_ref, out_ref):
    rows = x_ref.shape[0]
    wide = x_ref[...].astype(f32)
    out_ref[:rows] = (wide * column(gain_ref[...])).astype(bf16)
    squares = jnp.sum(wide * wide, axis=0, keepdims=True)
    high = squares.astype(bf16).astype(f32)
    row = lax.broadcasted_iota(jnp.int32, (side_rows, wide.shape[1]), 0)
    side = jnp.where(row == 0, high, jnp.where(row == 1, squares - high, 0.0))
    out_ref[rows:] = side.astype(bf16)


def prepare(x, gain):
    rows, tokens = x.shape
    return pl.pallas_call(
        prepare_kernel,
        in_specs=[in_vmem, in_vmem, in_vmem],
        out_specs=in_vmem,
        out_shape=shape_of((rows + side_rows, tokens), bf16),
        compiler_params=params,
        cost_estimate=estimate(3e9, 0),
        name="prepare",
    )(x, gain.reshape(1, rows), begin())


def chip_count():
    return lax.axis_size("fsdp") // 2


def ring_order(count):
    return list(range(0, count, 2)) + list(range(1, count, 2))[::-1]


def along_ring(block):
    chips = chip_count()
    order = ring_order(chips)
    pairs = []
    for i in range(chips):
        here, after = order[i], order[(i + 1) % chips]
        pairs += [(2 * here, 2 * after), (2 * after + 1, 2 * here + 1)]
    return lax.ppermute(block, "fsdp", pairs)


def other_core(block):
    return lax.ppermute(block, "fsdp", [(i, i ^ 1) for i in range(2 * chip_count())])


def my_core():
    return lax.axis_index("fsdp") & 1


def source_chip(steps):
    chips = chip_count()
    chip = lax.shift_right_logical(lax.axis_index("fsdp"), 1)
    half = lax.shift_right_logical(chip, 1)
    place = jnp.where(chip & 1 == 0, half, chips - 1 - half)
    place = place + jnp.where(my_core() == 0, chips - steps, steps)
    place = jnp.where(place >= chips, place - chips, place)
    return jnp.where(place < (chips + 1) // 2, 2 * place, 2 * (chips - 1 - place) + 1)


def take_from(refs, number):
    return [refs.pop(0) for _ in range(number)]


def products(items, weight, running, side, finish, cost, name, cut=(0, 1)):
    streams, out_rows, features = weight.shape
    out_rows //= cut[1]
    out_here = slice(cut[0] * out_rows, (cut[0] + 1) * out_rows)
    rows = features // lax.axis_size("fsdp")
    shards = [piece for _, _, pieces in items for piece in pieces]
    tokens = shards[0].shape[1]
    count = len(shards)
    first_group = running is None
    state = [] if first_group else list(running)
    body, extras, out_shape = finish if finish else (None, [], None)
    padded = rows % 128 != 0
    width = 2 * rows if padded else rows
    scratch_shapes = [pltpu.VMEM((len(items) * width, tokens), bf16)] if padded else []

    def kernel(*refs):
        refs = list(refs)
        take = lambda n: take_from(refs, n)
        shard_refs = take(count)
        (weight_ref,) = take(1)
        state_refs = take(len(state))
        extra_refs = take(len(extras))
        outs = take(len(out_shape))
        core = my_core()
        chip_of = {steps: source_chip(steps) for steps in sorted({item[0] for item in items})}
        if padded:
            (beside_ref,) = refs
            beside_ref[...] = jnp.zeros(beside_ref.shape, bf16)
        sides, right = [], []
        for k, (_, other, pieces) in enumerate(items):
            done = 0
            for piece_ref in take_from(shard_refs, len(pieces)):
                more = min(piece_ref.shape[0], rows - done)
                if padded:
                    at = k * width + jnp.where(core == other, 0, rows) + done
                    at = pl.multiple_of(at, math.gcd(rows, done or rows))
                    beside_ref[pl.ds(at, more)] = piece_ref[:more]
                else:
                    right.append(piece_ref[:more])
                if more < piece_ref.shape[0]:
                    sides.append(piece_ref[more:].astype(f32))
                done += more
        right = beside_ref[...] if padded else jnp.concatenate(right, axis=0)
        side_sum = None
        if side:
            parts = sides + ([] if first_group else [state_refs[1][...]])
            side_sum = sum(parts[1:], parts[0])

        def total(stream):
            left = []
            for steps, other, _ in items:
                block = chip_of[steps]
                if not padded:
                    block = 2 * block + (1 - core if other else core)
                at = pl.ds(pl.multiple_of(block * width, width), width)
                left.append(weight_ref[stream, out_here, at])
            product = dot(jnp.concatenate(left, axis=1), right)
            return product if first_group else state_refs[0][stream, out_here] + product

        if body is not None:
            body(total, side_sum, extra_refs, outs)
            return
        for stream in range(streams):
            outs[0][stream] = total(stream)
        if side:
            outs[1][...] = side_sum

    aliases = {}
    if body is None:
        out_shape = [shape_of((streams, out_rows, tokens), f32)]
        if side:
            out_shape.append(shape_of((side_rows, tokens), f32))
        if not first_group:
            aliases = {count + 1 + i: i for i in range(len(state))}
    return pl.pallas_call(
        kernel,
        in_specs=[in_vmem] * (count + 1 + len(state) + len(extras)),
        out_specs=[in_vmem] * len(out_shape),
        out_shape=out_shape,
        scratch_shapes=scratch_shapes,
        input_output_aliases=aliases,
        compiler_params=params,
        cost_estimate=estimate(cost, 0),
        name=name,
    )(*shards, weight, *state, *extras)


def gather_products(own, weight, beside, side, finish, name):
    chips = chip_count()
    last_step = chips // 2

    def send(way, pieces, scope):
        sent = []
        for k, piece in enumerate(pieces):
            with jax.named_scope(f"{name}_{scope}_{k}"):
                sent.append(way(piece))
        return sent

    def joined(pieces):
        return [jnp.concatenate(pieces, axis=0)] if len(pieces) > 1 else pieces

    near, far = own, send(other_core, own, "core_own")
    items = [(0, 0, near), (0, 1, far)]
    running = None
    for step in range(1, last_step + 1):
        near = joined(send(along_ring, near, f"near_{step}"))
        arrived = near
        if running is not None:
            arrived, running = lax.optimization_barrier((near, running))
        elif beside:
            arrived, beside = lax.optimization_barrier((near, beside))
        theirs = send(other_core, arrived, f"core_near_{step}")
        pair = [(step, 0, arrived), (chips - step, 1, theirs)]
        if step < last_step:
            running = products(items + pair, weight, running, side, None, 0, f"{name}_{step}")
            far = joined(send(along_ring, far, f"far_{step}"))
            theirs = send(other_core, far, f"core_far_{step}")
            items = [(step, 1, far), (chips - step, 0, theirs)]
        else:
            items.append(pair[0])
            running = products(items, weight, running, side, None, STAGGER, f"{name}_{step}")
            items = pair[1:]
    results = [
        products(items, weight, running, side, end, 0, f"{name}_last_{k}", (k, len(finish)))
        for k, end in enumerate(finish)
    ]
    return results, beside


def smooth(projected, taps, count, halo):
    lane = lax.broadcasted_iota(jnp.int32, projected.shape, 1)
    out = taps[:, :1] * projected
    for tap in range(1, count):
        moved = pltpu.roll(projected, tap, 1)
        for place in range(tap):
            edge = 0.0
            if halo is not None:
                at = halo.shape[1] - tap + place
                edge = halo[:, at : at + 1]
            moved = jnp.where(lane == place, edge, moved)
        out = out + taps[:, tap : tap + 1] * moved
    return out


def channel_parts(channels):
    return [(0, channels // 2), (channels // 2, channels // 2)]


def projection_finish(features, w_short, tokens, half_index):
    streams, count, channels = w_short.shape
    half = channels // 2
    begin = half_index * half
    parts = [part for part in channel_parts(channels) if begin <= part[0] < begin + half]

    def body(total, side_sum, extra_refs, outs):
        (taps_ref,) = extra_refs
        projected_ref, first_ref, *message_refs = outs
        mean = jnp.sum(side_sum, axis=0, keepdims=True) * (1.0 / features)
        factor = lax.rsqrt(mean + epsilon)
        tails = []
        for stream in range(streams):
            projected = (total(stream) * factor).astype(bf16)
            projected_ref[stream] = projected
            tail = projected[:, tokens - block_len :].astype(f32).T
            tails.append(tail[block_len - count + 1 :])
        tails.append(jnp.zeros((side_rows - streams * (count - 1), half), f32))
        side = jnp.concatenate(tails, axis=0)
        taps = [tap_columns(taps_ref[stream]) for stream in (1, 2)]
        for (first, rows), message_ref in zip(parts, message_refs):
            tile = min(rows, 64)
            for start in range(first, first + rows, tile):
                here = slice(start - begin, start - begin + tile)
                key, value = (
                    smooth(
                        projected_ref[s, here].astype(f32),
                        taps[s - 1][start : start + tile],
                        count,
                        None,
                    )
                    for s in (1, 2)
                )
                first_ref[0, here] = key[:, :block_len]
                first_ref[1, here] = value[:, :block_len]
                message_ref[start - first : start - first + tile] = (key * value).astype(bf16)
            message_ref[rows:] = jnp.zeros((side_rows, tokens), bf16)
            here = side[:, first - begin : first - begin + rows]
            message_ref[rows:, :rows] = here.astype(bf16)

    out_shape = [shape_of((streams, half, tokens), bf16), shape_of((2, half, block_len), f32)]
    out_shape += [shape_of((rows + side_rows, tokens), bf16) for _, rows in parts]
    return body, [w_short], out_shape


def halo_columns(message_ref, streams, count, inside):
    rows = message_ref.shape[0] - side_rows
    side = jnp.where(inside, message_ref[rows:, :rows].astype(f32), 0.0).T
    return [side[:, s * (count - 1) : (s + 1) * (count - 1)] for s in range(streams)]


def halo_edges(message_ref, taps, inside):
    streams, count, rows = taps.shape
    side = jnp.where(inside, message_ref[rows:, :rows].astype(f32), 0.0)
    lines = []
    for s in range(streams):
        for token in range(count - 1):
            line = jnp.zeros((1, rows), f32)
            for tap in range(token + 1, count):
                at = s * (count - 1) + count - 1 + token - tap
                line = line + taps[s, tap : tap + 1] * side[at : at + 1]
            lines.append(line)
    lines.append(jnp.zeros((-len(lines) % 8, rows), f32))
    columns = jnp.concatenate(lines, axis=0).T
    lane = lax.broadcasted_iota(jnp.int32, (rows, block_len), 1)
    edges = []
    for s in range(streams):
        edge = jnp.zeros((rows, block_len), f32)
        for token in range(count - 1):
            at = s * (count - 1) + token
            edge = jnp.where(lane == token, columns[:, at : at + 1], edge)
        edges.append(edge)
    return edges


def split_table(table):
    high = table.astype(bf16)
    return high, (table - high.astype(np.float64)).astype(bf16)


def dft_tables():
    size = 2 * block_len
    freq = np.arange(block_len) + 0.5
    angle = 2.0 * math.pi / size * np.arange(size)[:, None] * freq[None, :]
    high, low = split_table(np.concatenate([np.cos(angle), -np.sin(angle)], axis=1))
    block = np.concatenate([high[:block_len], low[:block_len]])
    segment = np.concatenate([high, low])
    back = angle[block_len:].T
    inverse = np.concatenate([np.cos(back), -np.sin(back)], axis=0) * (2.0 / size)
    high, low = split_table(inverse)
    return block, segment, np.concatenate([high, low], axis=1)


def spectrum_lanes(k):
    return slice(2 * k * block_len, 2 * (k + 1) * block_len)


def block_lanes(k):
    return slice(k * block_len, (k + 1) * block_len)


def filter_spectra(long_filter, table):
    channels, lags = long_filter.shape

    def kernel(filter_ref, table_ref, spectra_ref):
        before = jnp.zeros((channels, block_len), bf16)
        for k in range(lags // block_len):
            now = filter_ref[:, block_lanes(k)]
            segment = jnp.concatenate([before, now, before, now], axis=1)
            spectra_ref[:, spectrum_lanes(k)] = dot(segment, table_ref[...])
            before = now

    return pl.pallas_call(
        kernel,
        in_specs=[in_vmem, in_vmem],
        out_specs=in_vmem,
        out_shape=shape_of((channels, 2 * lags), f32),
        compiler_params=params,
        cost_estimate=estimate(6e9, 0),
        name="filter_spectra",
    )(long_filter, table)


def block_spectra(pieces, table_ref, spec_ref, first):
    rows = pieces[0].shape[0]
    stacked = jnp.concatenate(pieces, axis=0)
    spectra = dot(jnp.concatenate([stacked, stacked], axis=1), table_ref[...])
    for k in range(len(pieces)):
        spec_ref[:rows, spectrum_lanes(first + k)] = spectra[k * rows : (k + 1) * rows]


def multiply_spectra(source_ref, filters_ref, filter_start, pairs, before_ref, total_ref):
    used = [term for terms in pairs for term in terms]
    for start in range(0, total_ref.shape[0], 8):
        here = slice(start, start + 8)
        there = slice(filter_start + start, filter_start + start + 8)

        def parts(ref, rows, k):
            return ref[rows, block_lanes(2 * k)], ref[rows, block_lanes(2 * k + 1)]

        sources = {b: parts(source_ref, here, b) for b in sorted({b for b, _ in used})}
        filters = {d: parts(filters_ref, there, d) for d in sorted({d for _, d in used})}
        for a, terms in enumerate(pairs):
            real = imag = None
            if before_ref is not None:
                real, imag = parts(before_ref, here, a)
            for b, d in terms:
                gr, gi = sources[b]
                hr, hi = filters[d]
                more_real, more_imag = gr * hr - gi * hi, gr * hi + gi * hr
                real = more_real if real is None else real + more_real
                imag = more_imag if imag is None else imag + more_imag
            if real is None:
                real = imag = jnp.zeros((8, block_len), f32)
            total_ref[here, block_lanes(2 * a)] = real
            total_ref[here, block_lanes(2 * a + 1)] = imag


def own_part(projected, messages, moved, taps, filters, table):
    streams, half, tokens = projected[0].shape
    parts = channel_parts(2 * half)
    number = len(parts)
    count = taps.shape[1]
    blocks = tokens // block_len
    first = 0 if moved else 1
    pairs = [[(b, a - b) for b in range(first, a + 1)] for a in range(blocks)]

    def kernel(*refs):
        refs = list(refs)
        take = lambda n: take_from(refs, n)
        projected_refs, message_refs = take(2), take(number)
        taps_ref, filters_ref, table_ref = take(3)
        query_refs, total_refs = take(number), take(number)
        gated_refs = take(number) if moved else None
        (spec_ref,) = refs
        columns = [tap_columns(taps_ref[s]) for s in range(streams)]
        for part, (begin, rows) in enumerate(parts):
            if moved:
                inside = lax.axis_index("ctx") > 0
                halo = halo_columns(message_refs[part], streams, count, inside)
            tile = min(rows, 64)
            for start in range(0, rows, tile):
                here = slice(start, start + tile)
                there = slice(begin + start, begin + start + tile)
                in_half = (begin + start) % half
                projected_ref = projected_refs[begin // half]

                def smoothed(s):
                    edge = halo[s][here] if moved else None
                    wide = projected_ref[s, in_half : in_half + tile].astype(f32)
                    return smooth(wide, columns[s][there], count, edge)

                query_refs[part][here] = smoothed(0)
                if moved:
                    gated_refs[part][here] = (smoothed(1) * smoothed(2)).astype(bf16)
            source_ref = gated_refs[part] if moved else message_refs[part]
            pieces = [source_ref[:rows, block_lanes(b)] for b in range(first, blocks)]
            block_spectra(pieces, table_ref, spec_ref, first)
            multiply_spectra(spec_ref, filters_ref, begin, pairs, None, total_refs[part])

    out_shape = [shape_of((rows, tokens), f32) for _, rows in parts]
    out_shape += [shape_of((rows, 2 * tokens), f32) for _, rows in parts]
    if moved:
        out_shape += [shape_of((rows, tokens), bf16) for _, rows in parts]
    inputs = [*projected, *(moved or messages), taps, filters, table]
    outs = pl.pallas_call(
        kernel,
        in_specs=[in_vmem] * len(inputs),
        out_specs=[in_vmem] * len(out_shape),
        out_shape=out_shape,
        scratch_shapes=[pltpu.VMEM((half, 2 * tokens), f32)],
        compiler_params=params,
        cost_estimate=estimate(0, 0),
        name="own_part",
    )(*inputs)
    gated = list(outs[2 * number :]) if moved else messages
    return list(outs[:number]), list(outs[number : 2 * number]), gated


def far_part(turn, begin, moved, total, filters, table, last, own):
    rows, tokens = total.shape[0], moved.shape[1]
    blocks = tokens // block_len
    pairs = [[(b, turn * blocks + a - b) for b in range(blocks)] for a in range(blocks)]
    if own:
        pairs = [terms + [(blocks, a)] for a, terms in enumerate(pairs)]
    channels_here = slice(begin, begin + rows)

    def kernel(*refs):
        refs = list(refs)
        take = lambda n: take_from(refs, n)
        moved_ref, total_ref, filters_ref, table_ref = take(4)
        own_refs = take(2) if own else None
        spec_ref = refs.pop()
        inside = lax.axis_index("ctx") >= turn
        pieces = [
            jnp.where(inside, moved_ref[:rows, block_lanes(b)], jnp.zeros((), bf16))
            for b in range(blocks)
        ]
        if last is None:
            block_spectra(pieces, table_ref, spec_ref, 0)
            multiply_spectra(spec_ref, filters_ref, begin, pairs, total_ref, refs[0])
            return
        sum_ref = refs.pop()
        back_ref, query_ref, gated_ref, skip_ref = take(4)
        out_ref = refs[-1]
        query, gated = (
            [ref[:rows, block_lanes(a)] for a in range(blocks)] for ref in (query_ref, gated_ref)
        )
        if own:
            first_ref, taps_ref = own_refs
            in_half = slice(begin % first_ref.shape[1], begin % first_ref.shape[1] + rows)
            edges = halo_edges(moved_ref, taps_ref[:, :, channels_here], inside)
            query[0] = query[0] + edges[0]
            key, value = first_ref[0, in_half] + edges[1], first_ref[1, in_half] + edges[2]
            gated[0] = (key * value).astype(bf16)
            pieces.append(gated[0])
        block_spectra(pieces, table_ref, spec_ref, 0)
        multiply_spectra(spec_ref, filters_ref, begin, pairs, total_ref, sum_ref)
        skip = column(skip_ref[...])[channels_here]
        spectra = [sum_ref[:, spectrum_lanes(a)] for a in range(blocks)]
        highs = [spectrum.astype(bf16) for spectrum in spectra]
        lows = [(s - high.astype(f32)).astype(bf16) for s, high in zip(spectra, highs)]
        both = dot(jnp.concatenate(highs, axis=0), back_ref[...])
        small = dot(jnp.concatenate(lows, axis=0), back_ref[:, :block_len])
        filtered = both[:, :block_len] + (both[:, block_len:] + small)
        for a in range(blocks):
            here = filtered[a * rows : (a + 1) * rows]
            mixed = (query[a] * (here + skip * gated[a].astype(f32))).astype(bf16)
            out_ref[:, block_lanes(a)] = mixed

    args = [moved, total, filters, table]
    if own:
        args += list(own)
    scratch = [pltpu.VMEM((rows, 2 * (blocks + 1) * block_len), f32)]
    out_shape = shape_of((rows, 2 * tokens), f32)
    if last is not None:
        inverse, query, gated, skip = last
        args += [inverse, query, gated, skip.reshape(1, -1)]
        out_shape = shape_of((rows, tokens), bf16)
        scratch.append(pltpu.VMEM((rows, 2 * tokens), f32))
    return pl.pallas_call(
        kernel,
        in_specs=[in_vmem] * len(args),
        out_specs=in_vmem,
        out_shape=out_shape,
        scratch_shapes=scratch[::-1],
        compiler_params=params,
        cost_estimate=estimate(0, 0),
        name=f"far_part_{turn}_{begin}",
    )(*args)


def from_before(block):
    count = lax.axis_size("ctx")
    return lax.ppermute(block, "ctx", [(i, (i + 1) % count) for i in range(count)])


def output_finish(channels, tokens):
    def body(total, side_sum, extra_refs, outs):
        outs[0][...] = total(0).astype(bf16)

    return body, [], [shape_of((channels, tokens), bf16)]


def shards(activations, norm_gain, w_in, w_short, long_filter, skip_gain, w_out):
    channels, tokens = activations.shape
    features = w_in.shape[2]
    w_short = w_short.transpose(0, 2, 1)
    turns = lax.axis_size("ctx")
    parts = channel_parts(channels)
    forward, segments, inverse = (jnp.asarray(t) for t in dft_tables())
    own = prepare(activations, norm_gain)

    filters = filter_spectra(long_filter, segments)
    finish = [projection_finish(features, w_short, tokens, k) for k in range(2)]
    results, (filters,) = gather_products(
        [own], w_in, [filters], True, finish, "projection"
    )
    projected = [result[0] for result in results]
    first_blocks = [result[1] for result in results]
    messages = [message for result in results for message in result[2:]]
    moving = [from_before(message) for message in messages]
    exact = turns > 2
    query, totals, gated = own_part(
        projected, messages, moving if exact else None, w_short, filters, forward
    )
    if exact:
        moving = [from_before(part) for part in gated]
    mixed = []
    for turn in range(1, turns):
        for k, (begin, _) in enumerate(parts):
            last = own_block = None
            if turn == turns - 1:
                last = (inverse, query[k], gated[k], skip_gain)
                if not exact:
                    own_block = (first_blocks[2 * begin // channels], w_short)
            done = far_part(
                turn, begin, moving[k], totals[k], filters, forward, last, own_block
            )
            if last is None:
                totals[k] = done
                moving[k] = from_before(moving[k])
            else:
                mixed.append(done)

    finish = [output_finish(channels, tokens)]
    ((result,),), _ = gather_products(
        mixed, w_out[None], [], False, finish, "output"
    )
    return result


def solution(mesh):
    placed = (
        P("fsdp", "ctx"),
        P("fsdp"),
        P(None, "fsdp", None),
        P(None, "fsdp", None),
        P("fsdp", None),
        P("fsdp"),
        P("fsdp", None),
    )
    return jax.shard_map(
        shards, mesh=mesh, in_specs=placed, out_specs=P("fsdp", "ctx"), check_vma=False
    )
```

```python
import math

import jax
import jax.numpy as jnp
import numpy as np
from jax import lax
from jax.experimental import pallas as pl
from jax.experimental.pallas import tpu as pltpu
from jax.sharding import PartitionSpec as P

epsilon = 1e-05
block_len = 128
STAGGER = 2e9
side_rows = 8
bf16 = jnp.bfloat16
f32 = jnp.float32
in_vmem = pl.BlockSpec(memory_space=pltpu.VMEM)
params = pltpu.CompilerParams(vmem_limit_bytes=12 * 2**20)


def shape_of(shape, dtype):
    return jax.ShapeDtypeStruct(tuple(shape), dtype)


def dot(left, right):
    return jnp.dot(left, right, preferred_element_type=f32)


def column(row):
    return jnp.broadcast_to(row, (8, row.shape[1])).T[:, :1]


def tap_columns(taps):
    return jnp.concatenate([taps, jnp.zeros((8 - taps.shape[0], taps.shape[1]), f32)], axis=0).T


def estimate(flops, size):
    return pl.CostEstimate(flops=int(flops), bytes_accessed=int(size), transcendentals=0)


def begin():
    def kernel(out_ref):
        out_ref[...] = jnp.zeros(out_ref.shape, f32)

    return pl.pallas_call(
        kernel,
        out_specs=in_vmem,
        out_shape=shape_of((8, 128), f32),
        compiler_params=params,
        cost_estimate=estimate(3e9, 0),
        name="begin",
    )()


def prepare_kernel(x_ref, gain_ref, begun_ref, out_ref):
    rows = x_ref.shape[0]
    wide = x_ref[...].astype(f32)
    out_ref[:rows] = (wide * column(gain_ref[...])).astype(bf16)
    squares = jnp.sum(wide * wide, axis=0, keepdims=True)
    high = squares.astype(bf16).astype(f32)
    row = lax.broadcasted_iota(jnp.int32, (side_rows, wide.shape[1]), 0)
    side = jnp.where(row == 0, high, jnp.where(row == 1, squares - high, 0.0))
    out_ref[rows:] = side.astype(bf16)


def prepare(x, gain):
    rows, tokens = x.shape
    return pl.pallas_call(
        prepare_kernel,
        in_specs=[in_vmem, in_vmem, in_vmem],
        out_specs=in_vmem,
        out_shape=shape_of((rows + side_rows, tokens), bf16),
        compiler_params=params,
        cost_estimate=estimate(3e9, 0),
        name="prepare",
    )(x, gain.reshape(1, rows), begin())


def chip_count():
    return lax.axis_size("fsdp") // 2


def ring_order(count):
    return list(range(0, count, 2)) + list(range(1, count, 2))[::-1]


def along_ring(block):
    chips = chip_count()
    order = ring_order(chips)
    pairs = []
    for i in range(chips):
        here, after = order[i], order[(i + 1) % chips]
        pairs += [(2 * here, 2 * after), (2 * after + 1, 2 * here + 1)]
    return lax.ppermute(block, "fsdp", pairs)


def other_core(block):
    return lax.ppermute(block, "fsdp", [(i, i ^ 1) for i in range(2 * chip_count())])


def my_core():
    return lax.axis_index("fsdp") & 1


def source_chip(steps):
    chips = chip_count()
    chip = lax.shift_right_logical(lax.axis_index("fsdp"), 1)
    half = lax.shift_right_logical(chip, 1)
    place = jnp.where(chip & 1 == 0, half, chips - 1 - half)
    place = place + jnp.where(my_core() == 0, chips - steps, steps)
    place = jnp.where(place >= chips, place - chips, place)
    return jnp.where(place < (chips + 1) // 2, 2 * place, 2 * (chips - 1 - place) + 1)


def take_from(refs, number):
    return [refs.pop(0) for _ in range(number)]


def products(items, weight, running, side, finish, cost, name):
    body, extras, out_shape, cut, senders_only = finish or (None, [], None, None, False)
    streams, out_rows, features = weight.shape
    cut = cut or (0, out_rows)
    out_here, out_rows = slice(cut[0], cut[0] + cut[1]), cut[1]
    rows = features // lax.axis_size("fsdp")
    shards = [piece for _, _, pieces in items for piece in pieces]
    tokens = shards[0].shape[1]
    count = len(shards)
    first_group = running is None
    state = [] if first_group else list(running)
    padded = rows % 128 != 0
    width = 2 * rows if padded else rows
    scratch_shapes = [pltpu.VMEM((len(items) * width, tokens), bf16)] if padded else []

    def kernel(*refs):
        refs = list(refs)
        take = lambda n: take_from(refs, n)
        shard_refs = take(count)
        (weight_ref,) = take(1)
        state_refs = take(len(state))
        extra_refs = take(len(extras))
        outs = take(len(out_shape))

        def work():
            core = my_core()
            chip_of = {steps: source_chip(steps) for steps in sorted({item[0] for item in items})}
            if padded:
                (beside_ref,) = refs
                beside_ref[...] = jnp.zeros(beside_ref.shape, bf16)
            sides, right = [], []
            pieces_left = list(shard_refs)
            for k, (_, other, pieces) in enumerate(items):
                done = 0
                for piece_ref in take_from(pieces_left, len(pieces)):
                    more = min(piece_ref.shape[0], rows - done)
                    if padded:
                        at = k * width + jnp.where(core == other, 0, rows) + done
                        at = pl.multiple_of(at, math.gcd(rows, done or rows))
                        beside_ref[pl.ds(at, more)] = piece_ref[:more]
                    else:
                        right.append(piece_ref[:more])
                    if more < piece_ref.shape[0]:
                        sides.append(piece_ref[more:].astype(f32))
                    done += more
            right = beside_ref[...] if padded else jnp.concatenate(right, axis=0)
            side_sum = None
            if side:
                parts = sides + ([] if first_group else [state_refs[1][...]])
                side_sum = sum(parts[1:], parts[0])

            def total(stream, lanes=slice(None)):
                left = []
                for steps, other, _ in items:
                    block = chip_of[steps]
                    if not padded:
                        block = 2 * block + (1 - core if other else core)
                    at = pl.ds(pl.multiple_of(block * width, width), width)
                    left.append(weight_ref[stream, out_here, at])
                product = dot(jnp.concatenate(left, axis=1), right[:, lanes])
                if first_group:
                    return product
                return state_refs[0][stream, out_here, lanes] + product

            if body is not None:
                body(total, side_sum, extra_refs, outs)
                return
            for stream in range(streams):
                outs[0][stream] = total(stream)
            if side:
                outs[1][...] = side_sum

        if senders_only:
            pl.when(lax.axis_index("ctx") < lax.axis_size("ctx") - 1)(work)
        else:
            work()

    aliases = {}
    if body is None:
        out_shape = [shape_of((streams, out_rows, tokens), f32)]
        if side:
            out_shape.append(shape_of((side_rows, tokens), f32))
        if not first_group:
            aliases = {count + 1 + i: i for i in range(len(state))}
    return pl.pallas_call(
        kernel,
        in_specs=[in_vmem] * (count + 1 + len(state) + len(extras)),
        out_specs=[in_vmem] * len(out_shape),
        out_shape=out_shape,
        scratch_shapes=scratch_shapes,
        input_output_aliases=aliases,
        compiler_params=params,
        cost_estimate=estimate(cost, 0),
        name=name,
    )(*shards, weight, *state, *extras)


def gather_products(own, weight, beside, side, name):
    chips = chip_count()
    last_step = chips // 2

    def send(way, pieces, scope):
        sent = []
        for k, piece in enumerate(pieces):
            with jax.named_scope(f"{name}_{scope}_{k}"):
                sent.append(way(piece))
        return sent

    def joined(pieces):
        return [jnp.concatenate(pieces, axis=0)] if len(pieces) > 1 else pieces

    near, far = own, send(other_core, own, "core_own")
    items = [(0, 0, near), (0, 1, far)]
    running = None
    for step in range(1, last_step + 1):
        near = joined(send(along_ring, near, f"near_{step}"))
        arrived = near
        if running is not None:
            arrived, running = lax.optimization_barrier((near, running))
        elif beside:
            arrived, beside = lax.optimization_barrier((near, beside))
        theirs = send(other_core, arrived, f"core_near_{step}")
        pair = [(step, 0, arrived), (chips - step, 1, theirs)]
        if step < last_step:
            running = products(items + pair, weight, running, side, None, 0, f"{name}_{step}")
            far = joined(send(along_ring, far, f"far_{step}"))
            theirs = send(other_core, far, f"core_far_{step}")
            items = [(step, 1, far), (chips - step, 0, theirs)]
        else:
            items.append(pair[0])
            running = products(items, weight, running, side, None, STAGGER, f"{name}_{step}")
            items = pair[1:]

    def last(finish, running):
        return products(items, weight, running, side, finish, 0, f"{name}_last")

    return last, running, beside


def smooth(projected, taps, count, halo):
    lane = lax.broadcasted_iota(jnp.int32, projected.shape, 1)
    out = taps[:, :1] * projected
    for tap in range(1, count):
        moved = pltpu.roll(projected, tap, 1)
        for place in range(tap):
            edge = 0.0
            if halo is not None:
                at = halo.shape[1] - tap + place
                edge = halo[:, at : at + 1]
            moved = jnp.where(lane == place, edge, moved)
        out = out + taps[:, tap : tap + 1] * moved
    return out


def channel_parts(channels):
    first = channels * 4 // 8 // 16 * 16
    return [(0, first), (first, channels - first)]


def norm_factor(side_sum, features):
    mean = jnp.sum(side_sum, axis=0, keepdims=True) * (1.0 / features)
    return lax.rsqrt(mean + epsilon)


def gate(projected, taps_ref, begin, write):
    count = taps_ref.shape[1]
    columns = [tap_columns(taps_ref[stream]) for stream in (1, 2)]
    rows = projected[0].shape[0]
    tile = math.gcd(rows, 64)
    for start in range(0, rows, tile):
        here = slice(start, start + tile)
        there = slice(begin + start, begin + start + tile)
        key, value = (
            smooth(wide[here].astype(f32), column[there], count, None)
            for wide, column in zip(projected, columns)
        )
        write(here, key, value)


def message_finish(features, w_short, tokens, part):
    streams, count, channels = w_short.shape
    parts = channel_parts(channels)
    begin, rows = parts[part]
    last = slice(tokens - block_len, tokens)

    def body(total, side_sum, extra_refs, outs):
        (taps_ref,), (message_ref,) = extra_refs, outs
        factor = norm_factor(side_sum, features)
        projected = [(total(stream) * factor).astype(bf16) for stream in (1, 2)]
        ends = [(total(0, last) * factor[:, last]).astype(bf16)]
        ends += [wide[:, last] for wide in projected]
        lines = [end.astype(f32).T[block_len - count + 1 :] for end in ends]
        lines.append(jnp.zeros((side_rows - streams * (count - 1), rows), f32))

        def write(here, key, value):
            message_ref[here] = (key * value).astype(bf16)

        gate(projected, taps_ref, begin, write)
        message_ref[rows:] = jnp.zeros((side_rows, tokens), bf16)
        message_ref[rows:, :rows] = jnp.concatenate(lines, axis=0).astype(bf16)

    out_shape = [shape_of((rows + side_rows, tokens), bf16)]
    return body, [w_short], out_shape, parts[part], True


def projection_finish(features, w_short, tokens, part):
    streams, _, channels = w_short.shape
    parts = channel_parts(channels)
    begin, rows = parts[part]

    def body(total, side_sum, extra_refs, outs):
        (taps_ref,), (projected_ref, first_ref, gated_ref) = extra_refs, outs
        factor = norm_factor(side_sum, features)
        projected = [(total(stream) * factor).astype(bf16) for stream in range(streams)]
        for stream in range(streams):
            projected_ref[stream] = projected[stream]

        def write(here, key, value):
            first_ref[0, here] = key[:, :block_len]
            first_ref[1, here] = value[:, :block_len]
            gated_ref[here] = (key * value).astype(bf16)

        gate(projected[1:], taps_ref, begin, write)

    out_shape = [
        shape_of((streams, rows, tokens), bf16),
        shape_of((2, rows, block_len), f32),
        shape_of((rows, tokens), bf16),
    ]
    return body, [w_short], out_shape, parts[part], False


def halo_columns(message_ref, streams, count, inside):
    rows = message_ref.shape[0] - side_rows
    side = jnp.where(inside, message_ref[rows:, :rows].astype(f32), 0.0).T
    return [side[:, s * (count - 1) : (s + 1) * (count - 1)] for s in range(streams)]


def halo_edges(message_ref, taps):
    streams, count, rows = taps.shape
    side = message_ref[rows:, :rows].astype(f32)
    lines = []
    for s in range(streams):
        for token in range(count - 1):
            line = jnp.zeros((1, rows), f32)
            for tap in range(token + 1, count):
                at = s * (count - 1) + count - 1 + token - tap
                line = line + taps[s, tap : tap + 1] * side[at : at + 1]
            lines.append(line)
    lines.append(jnp.zeros((-len(lines) % 8, rows), f32))
    columns = jnp.concatenate(lines, axis=0).T
    lane = lax.broadcasted_iota(jnp.int32, (rows, block_len), 1)
    edges = []
    for s in range(streams):
        edge = jnp.zeros((rows, block_len), f32)
        for token in range(count - 1):
            at = s * (count - 1) + token
            edge = jnp.where(lane == token, columns[:, at : at + 1], edge)
        edges.append(edge)
    return edges


def split_table(table):
    high = table.astype(bf16)
    return high, (table - high.astype(np.float64)).astype(bf16)


def dft_tables():
    size = 2 * block_len
    freq = np.arange(block_len) + 0.5
    angle = 2.0 * math.pi / size * np.arange(size)[:, None] * freq[None, :]
    high, low = split_table(np.concatenate([np.cos(angle), -np.sin(angle)], axis=1))
    block = np.concatenate([high[:block_len], low[:block_len]])
    segment = np.concatenate([high, low])
    back = angle[block_len:].T
    inverse = np.concatenate([np.cos(back), -np.sin(back)], axis=0) * (2.0 / size)
    high, low = split_table(inverse)
    return block, segment, np.concatenate([high, low], axis=1)


def spectrum_lanes(k):
    return slice(2 * k * block_len, 2 * (k + 1) * block_len)


def block_lanes(k):
    return slice(k * block_len, (k + 1) * block_len)


def filter_spectra(long_filter, table):
    channels, lags = long_filter.shape

    def kernel(filter_ref, table_ref, spectra_ref):
        before = jnp.zeros((channels, block_len), bf16)
        for k in range(lags // block_len):
            now = filter_ref[:, block_lanes(k)]
            segment = jnp.concatenate([before, now, before, now], axis=1)
            spectra_ref[:, spectrum_lanes(k)] = dot(segment, table_ref[...])
            before = now

    return pl.pallas_call(
        kernel,
        in_specs=[in_vmem, in_vmem],
        out_specs=in_vmem,
        out_shape=shape_of((channels, 2 * lags), f32),
        compiler_params=params,
        cost_estimate=estimate(6e9, 0),
        name="filter_spectra",
    )(long_filter, table)


def block_spectra(pieces, table_ref, spec_ref, first):
    rows = pieces[0].shape[0]
    stacked = jnp.concatenate(pieces, axis=0)
    spectra = dot(jnp.concatenate([stacked, stacked], axis=1), table_ref[...])
    for k in range(len(pieces)):
        spec_ref[:rows, spectrum_lanes(first + k)] = spectra[k * rows : (k + 1) * rows]


def multiply_spectra(source_ref, filters_ref, filter_start, pairs, before_ref, total_ref):
    used = [term for terms in pairs for term in terms]
    for start in range(0, total_ref.shape[0], 8):
        here = slice(start, start + 8)
        there = slice(filter_start + start, filter_start + start + 8)

        def parts(ref, rows, k):
            return ref[rows, block_lanes(2 * k)], ref[rows, block_lanes(2 * k + 1)]

        sources = {b: parts(source_ref, here, b) for b in sorted({b for b, _ in used})}
        filters = {d: parts(filters_ref, there, d) for d in sorted({d for _, d in used})}
        for a, terms in enumerate(pairs):
            real = imag = None
            if before_ref is not None:
                real, imag = parts(before_ref, here, a)
            for b, d in terms:
                gr, gi = sources[b]
                hr, hi = filters[d]
                more_real, more_imag = gr * hr - gi * hi, gr * hi + gi * hr
                real = more_real if real is None else real + more_real
                imag = more_imag if imag is None else imag + more_imag
            if real is None:
                real = imag = jnp.zeros((8, block_len), f32)
            total_ref[here, block_lanes(2 * a)] = real
            total_ref[here, block_lanes(2 * a + 1)] = imag


def own_part(projected, alone, moved, taps, filters, table):
    streams, _, tokens = projected[0].shape
    parts = channel_parts(taps.shape[2])
    number = len(parts)
    count = taps.shape[1]
    blocks = tokens // block_len
    first = 0 if moved else 1
    pairs = [[(b, a - b) for b in range(first, a + 1)] for a in range(blocks)]

    def kernel(*refs):
        refs = list(refs)
        take = lambda n: take_from(refs, n)
        projected_refs, message_refs = take(number), take(number)
        taps_ref, filters_ref, table_ref = take(3)
        query_refs, total_refs = take(number), take(number)
        gated_refs = take(number) if moved else None
        (spec_ref,) = refs
        columns = [tap_columns(taps_ref[s]) for s in range(streams)]
        for part, (begin, rows) in enumerate(parts):
            if moved:
                inside = lax.axis_index("ctx") > 0
                halo = halo_columns(message_refs[part], streams, count, inside)
            tile = math.gcd(rows, 64)
            for start in range(0, rows, tile):
                here = slice(start, start + tile)
                there = slice(begin + start, begin + start + tile)
                projected_ref = projected_refs[part]

                def smoothed(s):
                    edge = halo[s][here] if moved else None
                    wide = projected_ref[s, here].astype(f32)
                    return smooth(wide, columns[s][there], count, edge)

                query_refs[part][here] = smoothed(0)
                if moved:
                    gated_refs[part][here] = (smoothed(1) * smoothed(2)).astype(bf16)
            source_ref = gated_refs[part] if moved else message_refs[part]
            pieces = [source_ref[:rows, block_lanes(b)] for b in range(first, blocks)]
            block_spectra(pieces, table_ref, spec_ref, first)
            multiply_spectra(spec_ref, filters_ref, begin, pairs, None, total_refs[part])

    out_shape = [shape_of((rows, tokens), f32) for _, rows in parts]
    out_shape += [shape_of((rows, 2 * tokens), f32) for _, rows in parts]
    if moved:
        out_shape += [shape_of((rows, tokens), bf16) for _, rows in parts]
    inputs = [*projected, *(moved or alone), taps, filters, table]
    outs = pl.pallas_call(
        kernel,
        in_specs=[in_vmem] * len(inputs),
        out_specs=[in_vmem] * len(out_shape),
        out_shape=out_shape,
        scratch_shapes=[pltpu.VMEM((max(rows for _, rows in parts), 2 * tokens), f32)],
        compiler_params=params,
        cost_estimate=estimate(0, 0),
        name="own_part",
    )(*inputs)
    gated = list(outs[2 * number :]) if moved else alone
    return list(outs[:number]), list(outs[number : 2 * number]), gated


def far_part(turn, begin, moved, total, filters, table, last, own):
    rows, tokens = total.shape[0], moved.shape[1]
    blocks = tokens // block_len
    far_pairs = [[(b, turn * blocks + a - b) for b in range(blocks)] for a in range(blocks)]
    channels_here = slice(begin, begin + rows)

    def kernel(*refs):
        refs = list(refs)
        take = lambda n: take_from(refs, n)
        moved_ref, total_ref, filters_ref, table_ref = take(4)
        own_refs = take(2) if own else None
        spec_ref = refs.pop()
        sum_ref = refs.pop()
        if last:
            last_refs = take(4)
            (out_ref,) = refs

        def work(inside):
            pieces = [moved_ref[:rows, block_lanes(b)] for b in range(blocks)] if inside else []
            pairs = far_pairs if inside else [[] for _ in range(blocks)]
            if last:
                back_ref, query_ref, gated_ref, skip_ref = last_refs
                query, gated = (
                    [ref[:rows, block_lanes(a)] for a in range(blocks)]
                    for ref in (query_ref, gated_ref)
                )
            if own:
                first_ref, taps_ref = own_refs
                key, value = first_ref[0], first_ref[1]
                if inside:
                    edges = halo_edges(moved_ref, taps_ref[:, :, channels_here])
                    query[0] = query[0] + edges[0]
                    key, value = key + edges[1], value + edges[2]
                gated[0] = (key * value).astype(bf16)
                pairs = [terms + [(len(pieces), a)] for a, terms in enumerate(pairs)]
                pieces.append(gated[0])
            if pieces:
                block_spectra(pieces, table_ref, spec_ref, 0)
            multiply_spectra(spec_ref, filters_ref, begin, pairs, total_ref, sum_ref)
            if not last:
                return
            skip = column(skip_ref[...])[channels_here]
            spectra = [sum_ref[:, spectrum_lanes(a)] for a in range(blocks)]
            highs = [spectrum.astype(bf16) for spectrum in spectra]
            lows = [(s - high.astype(f32)).astype(bf16) for s, high in zip(spectra, highs)]
            both = dot(jnp.concatenate(highs, axis=0), back_ref[...])
            small = dot(jnp.concatenate(lows, axis=0), back_ref[:, :block_len])
            filtered = both[:, :block_len] + (both[:, block_len:] + small)
            for a in range(blocks):
                here = filtered[a * rows : (a + 1) * rows]
                mixed = query[a] * (here + skip * gated[a].astype(f32))
                out_ref[:, block_lanes(a)] = mixed.astype(bf16)

        inside = lax.axis_index("ctx") >= turn
        pl.when(inside)(lambda: work(True))
        pl.when(jnp.logical_not(inside))(lambda: work(False))

    args = [moved, total, filters, table]
    if own:
        args += list(own)
    scratch = [pltpu.VMEM((rows, 2 * (blocks + 1) * block_len), f32)]
    out_shape = shape_of((rows, 2 * tokens), f32)
    if last is not None:
        inverse, query, gated, skip = last
        args += [inverse, query, gated, skip.reshape(1, -1)]
        out_shape = shape_of((rows, tokens), bf16)
        scratch.append(pltpu.VMEM((rows, 2 * tokens), f32))
    return pl.pallas_call(
        kernel,
        in_specs=[in_vmem] * len(args),
        out_specs=in_vmem,
        out_shape=out_shape,
        scratch_shapes=scratch[::-1],
        compiler_params=params,
        cost_estimate=estimate(0, 0),
        name=f"far_part_{turn}_{begin}",
    )(*args)


def from_before(block):
    count = lax.axis_size("ctx")
    return lax.ppermute(block, "ctx", [(i, (i + 1) % count) for i in range(count)])


def output_finish(channels, tokens):
    def body(total, side_sum, extra_refs, outs):
        outs[0][...] = total(0).astype(bf16)

    return body, [], [shape_of((channels, tokens), bf16)], None, False


def shards(activations, norm_gain, w_in, w_short, long_filter, skip_gain, w_out):
    channels, tokens = activations.shape
    features = w_in.shape[2]
    w_short = w_short.transpose(0, 2, 1)
    turns = lax.axis_size("ctx")
    parts = channel_parts(channels)
    forward, segments, inverse = (jnp.asarray(t) for t in dft_tables())
    own = prepare(activations, norm_gain)

    filters = filter_spectra(long_filter, segments)
    last, running, (filters,) = gather_products([own], w_in, [filters], True, "projection")

    def message(part, running):
        (sent,) = last(message_finish(features, w_short, tokens, part), running)
        return from_before(sent)

    exact = turns > 2
    moving = [message(0, running)]
    results = [last(projection_finish(features, w_short, tokens, k), running) for k in range(2)]
    projected, first_blocks, gated = zip(*results)
    later, gated = lax.optimization_barrier((running, gated))
    moving.append(message(1, later))
    query, totals, gated = own_part(
        projected, gated, moving if exact else None, w_short, filters, forward
    )
    if exact:
        moving = [from_before(part) for part in gated]
    mixed = []
    for turn in range(1, turns):
        for k, (begin, _) in enumerate(parts):
            last = own_block = None
            if turn == turns - 1:
                last = (inverse, query[k], gated[k], skip_gain)
                if not exact:
                    own_block = (first_blocks[k], w_short)
            done = far_part(
                turn, begin, moving[k], totals[k], filters, forward, last, own_block
            )
            if last is None:
                totals[k] = done
                moving[k] = from_before(moving[k])
            else:
                mixed.append(done)

    last, running, _ = gather_products(mixed, w_out[None], [], False, "output")
    (result,) = last(output_finish(channels, tokens), running)
    return result


def solution(mesh):
    placed = (
        P("fsdp", "ctx"),
        P("fsdp"),
        P(None, "fsdp", None),
        P(None, "fsdp", None),
        P("fsdp", None),
        P("fsdp"),
        P("fsdp", None),
    )
    return jax.shard_map(
        shards, mesh=mesh, in_specs=placed, out_specs=P("fsdp", "ctx"), check_vma=False
    )
```

```python
import math

import jax
import jax.numpy as jnp
import numpy as np
from jax import lax
from jax.experimental import pallas as pl
from jax.experimental.pallas import tpu as pltpu
from jax.sharding import PartitionSpec as P

epsilon = 1e-05
block_len = 128
STAGGER = 2e9
side_rows = 8
bf16 = jnp.bfloat16
f32 = jnp.float32
in_vmem = pl.BlockSpec(memory_space=pltpu.VMEM)
params = pltpu.CompilerParams(vmem_limit_bytes=12 * 2**20)


def shape_of(shape, dtype):
    return jax.ShapeDtypeStruct(tuple(shape), dtype)


def dot(left, right):
    return jnp.dot(left, right, preferred_element_type=f32)


def column(row):
    return jnp.broadcast_to(row, (8, row.shape[1])).T[:, :1]


def tap_columns(taps):
    return jnp.concatenate([taps, jnp.zeros((8 - taps.shape[0], taps.shape[1]), f32)], axis=0).T


def estimate(flops, size):
    return pl.CostEstimate(flops=int(flops), bytes_accessed=int(size), transcendentals=0)


def begin():
    def kernel(out_ref):
        out_ref[...] = jnp.zeros(out_ref.shape, f32)

    return pl.pallas_call(
        kernel,
        out_specs=in_vmem,
        out_shape=shape_of((8, 128), f32),
        compiler_params=params,
        cost_estimate=estimate(3e9, 0),
        name="begin",
    )()


def prepare_kernel(x_ref, gain_ref, begun_ref, out_ref):
    rows = x_ref.shape[0]
    wide = x_ref[...].astype(f32)
    out_ref[:rows] = (wide * column(gain_ref[...])).astype(bf16)
    squares = jnp.sum(wide * wide, axis=0, keepdims=True)
    high = squares.astype(bf16).astype(f32)
    row = lax.broadcasted_iota(jnp.int32, (side_rows, wide.shape[1]), 0)
    side = jnp.where(row == 0, high, jnp.where(row == 1, squares - high, 0.0))
    out_ref[rows:] = side.astype(bf16)


def prepare(x, gain):
    rows, tokens = x.shape
    return pl.pallas_call(
        prepare_kernel,
        in_specs=[in_vmem, in_vmem, in_vmem],
        out_specs=in_vmem,
        out_shape=shape_of((rows + side_rows, tokens), bf16),
        compiler_params=params,
        cost_estimate=estimate(3e9, 0),
        name="prepare",
    )(x, gain.reshape(1, rows), begin())


def chip_count():
    return lax.axis_size("fsdp") // 2


def ring_order(count):
    return list(range(0, count, 2)) + list(range(1, count, 2))[::-1]


def along_ring(block):
    chips = chip_count()
    order = ring_order(chips)
    pairs = []
    for i in range(chips):
        here, after = order[i], order[(i + 1) % chips]
        pairs += [(2 * here, 2 * after), (2 * after + 1, 2 * here + 1)]
    return lax.ppermute(block, "fsdp", pairs)


def other_core(block):
    return lax.ppermute(block, "fsdp", [(i, i ^ 1) for i in range(2 * chip_count())])


def my_core():
    return lax.axis_index("fsdp") & 1


def source_chip(steps):
    chips = chip_count()
    chip = lax.shift_right_logical(lax.axis_index("fsdp"), 1)
    half = lax.shift_right_logical(chip, 1)
    place = jnp.where(chip & 1 == 0, half, chips - 1 - half)
    place = place + jnp.where(my_core() == 0, chips - steps, steps)
    place = jnp.where(place >= chips, place - chips, place)
    return jnp.where(place < (chips + 1) // 2, 2 * place, 2 * (chips - 1 - place) + 1)


def take_from(refs, number):
    return [refs.pop(0) for _ in range(number)]


def products(items, weight, running, side, finish, cost, name):
    body, extras, out_shape, cut, senders_only = finish or (None, [], None, None, False)
    streams, out_rows, features = weight.shape
    cut = cut or (0, out_rows)
    out_here, out_rows = slice(cut[0], cut[0] + cut[1]), cut[1]
    rows = features // lax.axis_size("fsdp")
    shards = [piece for _, _, pieces in items for piece in pieces]
    tokens = shards[0].shape[1]
    count = len(shards)
    first_group = running is None
    state = [] if first_group else list(running)
    padded = rows % 128 != 0
    width = 2 * rows if padded else rows
    scratch_shapes = [pltpu.VMEM((len(items) * width, tokens), bf16)] if padded else []

    def kernel(*refs):
        refs = list(refs)
        take = lambda n: take_from(refs, n)
        shard_refs = take(count)
        (weight_ref,) = take(1)
        state_refs = take(len(state))
        extra_refs = take(len(extras))
        outs = take(len(out_shape))

        def work():
            core = my_core()
            chip_of = {steps: source_chip(steps) for steps in sorted({item[0] for item in items})}
            if padded:
                (beside_ref,) = refs
                beside_ref[...] = jnp.zeros(beside_ref.shape, bf16)
            sides, right = [], []
            pieces_left = list(shard_refs)
            for k, (_, other, pieces) in enumerate(items):
                done = 0
                for piece_ref in take_from(pieces_left, len(pieces)):
                    more = min(piece_ref.shape[0], rows - done)
                    if padded:
                        at = k * width + jnp.where(core == other, 0, rows) + done
                        at = pl.multiple_of(at, math.gcd(rows, done or rows))
                        beside_ref[pl.ds(at, more)] = piece_ref[:more]
                    else:
                        right.append(piece_ref[:more])
                    if more < piece_ref.shape[0]:
                        sides.append(piece_ref[more:].astype(f32))
                    done += more
            right = beside_ref[...] if padded else jnp.concatenate(right, axis=0)
            side_sum = None
            if side:
                parts = sides + ([] if first_group else [state_refs[1][...]])
                side_sum = sum(parts[1:], parts[0])

            def total(stream, lanes=slice(None), out_here=out_here):
                left = []
                for steps, other, _ in items:
                    block = chip_of[steps]
                    if not padded:
                        block = 2 * block + (1 - core if other else core)
                    at = pl.ds(pl.multiple_of(block * width, width), width)
                    left.append(weight_ref[stream, out_here, at])
                product = dot(jnp.concatenate(left, axis=1), right[:, lanes])
                if first_group:
                    return product
                return state_refs[0][stream, out_here, lanes] + product

            if body is not None:
                body(total, side_sum, extra_refs, outs)
                return
            for stream in range(streams):
                outs[0][stream] = total(stream)
            if side:
                outs[1][...] = side_sum

        if senders_only:
            pl.when(lax.axis_index("ctx") < lax.axis_size("ctx") - 1)(work)
        else:
            work()

    aliases = {}
    if body is None:
        out_shape = [shape_of((streams, out_rows, tokens), f32)]
        if side:
            out_shape.append(shape_of((side_rows, tokens), f32))
        if not first_group:
            aliases = {count + 1 + i: i for i in range(len(state))}
    return pl.pallas_call(
        kernel,
        in_specs=[in_vmem] * (count + 1 + len(state) + len(extras)),
        out_specs=[in_vmem] * len(out_shape),
        out_shape=out_shape,
        scratch_shapes=scratch_shapes,
        input_output_aliases=aliases,
        compiler_params=params,
        cost_estimate=estimate(cost, 0),
        name=name,
    )(*shards, weight, *state, *extras)


def pass_on(near, far):
    rows = near.shape[0] - side_rows

    def kernel(near_ref, far_ref, out_ref):
        out_ref[:rows] = near_ref[:rows]
        below = pltpu.roll(far_ref[rows:].astype(f32), 2, 0)
        out_ref[rows:] = (near_ref[rows:].astype(f32) + below).astype(bf16)

    return pl.pallas_call(
        kernel,
        in_specs=[in_vmem, in_vmem],
        out_specs=in_vmem,
        out_shape=shape_of(near.shape, bf16),
        compiler_params=params,
        cost_estimate=estimate(0, 0),
        name="pass_on",
    )(near, far)


def gather_products(own, weight, beside, side, name):
    chips = chip_count()
    last_step = chips // 2

    def send(way, pieces, scope):
        sent = []
        for k, piece in enumerate(pieces):
            with jax.named_scope(f"{name}_{scope}_{k}"):
                sent.append(way(piece))
        return sent

    def joined(pieces):
        return [jnp.concatenate(pieces, axis=0)] if len(pieces) > 1 else pieces

    near, far = own, send(other_core, own, "core_own")
    items = [(0, 0, near), (0, 1, far)]
    sibling = far
    if side:
        far = [far[0][: far[0].shape[0] - side_rows]]
    running = None
    for step in range(1, last_step + 1):
        near = joined(send(along_ring, near, f"near_{step}"))
        arrived = near
        if running is not None:
            arrived, running = lax.optimization_barrier((near, running))
        elif beside:
            arrived, beside = lax.optimization_barrier((near, beside))
        theirs = send(other_core, arrived, f"core_near_{step}")
        pair = [(step, 0, arrived), (chips - step, 1, theirs)]
        if step < last_step:
            running = products(items + pair, weight, running, side, None, 0, f"{name}_{step}")
            if side and step == 1:
                near = [pass_on(near[0], sibling[0])]
            far = joined(send(along_ring, far, f"far_{step}"))
            theirs = send(other_core, far, f"core_far_{step}")
            items = [(step, 1, far), (chips - step, 0, theirs)]
        else:
            items.append(pair[0])
            running = products(items, weight, running, side, None, STAGGER, f"{name}_{step}")
            items = pair[1:]

    def last(finish, running):
        return products(items, weight, running, side, finish, 0, f"{name}_last")

    return last, running, beside


def smooth(projected, taps, count, halo):
    lane = lax.broadcasted_iota(jnp.int32, projected.shape, 1)
    out = taps[:, :1] * projected
    for tap in range(1, count):
        moved = pltpu.roll(projected, tap, 1)
        for place in range(tap):
            edge = 0.0
            if halo is not None:
                at = halo.shape[1] - tap + place
                edge = halo[:, at : at + 1]
            moved = jnp.where(lane == place, edge, moved)
        out = out + taps[:, tap : tap + 1] * moved
    return out


def channel_parts(channels):
    first = channels * 4 // 8 // 16 * 16
    return [(0, first), (first, channels - first)]


def norm_factor(side_sum, features):
    mean = jnp.sum(side_sum, axis=0, keepdims=True) * (1.0 / features)
    return lax.rsqrt(mean + epsilon)


def gate(projected, taps_ref, begin, write):
    count = taps_ref.shape[1]
    columns = [tap_columns(taps_ref[stream]) for stream in (1, 2)]
    rows = projected[0].shape[0]
    tile = math.gcd(rows, 64)
    for start in range(0, rows, tile):
        here = slice(start, start + tile)
        there = slice(begin + start, begin + start + tile)
        key, value = (
            smooth(wide[here].astype(f32), column[there], count, None)
            for wide, column in zip(projected, columns)
        )
        write(here, key, value)


def message_finish(features, w_short, tokens, part):
    streams, count, channels = w_short.shape
    parts = channel_parts(channels)
    begin, rows = parts[part]
    last = slice(tokens - block_len, tokens)

    def body(total, side_sum, extra_refs, outs):
        (taps_ref,), (message_ref,) = extra_refs, outs
        factor = norm_factor(side_sum, features)
        projected = [(total(stream) * factor).astype(bf16) for stream in (1, 2)]

        def write(here, key, value):
            message_ref[here] = (key * value).astype(bf16)

        gate(projected, taps_ref, begin, write)
        if part == 0:
            lines = []
            for stream in range(streams):
                end = (total(stream, last, slice(0, channels)) * factor[:, last]).astype(bf16)
                lines.append(end.astype(f32).T[block_len - count + 1 :])
            lines.append(jnp.zeros((side_rows - streams * (count - 1), channels), f32))
            message_ref[rows:] = jnp.zeros((side_rows, tokens), bf16)
            message_ref[rows:, :channels] = jnp.concatenate(lines, axis=0).astype(bf16)

    out_shape = [shape_of((rows + (side_rows if part == 0 else 0), tokens), bf16)]
    return body, [w_short], out_shape, parts[part], True


def projection_finish(features, w_short, tokens, part):
    streams, _, channels = w_short.shape
    parts = channel_parts(channels)
    begin, rows = parts[part]

    def body(total, side_sum, extra_refs, outs):
        (taps_ref,), (projected_ref, first_ref, gated_ref) = extra_refs, outs
        factor = norm_factor(side_sum, features)
        projected = [(total(stream) * factor).astype(bf16) for stream in range(streams)]
        for stream in range(streams):
            projected_ref[stream] = projected[stream]

        def write(here, key, value):
            first_ref[0, here] = key[:, :block_len]
            first_ref[1, here] = value[:, :block_len]
            gated_ref[here] = (key * value).astype(bf16)

        gate(projected[1:], taps_ref, begin, write)

    out_shape = [
        shape_of((streams, rows, tokens), bf16),
        shape_of((2, rows, block_len), f32),
        shape_of((rows, tokens), bf16),
    ]
    return body, [w_short], out_shape, parts[part], False


def halo_columns(message_ref, streams, count, channels, inside):
    side = message_ref[message_ref.shape[0] - side_rows :, :channels].astype(f32)
    side = jnp.where(inside, side, 0.0).T
    return [side[:, s * (count - 1) : (s + 1) * (count - 1)] for s in range(streams)]


def halo_edges(message_ref, taps, begin):
    streams, count, rows = taps.shape
    side = message_ref[message_ref.shape[0] - side_rows :, begin : begin + rows].astype(f32)
    lines = []
    for s in range(streams):
        for token in range(count - 1):
            line = jnp.zeros((1, rows), f32)
            for tap in range(token + 1, count):
                at = s * (count - 1) + count - 1 + token - tap
                line = line + taps[s, tap : tap + 1] * side[at : at + 1]
            lines.append(line)
    lines.append(jnp.zeros((-len(lines) % 8, rows), f32))
    columns = jnp.concatenate(lines, axis=0).T
    lane = lax.broadcasted_iota(jnp.int32, (rows, block_len), 1)
    edges = []
    for s in range(streams):
        edge = jnp.zeros((rows, block_len), f32)
        for token in range(count - 1):
            at = s * (count - 1) + token
            edge = jnp.where(lane == token, columns[:, at : at + 1], edge)
        edges.append(edge)
    return edges


def split_table(table):
    high = table.astype(bf16)
    return high, (table - high.astype(np.float64)).astype(bf16)


def dft_tables():
    size = 2 * block_len
    freq = np.arange(block_len) + 0.5
    angle = 2.0 * math.pi / size * np.arange(size)[:, None] * freq[None, :]
    high, low = split_table(np.concatenate([np.cos(angle), -np.sin(angle)], axis=1))
    block = np.concatenate([high[:block_len], low[:block_len]])
    segment = np.concatenate([high, low])
    back = angle[block_len:].T
    inverse = np.concatenate([np.cos(back), -np.sin(back)], axis=0) * (2.0 / size)
    high, low = split_table(inverse)
    return block, segment, np.concatenate([high, low], axis=1)


def spectrum_lanes(k):
    return slice(2 * k * block_len, 2 * (k + 1) * block_len)


def block_lanes(k):
    return slice(k * block_len, (k + 1) * block_len)


def filter_spectra(long_filter, table):
    channels, lags = long_filter.shape

    def kernel(filter_ref, table_ref, spectra_ref):
        before = jnp.zeros((channels, block_len), bf16)
        for k in range(lags // block_len):
            now = filter_ref[:, block_lanes(k)]
            segment = jnp.concatenate([before, now, before, now], axis=1)
            spectra_ref[:, spectrum_lanes(k)] = dot(segment, table_ref[...])
            before = now

    return pl.pallas_call(
        kernel,
        in_specs=[in_vmem, in_vmem],
        out_specs=in_vmem,
        out_shape=shape_of((channels, 2 * lags), f32),
        compiler_params=params,
        cost_estimate=estimate(6e9, 0),
        name="filter_spectra",
    )(long_filter, table)


def block_spectra(pieces, table_ref, spec_ref, first):
    rows = pieces[0].shape[0]
    stacked = jnp.concatenate(pieces, axis=0)
    spectra = dot(jnp.concatenate([stacked, stacked], axis=1), table_ref[...])
    for k in range(len(pieces)):
        spec_ref[:rows, spectrum_lanes(first + k)] = spectra[k * rows : (k + 1) * rows]


def multiply_spectra(source_ref, filters_ref, filter_start, pairs, before_ref, total_ref):
    used = [term for terms in pairs for term in terms]
    for start in range(0, total_ref.shape[0], 8):
        here = slice(start, start + 8)
        there = slice(filter_start + start, filter_start + start + 8)

        def parts(ref, rows, k):
            return ref[rows, block_lanes(2 * k)], ref[rows, block_lanes(2 * k + 1)]

        sources = {b: parts(source_ref, here, b) for b in sorted({b for b, _ in used})}
        filters = {d: parts(filters_ref, there, d) for d in sorted({d for _, d in used})}
        for a, terms in enumerate(pairs):
            real = imag = None
            if before_ref is not None:
                real, imag = parts(before_ref, here, a)
            for b, d in terms:
                gr, gi = sources[b]
                hr, hi = filters[d]
                more_real, more_imag = gr * hr - gi * hi, gr * hi + gi * hr
                real = more_real if real is None else real + more_real
                imag = more_imag if imag is None else imag + more_imag
            if real is None:
                real = imag = jnp.zeros((8, block_len), f32)
            total_ref[here, block_lanes(2 * a)] = real
            total_ref[here, block_lanes(2 * a + 1)] = imag


def own_part(projected, alone, moved, taps, filters, table):
    streams, _, tokens = projected[0].shape
    parts = channel_parts(taps.shape[2])
    number = len(parts)
    count = taps.shape[1]
    blocks = tokens // block_len
    first = 0 if moved else 1
    pairs = [[(b, a - b) for b in range(first, a + 1)] for a in range(blocks)]

    def kernel(*refs):
        refs = list(refs)
        take = lambda n: take_from(refs, n)
        projected_refs, message_refs = take(number), take(number)
        taps_ref, filters_ref, table_ref = take(3)
        query_refs, total_refs = take(number), take(number)
        gated_refs = take(number) if moved else None
        (spec_ref,) = refs
        columns = [tap_columns(taps_ref[s]) for s in range(streams)]
        if moved:
            inside = lax.axis_index("ctx") > 0
            halo = halo_columns(message_refs[0], streams, count, taps_ref.shape[2], inside)
        for part, (begin, rows) in enumerate(parts):
            tile = math.gcd(rows, 64)
            for start in range(0, rows, tile):
                here = slice(start, start + tile)
                there = slice(begin + start, begin + start + tile)
                projected_ref = projected_refs[part]

                def smoothed(s):
                    edge = halo[s][there] if moved else None
                    wide = projected_ref[s, here].astype(f32)
                    return smooth(wide, columns[s][there], count, edge)

                query_refs[part][here] = smoothed(0)
                if moved:
                    gated_refs[part][here] = (smoothed(1) * smoothed(2)).astype(bf16)
            source_ref = gated_refs[part] if moved else message_refs[part]
            pieces = [source_ref[:rows, block_lanes(b)] for b in range(first, blocks)]
            block_spectra(pieces, table_ref, spec_ref, first)
            multiply_spectra(spec_ref, filters_ref, begin, pairs, None, total_refs[part])

    out_shape = [shape_of((rows, tokens), f32) for _, rows in parts]
    out_shape += [shape_of((rows, 2 * tokens), f32) for _, rows in parts]
    if moved:
        out_shape += [shape_of((rows, tokens), bf16) for _, rows in parts]
    inputs = [*projected, *(moved or alone), taps, filters, table]
    outs = pl.pallas_call(
        kernel,
        in_specs=[in_vmem] * len(inputs),
        out_specs=[in_vmem] * len(out_shape),
        out_shape=out_shape,
        scratch_shapes=[pltpu.VMEM((max(rows for _, rows in parts), 2 * tokens), f32)],
        compiler_params=params,
        cost_estimate=estimate(0, 0),
        name="own_part",
    )(*inputs)
    gated = list(outs[2 * number :]) if moved else alone
    return list(outs[:number]), list(outs[number : 2 * number]), gated


def far_part(turn, begin, moved, total, filters, table, last, own):
    rows, tokens = total.shape[0], moved.shape[1]
    blocks = tokens // block_len
    far_pairs = [[(b, turn * blocks + a - b) for b in range(blocks)] for a in range(blocks)]
    channels_here = slice(begin, begin + rows)

    def kernel(*refs):
        refs = list(refs)
        take = lambda n: take_from(refs, n)
        moved_ref, total_ref, filters_ref, table_ref = take(4)
        own_refs = take(3) if own else None
        spec_ref = refs.pop()
        sum_ref = refs.pop()
        if last:
            last_refs = take(4)
            (out_ref,) = refs

        def work(inside):
            pieces = [moved_ref[:rows, block_lanes(b)] for b in range(blocks)] if inside else []
            pairs = far_pairs if inside else [[] for _ in range(blocks)]
            if last:
                back_ref, query_ref, gated_ref, skip_ref = last_refs
                query, gated = (
                    [ref[:rows, block_lanes(a)] for a in range(blocks)]
                    for ref in (query_ref, gated_ref)
                )
            if own:
                first_ref, taps_ref, halo_ref = own_refs
                key, value = first_ref[0], first_ref[1]
                if inside:
                    edges = halo_edges(halo_ref, taps_ref[:, :, channels_here], begin)
                    query[0] = query[0] + edges[0]
                    key, value = key + edges[1], value + edges[2]
                gated[0] = (key * value).astype(bf16)
                pairs = [terms + [(len(pieces), a)] for a, terms in enumerate(pairs)]
                pieces.append(gated[0])
            if pieces:
                block_spectra(pieces, table_ref, spec_ref, 0)
            multiply_spectra(spec_ref, filters_ref, begin, pairs, total_ref, sum_ref)
            if not last:
                return
            skip = column(skip_ref[...])[channels_here]
            spectra = [sum_ref[:, spectrum_lanes(a)] for a in range(blocks)]
            highs = [spectrum.astype(bf16) for spectrum in spectra]
            lows = [(s - high.astype(f32)).astype(bf16) for s, high in zip(spectra, highs)]
            both = dot(jnp.concatenate(highs, axis=0), back_ref[...])
            small = dot(jnp.concatenate(lows, axis=0), back_ref[:, :block_len])
            filtered = both[:, :block_len] + (both[:, block_len:] + small)
            for a in range(blocks):
                here = filtered[a * rows : (a + 1) * rows]
                mixed = query[a] * (here + skip * gated[a].astype(f32))
                out_ref[:, block_lanes(a)] = mixed.astype(bf16)

        inside = lax.axis_index("ctx") >= turn
        pl.when(inside)(lambda: work(True))
        pl.when(jnp.logical_not(inside))(lambda: work(False))

    args = [moved, total, filters, table]
    if own:
        args += list(own)
    scratch = [pltpu.VMEM((rows, 2 * (blocks + 1) * block_len), f32)]
    out_shape = shape_of((rows, 2 * tokens), f32)
    if last is not None:
        inverse, query, gated, skip = last
        args += [inverse, query, gated, skip.reshape(1, -1)]
        out_shape = shape_of((rows, tokens), bf16)
        scratch.append(pltpu.VMEM((rows, 2 * tokens), f32))
    return pl.pallas_call(
        kernel,
        in_specs=[in_vmem] * len(args),
        out_specs=in_vmem,
        out_shape=out_shape,
        scratch_shapes=scratch[::-1],
        compiler_params=params,
        cost_estimate=estimate(0, 0),
        name=f"far_part_{turn}_{begin}",
    )(*args)


def from_before(block):
    count = lax.axis_size("ctx")
    return lax.ppermute(block, "ctx", [(i, (i + 1) % count) for i in range(count)])


def output_finish(channels, tokens):
    def body(total, side_sum, extra_refs, outs):
        outs[0][...] = total(0).astype(bf16)

    return body, [], [shape_of((channels, tokens), bf16)], None, False


def shards(activations, norm_gain, w_in, w_short, long_filter, skip_gain, w_out):
    channels, tokens = activations.shape
    features = w_in.shape[2]
    w_short = w_short.transpose(0, 2, 1)
    turns = lax.axis_size("ctx")
    parts = channel_parts(channels)
    forward, segments, inverse = (jnp.asarray(t) for t in dft_tables())
    own = prepare(activations, norm_gain)

    filters = filter_spectra(long_filter, segments)
    last, running, (filters,) = gather_products([own], w_in, [filters], True, "projection")

    def message(part, running):
        (sent,) = last(message_finish(features, w_short, tokens, part), running)
        return from_before(sent)

    exact = turns > 2
    moving = [message(0, running)]
    results = [last(projection_finish(features, w_short, tokens, k), running) for k in range(2)]
    projected, first_blocks, gated = zip(*results)
    later, gated = lax.optimization_barrier((running, gated))
    moving.append(message(1, later))
    query, totals, gated = own_part(
        projected, gated, moving if exact else None, w_short, filters, forward
    )
    if exact:
        moving = [from_before(part) for part in gated]
    mixed = []
    for turn in range(1, turns):
        for k, (begin, _) in enumerate(parts):
            last = own_block = None
            if turn == turns - 1:
                last = (inverse, query[k], gated[k], skip_gain)
                if not exact:
                    own_block = (first_blocks[k], w_short, moving[0])
            done = far_part(
                turn, begin, moving[k], totals[k], filters, forward, last, own_block
            )
            if last is None:
                totals[k] = done
                moving[k] = from_before(moving[k])
            else:
                mixed.append(done)

    last, running, _ = gather_products(mixed, w_out[None], [], False, "output")
    (result,) = last(output_finish(channels, tokens), running)
    return result


def solution(mesh):
    placed = (
        P("fsdp", "ctx"),
        P("fsdp"),
        P(None, "fsdp", None),
        P(None, "fsdp", None),
        P("fsdp", None),
        P("fsdp"),
        P("fsdp", None),
    )
    return jax.shard_map(
        shards, mesh=mesh, in_specs=placed, out_specs=P("fsdp", "ctx"), check_vma=False
    )
```

```python
import math

import jax
import jax.numpy as jnp
import numpy as np
from jax import lax
from jax.experimental import pallas as pl
from jax.experimental.pallas import tpu as pltpu
from jax.sharding import PartitionSpec as P

epsilon = 1e-05
block_len = 128
STAGGER = 2e9
side_rows = 8
bf16 = jnp.bfloat16
f32 = jnp.float32
in_vmem = pl.BlockSpec(memory_space=pltpu.VMEM)
params = pltpu.CompilerParams(vmem_limit_bytes=12 * 2**20)


def shape_of(shape, dtype):
    return jax.ShapeDtypeStruct(tuple(shape), dtype)


def dot(left, right):
    return jnp.dot(left, right, preferred_element_type=f32)


def column(row):
    return jnp.broadcast_to(row, (8, row.shape[1])).T[:, :1]


def tap_columns(taps):
    return jnp.concatenate([taps, jnp.zeros((8 - taps.shape[0], taps.shape[1]), f32)], axis=0).T


def estimate(flops, size):
    return pl.CostEstimate(flops=int(flops), bytes_accessed=int(size), transcendentals=0)


def begin():
    def kernel(out_ref):
        out_ref[...] = jnp.zeros(out_ref.shape, f32)

    return pl.pallas_call(
        kernel,
        out_specs=in_vmem,
        out_shape=shape_of((8, 128), f32),
        compiler_params=params,
        cost_estimate=estimate(3e9, 0),
        name="begin",
    )()


def prepare_kernel(x_ref, gain_ref, begun_ref, out_ref):
    rows = x_ref.shape[0]
    wide = x_ref[...].astype(f32)
    out_ref[:rows] = (wide * column(gain_ref[...])).astype(bf16)
    squares = jnp.sum(wide * wide, axis=0, keepdims=True)
    high = squares.astype(bf16).astype(f32)
    row = lax.broadcasted_iota(jnp.int32, (side_rows, wide.shape[1]), 0)
    side = jnp.where(row == 0, high, jnp.where(row == 1, squares - high, 0.0))
    out_ref[rows:] = side.astype(bf16)


def prepare(x, gain):
    rows, tokens = x.shape
    return pl.pallas_call(
        prepare_kernel,
        in_specs=[in_vmem, in_vmem, in_vmem],
        out_specs=in_vmem,
        out_shape=shape_of((rows + side_rows, tokens), bf16),
        compiler_params=params,
        cost_estimate=estimate(3e9, 0),
        name="prepare",
    )(x, gain.reshape(1, rows), begin())


def chip_count():
    return lax.axis_size("fsdp") // 2


def ring_order(count):
    return list(range(0, count, 2)) + list(range(1, count, 2))[::-1]


def along_ring(block):
    chips = chip_count()
    order = ring_order(chips)
    pairs = []
    for i in range(chips):
        here, after = order[i], order[(i + 1) % chips]
        pairs += [(2 * here, 2 * after), (2 * after + 1, 2 * here + 1)]
    return lax.ppermute(block, "fsdp", pairs)


def other_core(block):
    return lax.ppermute(block, "fsdp", [(i, i ^ 1) for i in range(2 * chip_count())])


def my_core():
    return lax.axis_index("fsdp") & 1


def source_chip(steps):
    chips = chip_count()
    chip = lax.shift_right_logical(lax.axis_index("fsdp"), 1)
    half = lax.shift_right_logical(chip, 1)
    place = jnp.where(chip & 1 == 0, half, chips - 1 - half)
    place = place + jnp.where(my_core() == 0, chips - steps, steps)
    place = jnp.where(place >= chips, place - chips, place)
    return jnp.where(place < (chips + 1) // 2, 2 * place, 2 * (chips - 1 - place) + 1)


def take_from(refs, number):
    return [refs.pop(0) for _ in range(number)]


def products(items, weight, running, side, finish, cost, name):
    body, extras, out_shape, cut, senders_only = finish or (None, [], None, None, False)
    streams, out_rows, features = weight.shape
    cut = cut or (0, out_rows)
    out_here, out_rows = slice(cut[0], cut[0] + cut[1]), cut[1]
    rows = features // lax.axis_size("fsdp")
    shards = [piece for _, _, pieces in items for piece in pieces]
    tokens = shards[0].shape[1]
    count = len(shards)
    first_group = running is None
    state = [] if first_group else list(running)
    padded = rows % 128 != 0
    width = 2 * rows if padded else rows
    scratch_shapes = [pltpu.VMEM((len(items) * width, tokens), bf16)] if padded else []

    def kernel(*refs):
        refs = list(refs)
        take = lambda n: take_from(refs, n)
        shard_refs = take(count)
        (weight_ref,) = take(1)
        state_refs = take(len(state))
        extra_refs = take(len(extras))
        outs = take(len(out_shape))

        def work():
            core = my_core()
            chip_of = {steps: source_chip(steps) for steps in sorted({item[0] for item in items})}
            if padded:
                (beside_ref,) = refs
                beside_ref[...] = jnp.zeros(beside_ref.shape, bf16)
            sides, right = [], []
            pieces_left = list(shard_refs)
            for k, (_, other, pieces) in enumerate(items):
                done = 0
                for piece_ref in take_from(pieces_left, len(pieces)):
                    more = min(piece_ref.shape[0], rows - done)
                    if padded:
                        at = k * width + jnp.where(core == other, 0, rows) + done
                        at = pl.multiple_of(at, math.gcd(rows, done or rows))
                        beside_ref[pl.ds(at, more)] = piece_ref[:more]
                    else:
                        right.append(piece_ref[:more])
                    if more < piece_ref.shape[0]:
                        sides.append(piece_ref[more:].astype(f32))
                    done += more
            right = beside_ref[...] if padded else jnp.concatenate(right, axis=0)
            side_sum = None
            if side:
                parts = sides + ([] if first_group else [state_refs[1][...]])
                side_sum = sum(parts[1:], parts[0])

            def total(stream, lanes=slice(None), out_here=out_here):
                left = []
                for steps, other, _ in items:
                    block = chip_of[steps]
                    if not padded:
                        block = 2 * block + (1 - core if other else core)
                    at = pl.ds(pl.multiple_of(block * width, width), width)
                    left.append(weight_ref[stream, out_here, at])
                product = dot(jnp.concatenate(left, axis=1), right[:, lanes])
                if first_group:
                    return product
                return state_refs[0][stream, out_here, lanes] + product

            if body is not None:
                body(total, side_sum, extra_refs, outs)
                return
            for stream in range(streams):
                outs[0][stream] = total(stream)
            if side:
                outs[1][...] = side_sum

        if senders_only:
            pl.when(lax.axis_index("ctx") < lax.axis_size("ctx") - 1)(work)
        else:
            work()

    aliases = {}
    if body is None:
        out_shape = [shape_of((streams, out_rows, tokens), f32)]
        if side:
            out_shape.append(shape_of((side_rows, tokens), f32))
        if not first_group:
            aliases = {count + 1 + i: i for i in range(len(state))}
    return pl.pallas_call(
        kernel,
        in_specs=[in_vmem] * (count + 1 + len(state) + len(extras)),
        out_specs=[in_vmem] * len(out_shape),
        out_shape=out_shape,
        scratch_shapes=scratch_shapes,
        input_output_aliases=aliases,
        compiler_params=params,
        cost_estimate=estimate(cost, 0),
        name=name,
    )(*shards, weight, *state, *extras)


def pass_on(near, far):
    rows = near.shape[0] - side_rows

    def kernel(near_ref, far_ref, out_ref):
        out_ref[:rows] = near_ref[:rows]
        below = pltpu.roll(far_ref[rows:].astype(f32), 2, 0)
        out_ref[rows:] = (near_ref[rows:].astype(f32) + below).astype(bf16)

    return pl.pallas_call(
        kernel,
        in_specs=[in_vmem, in_vmem],
        out_specs=in_vmem,
        out_shape=shape_of(near.shape, bf16),
        compiler_params=params,
        cost_estimate=estimate(0, 0),
        name="pass_on",
    )(near, far)


def gather_products(own, weight, beside, side, name):
    chips = chip_count()
    last_step = chips // 2

    def send(way, pieces, scope):
        sent = []
        for k, piece in enumerate(pieces):
            with jax.named_scope(f"{name}_{scope}_{k}"):
                sent.append(way(piece))
        return sent

    def joined(pieces):
        return [jnp.concatenate(pieces, axis=0)] if len(pieces) > 1 else pieces

    near, far = own, send(other_core, own, "core_own")
    items = [(0, 0, near), (0, 1, far)]
    sibling = far
    if side:
        far = [far[0][: far[0].shape[0] - side_rows]]
    running = None
    for step in range(1, last_step + 1):
        near = joined(send(along_ring, near, f"near_{step}"))
        arrived = near
        if running is not None:
            arrived, running = lax.optimization_barrier((near, running))
        elif beside:
            arrived, beside = lax.optimization_barrier((near, beside))
        theirs = send(other_core, arrived, f"core_near_{step}")
        pair = [(step, 0, arrived), (chips - step, 1, theirs)]
        if step < last_step:
            running = products(items + pair, weight, running, side, None, 0, f"{name}_{step}")
            if side and step == 1:
                near = [pass_on(near[0], sibling[0])]
            far = joined(send(along_ring, far, f"far_{step}"))
            theirs = send(other_core, far, f"core_far_{step}")
            items = [(step, 1, far), (chips - step, 0, theirs)]
        else:
            items.append(pair[0])
            running = products(items, weight, running, side, None, STAGGER, f"{name}_{step}")
            items = pair[1:]

    def last(finish, running):
        return products(items, weight, running, side, finish, 0, f"{name}_last")

    return last, running, beside


def smooth(projected, taps, count, halo):
    lane = lax.broadcasted_iota(jnp.int32, projected.shape, 1)
    out = taps[:, :1] * projected
    for tap in range(1, count):
        moved = pltpu.roll(projected, tap, 1)
        for place in range(tap):
            edge = 0.0
            if halo is not None:
                at = halo.shape[1] - tap + place
                edge = halo[:, at : at + 1]
            moved = jnp.where(lane == place, edge, moved)
        out = out + taps[:, tap : tap + 1] * moved
    return out


def channel_parts(channels):
    first = channels * 4 // 8 // 16 * 16
    return [(0, first), (first, channels - first)]


def norm_factor(side_sum, features):
    mean = jnp.sum(side_sum, axis=0, keepdims=True) * (1.0 / features)
    return lax.rsqrt(mean + epsilon)


def gate(projected, taps_ref, begin, write):
    count = taps_ref.shape[1]
    columns = [tap_columns(taps_ref[stream]) for stream in (1, 2)]
    rows = projected[0].shape[0]
    tile = math.gcd(rows, 64)
    for start in range(0, rows, tile):
        here = slice(start, start + tile)
        there = slice(begin + start, begin + start + tile)
        key, value = (
            smooth(wide[here].astype(f32), column[there], count, None)
            for wide, column in zip(projected, columns)
        )
        write(here, key, value)


def message_finish(features, w_short, tokens, part):
    streams, count, channels = w_short.shape
    parts = channel_parts(channels)
    begin, rows = parts[part]
    last = slice(tokens - block_len, tokens)

    def body(total, side_sum, extra_refs, outs):
        (taps_ref,), (message_ref,) = extra_refs, outs
        factor = norm_factor(side_sum, features)
        projected = [(total(stream) * factor).astype(bf16) for stream in (1, 2)]

        def write(here, key, value):
            message_ref[here] = (key * value).astype(bf16)

        gate(projected, taps_ref, begin, write)
        if part == 0:
            lines = []
            for stream in range(streams):
                end = (total(stream, last, slice(0, channels)) * factor[:, last]).astype(bf16)
                lines.append(end.astype(f32).T[block_len - count + 1 :])
            lines.append(jnp.zeros((side_rows - streams * (count - 1), channels), f32))
            message_ref[rows:] = jnp.zeros((side_rows, tokens), bf16)
            message_ref[rows:, :channels] = jnp.concatenate(lines, axis=0).astype(bf16)

    out_shape = [shape_of((rows + (side_rows if part == 0 else 0), tokens), bf16)]
    return body, [w_short], out_shape, parts[part], True


def projection_finish(features, w_short, tokens, part):
    streams, _, channels = w_short.shape
    parts = channel_parts(channels)
    begin, rows = parts[part]

    def body(total, side_sum, extra_refs, outs):
        (taps_ref,), (projected_ref, first_ref, gated_ref) = extra_refs, outs
        factor = norm_factor(side_sum, features)
        projected = [(total(stream) * factor).astype(bf16) for stream in range(streams)]
        for stream in range(streams):
            projected_ref[stream] = projected[stream]

        def write(here, key, value):
            first_ref[0, here] = key[:, :block_len]
            first_ref[1, here] = value[:, :block_len]
            gated_ref[here] = (key * value).astype(bf16)

        gate(projected[1:], taps_ref, begin, write)

    out_shape = [
        shape_of((streams, rows, tokens), bf16),
        shape_of((2, rows, block_len), f32),
        shape_of((rows, tokens), bf16),
    ]
    return body, [w_short], out_shape, parts[part], False


def halo_columns(message_ref, streams, count, channels, inside):
    side = message_ref[message_ref.shape[0] - side_rows :, :channels].astype(f32)
    side = jnp.where(inside, side, 0.0).T
    return [side[:, s * (count - 1) : (s + 1) * (count - 1)] for s in range(streams)]


def halo_edges(message_ref, taps, begin):
    streams, count, rows = taps.shape
    side = message_ref[message_ref.shape[0] - side_rows :, begin : begin + rows].astype(f32)
    lines = []
    for s in range(streams):
        for token in range(count - 1):
            line = jnp.zeros((1, rows), f32)
            for tap in range(token + 1, count):
                at = s * (count - 1) + count - 1 + token - tap
                line = line + taps[s, tap : tap + 1] * side[at : at + 1]
            lines.append(line)
    lines.append(jnp.zeros((-len(lines) % 8, rows), f32))
    columns = jnp.concatenate(lines, axis=0).T
    lane = lax.broadcasted_iota(jnp.int32, (rows, block_len), 1)
    edges = []
    for s in range(streams):
        edge = jnp.zeros((rows, block_len), f32)
        for token in range(count - 1):
            at = s * (count - 1) + token
            edge = jnp.where(lane == token, columns[:, at : at + 1], edge)
        edges.append(edge)
    return edges


def split_table(table):
    high = table.astype(bf16)
    return high, (table - high.astype(np.float64)).astype(bf16)


def dft_tables():
    size = 2 * block_len
    freq = np.arange(block_len) + 0.5
    angle = 2.0 * math.pi / size * np.arange(size)[:, None] * freq[None, :]
    high, low = split_table(np.concatenate([np.cos(angle), -np.sin(angle)], axis=1))
    block = np.concatenate([high[:block_len], low[:block_len]])
    segment = np.concatenate([high, low])
    back = angle[block_len:].T
    inverse = np.concatenate([np.cos(back), -np.sin(back)], axis=0) * (2.0 / size)
    high, low = split_table(inverse)
    return block, segment, np.concatenate([high, low], axis=1)


def spectrum_lanes(k):
    return slice(2 * k * block_len, 2 * (k + 1) * block_len)


def block_lanes(k):
    return slice(k * block_len, (k + 1) * block_len)


def filter_spectra(long_filter, table):
    channels, lags = long_filter.shape

    def kernel(filter_ref, table_ref, spectra_ref):
        before = jnp.zeros((channels, block_len), bf16)
        for k in range(lags // block_len):
            now = filter_ref[:, block_lanes(k)]
            segment = jnp.concatenate([before, now, before, now], axis=1)
            spectra_ref[:, spectrum_lanes(k)] = dot(segment, table_ref[...])
            before = now

    return pl.pallas_call(
        kernel,
        in_specs=[in_vmem, in_vmem],
        out_specs=in_vmem,
        out_shape=shape_of((channels, 2 * lags), f32),
        compiler_params=params,
        cost_estimate=estimate(6e9, 0),
        name="filter_spectra",
    )(long_filter, table)


def block_spectra(pieces, table_ref, spec_ref, first):
    rows = pieces[0].shape[0]
    stacked = jnp.concatenate(pieces, axis=0)
    spectra = dot(jnp.concatenate([stacked, stacked], axis=1), table_ref[...])
    for k in range(len(pieces)):
        spec_ref[:rows, spectrum_lanes(first + k)] = spectra[k * rows : (k + 1) * rows]


def multiply_spectra(source_ref, filters_ref, filter_start, pairs, before_ref, total_ref):
    used = [term for terms in pairs for term in terms]
    for start in range(0, total_ref.shape[0], 8):
        here = slice(start, start + 8)
        there = slice(filter_start + start, filter_start + start + 8)

        def parts(ref, rows, k):
            return ref[rows, block_lanes(2 * k)], ref[rows, block_lanes(2 * k + 1)]

        sources = {b: parts(source_ref, here, b) for b in sorted({b for b, _ in used})}
        filters = {d: parts(filters_ref, there, d) for d in sorted({d for _, d in used})}
        for a, terms in enumerate(pairs):
            real = imag = None
            if before_ref is not None:
                real, imag = parts(before_ref, here, a)
            for b, d in terms:
                gr, gi = sources[b]
                hr, hi = filters[d]
                more_real, more_imag = gr * hr - gi * hi, gr * hi + gi * hr
                real = more_real if real is None else real + more_real
                imag = more_imag if imag is None else imag + more_imag
            if real is None:
                real = imag = jnp.zeros((8, block_len), f32)
            total_ref[here, block_lanes(2 * a)] = real
            total_ref[here, block_lanes(2 * a + 1)] = imag


def mix(sum_ref, back_ref, query, gated, skip, out_ref):
    rows = out_ref.shape[0]
    spectra = [sum_ref[:, spectrum_lanes(a)] for a in range(len(query))]
    highs = [spectrum.astype(bf16) for spectrum in spectra]
    lows = [(s - high.astype(f32)).astype(bf16) for s, high in zip(spectra, highs)]
    both = dot(jnp.concatenate(highs, axis=0), back_ref[...])
    small = dot(jnp.concatenate(lows, axis=0), back_ref[:, :block_len])
    filtered = both[:, :block_len] + (both[:, block_len:] + small)
    for a in range(len(query)):
        here = filtered[a * rows : (a + 1) * rows]
        mixed = query[a] * (here + skip * gated[a].astype(f32))
        out_ref[:, block_lanes(a)] = mixed.astype(bf16)


def own_part(projected, alone, moved, taps, filters, table, inverse, skip):
    streams, _, tokens = projected[0].shape
    parts = channel_parts(taps.shape[2])
    number = len(parts)
    count = taps.shape[1]
    blocks = tokens // block_len
    first = 0 if moved else 1
    pairs = [[(b, a - b) for b in range(first, a + 1)] for a in range(blocks)]

    def kernel(*refs):
        refs = list(refs)
        take = lambda n: take_from(refs, n)
        projected_refs, message_refs = take(number), take(number)
        taps_ref, filters_ref, table_ref, back_ref, skip_ref = take(5)
        query_refs, total_refs = take(number), take(number)
        gated_refs = take(number)
        (spec_ref,) = refs
        columns = [tap_columns(taps_ref[s]) for s in range(streams)]
        if moved:
            inside = lax.axis_index("ctx") > 0
            halo = halo_columns(message_refs[0], streams, count, taps_ref.shape[2], inside)
        for part, (begin, rows) in enumerate(parts):
            tile = math.gcd(rows, 64)
            for start in range(0, rows, tile):
                here = slice(start, start + tile)
                there = slice(begin + start, begin + start + tile)
                projected_ref = projected_refs[part]

                def smoothed(s):
                    edge = halo[s][there] if moved else None
                    wide = projected_ref[s, here].astype(f32)
                    return smooth(wide, columns[s][there], count, edge)

                query_refs[part][here] = smoothed(0)
                if moved:
                    gated_refs[part][here] = (smoothed(1) * smoothed(2)).astype(bf16)
            source_ref = gated_refs[part] if moved else message_refs[part]
            pieces = [source_ref[:rows, block_lanes(b)] for b in range(first, blocks)]
            block_spectra(pieces, table_ref, spec_ref, first)
            multiply_spectra(spec_ref, filters_ref, begin, pairs, None, total_refs[part])
            if not moved:

                @pl.when(lax.axis_index("ctx") == 0)
                def _():
                    lanes = [block_lanes(a) for a in range(blocks)]
                    block_spectra([source_ref[:rows, lanes[0]]], table_ref, spec_ref, 0)
                    sum_ref = total_refs[part]
                    first_pairs = [[(0, a)] for a in range(blocks)]
                    multiply_spectra(spec_ref, filters_ref, begin, first_pairs, sum_ref, sum_ref)
                    query = [query_refs[part][:, at] for at in lanes]
                    gated = [source_ref[:rows, at] for at in lanes]
                    column_here = column(skip_ref[...])[begin : begin + rows]
                    mix(sum_ref, back_ref, query, gated, column_here, gated_refs[part])

    out_shape = [shape_of((rows, tokens), f32) for _, rows in parts]
    out_shape += [shape_of((rows, 2 * tokens), f32) for _, rows in parts]
    out_shape += [shape_of((rows, tokens), bf16) for _, rows in parts]
    inputs = [*projected, *(moved or alone), taps, filters, table, inverse, skip.reshape(1, -1)]
    outs = pl.pallas_call(
        kernel,
        in_specs=[in_vmem] * len(inputs),
        out_specs=[in_vmem] * len(out_shape),
        out_shape=out_shape,
        scratch_shapes=[pltpu.VMEM((max(rows for _, rows in parts), 2 * tokens), f32)],
        compiler_params=params,
        cost_estimate=estimate(0, 0),
        name="own_part",
    )(*inputs)
    gated = list(outs[2 * number :])
    return list(outs[:number]), list(outs[number : 2 * number]), gated


def far_part(turn, begin, moved, total, filters, table, last, own):
    rows, tokens = total.shape[0], moved.shape[1]
    blocks = tokens // block_len
    far_pairs = [[(b, turn * blocks + a - b) for b in range(blocks)] for a in range(blocks)]
    channels_here = slice(begin, begin + rows)

    def kernel(*refs):
        refs = list(refs)
        take = lambda n: take_from(refs, n)
        moved_ref, total_ref, filters_ref, table_ref = take(4)
        own_refs = take(4) if own else None
        spec_ref = refs.pop()
        sum_ref = refs.pop()
        if last:
            last_refs = take(4)
            (out_ref,) = refs

        def work(inside):
            pieces = [moved_ref[:rows, block_lanes(b)] for b in range(blocks)] if inside else []
            pairs = far_pairs if inside else [[] for _ in range(blocks)]
            if last:
                back_ref, query_ref, gated_ref, skip_ref = last_refs
                query, gated = (
                    [ref[:rows, block_lanes(a)] for a in range(blocks)]
                    for ref in (query_ref, gated_ref)
                )
            if own:
                first_ref, taps_ref, halo_ref, ready_ref = own_refs
                if not inside:
                    out_ref[...] = ready_ref[...]
                    return
                key, value = first_ref[0], first_ref[1]
                if inside:
                    edges = halo_edges(halo_ref, taps_ref[:, :, channels_here], begin)
                    query[0] = query[0] + edges[0]
                    key, value = key + edges[1], value + edges[2]
                gated[0] = (key * value).astype(bf16)
                pairs = [terms + [(len(pieces), a)] for a, terms in enumerate(pairs)]
                pieces.append(gated[0])
            if pieces:
                block_spectra(pieces, table_ref, spec_ref, 0)
            multiply_spectra(spec_ref, filters_ref, begin, pairs, total_ref, sum_ref)
            if not last:
                return
            mix(sum_ref, back_ref, query, gated, column(skip_ref[...])[channels_here], out_ref)

        inside = lax.axis_index("ctx") >= turn
        pl.when(inside)(lambda: work(True))
        pl.when(jnp.logical_not(inside))(lambda: work(False))

    args = [moved, total, filters, table]
    if own:
        args += list(own)
    scratch = [pltpu.VMEM((rows, 2 * (blocks + 1) * block_len), f32)]
    out_shape = shape_of((rows, 2 * tokens), f32)
    if last is not None:
        inverse, query, gated, skip = last
        args += [inverse, query, gated, skip.reshape(1, -1)]
        out_shape = shape_of((rows, tokens), bf16)
        scratch.append(pltpu.VMEM((rows, 2 * tokens), f32))
    return pl.pallas_call(
        kernel,
        in_specs=[in_vmem] * len(args),
        out_specs=in_vmem,
        out_shape=out_shape,
        scratch_shapes=scratch[::-1],
        compiler_params=params,
        cost_estimate=estimate(0, 0),
        name=f"far_part_{turn}_{begin}",
    )(*args)


def from_before(block):
    count = lax.axis_size("ctx")
    return lax.ppermute(block, "ctx", [(i, (i + 1) % count) for i in range(count)])


def output_finish(channels, tokens):
    def body(total, side_sum, extra_refs, outs):
        outs[0][...] = total(0).astype(bf16)

    return body, [], [shape_of((channels, tokens), bf16)], None, False


def shards(activations, norm_gain, w_in, w_short, long_filter, skip_gain, w_out):
    channels, tokens = activations.shape
    features = w_in.shape[2]
    w_short = w_short.transpose(0, 2, 1)
    turns = lax.axis_size("ctx")
    parts = channel_parts(channels)
    forward, segments, inverse = (jnp.asarray(t) for t in dft_tables())
    own = prepare(activations, norm_gain)

    filters = filter_spectra(long_filter, segments)
    last, running, (filters,) = gather_products([own], w_in, [filters], True, "projection")

    def message(part, running):
        (sent,) = last(message_finish(features, w_short, tokens, part), running)
        return from_before(sent)

    exact = turns > 2
    moving = [message(0, running)]
    results = [last(projection_finish(features, w_short, tokens, k), running) for k in range(2)]
    projected, first_blocks, gated = zip(*results)
    later, gated = lax.optimization_barrier((running, gated))
    moving.append(message(1, later))
    query, totals, ready = own_part(
        projected, gated, moving if exact else None, w_short, filters, forward, inverse, skip_gain
    )
    if exact:
        gated = ready
        moving = [from_before(part) for part in gated]
    mixed = []
    for turn in range(1, turns):
        for k, (begin, _) in enumerate(parts):
            last = own_block = None
            if turn == turns - 1:
                last = (inverse, query[k], gated[k], skip_gain)
                if not exact:
                    own_block = (first_blocks[k], w_short, moving[0], ready[k])
            done = far_part(
                turn, begin, moving[k], totals[k], filters, forward, last, own_block
            )
            if last is None:
                totals[k] = done
                moving[k] = from_before(moving[k])
            else:
                mixed.append(done)

    last, running, _ = gather_products(mixed, w_out[None], [], False, "output")
    (result,) = last(output_finish(channels, tokens), running)
    return result


def solution(mesh):
    placed = (
        P("fsdp", "ctx"),
        P("fsdp"),
        P(None, "fsdp", None),
        P(None, "fsdp", None),
        P("fsdp", None),
        P("fsdp"),
        P("fsdp", None),
    )
    return jax.shard_map(
        shards, mesh=mesh, in_specs=placed, out_specs=P("fsdp", "ctx"), check_vma=False
    )
```

```python
import math

import jax
import jax.numpy as jnp
import numpy as np
from jax import lax
from jax.experimental import pallas as pl
from jax.experimental.pallas import tpu as pltpu
from jax.sharding import PartitionSpec as P

epsilon = 1e-05
block_len = 128
STAGGER = 2e9
side_rows = 8
bf16 = jnp.bfloat16
f32 = jnp.float32
in_vmem = pl.BlockSpec(memory_space=pltpu.VMEM)
params = pltpu.CompilerParams(vmem_limit_bytes=12 * 2**20)


def shape_of(shape, dtype):
    return jax.ShapeDtypeStruct(tuple(shape), dtype)


def dot(left, right):
    return jnp.dot(left, right, preferred_element_type=f32)


def column(row):
    return jnp.broadcast_to(row, (8, row.shape[1])).T[:, :1]


def tap_columns(taps):
    return jnp.concatenate([taps, jnp.zeros((8 - taps.shape[0], taps.shape[1]), f32)], axis=0).T


def estimate(flops, size):
    return pl.CostEstimate(flops=int(flops), bytes_accessed=int(size), transcendentals=0)


def begin():
    def kernel(out_ref):
        out_ref[...] = jnp.zeros(out_ref.shape, f32)

    return pl.pallas_call(
        kernel,
        out_specs=in_vmem,
        out_shape=shape_of((8, 128), f32),
        compiler_params=params,
        cost_estimate=estimate(3e9, 0),
        name="begin",
    )()


def prepare_kernel(x_ref, gain_ref, begun_ref, out_ref):
    rows = x_ref.shape[0]
    wide = x_ref[...].astype(f32)
    out_ref[:rows] = (wide * column(gain_ref[...])).astype(bf16)
    squares = jnp.sum(wide * wide, axis=0, keepdims=True)
    high = squares.astype(bf16).astype(f32)
    row = lax.broadcasted_iota(jnp.int32, (side_rows, wide.shape[1]), 0)
    side = jnp.where(row == 0, high, jnp.where(row == 1, squares - high, 0.0))
    out_ref[rows:] = side.astype(bf16)


def prepare(x, gain):
    rows, tokens = x.shape
    return pl.pallas_call(
        prepare_kernel,
        in_specs=[in_vmem, in_vmem, in_vmem],
        out_specs=in_vmem,
        out_shape=shape_of((rows + side_rows, tokens), bf16),
        compiler_params=params,
        cost_estimate=estimate(3e9, 0),
        name="prepare",
    )(x, gain.reshape(1, rows), begin())


def chip_count():
    return lax.axis_size("fsdp") // 2


def ring_order(count):
    return list(range(0, count, 2)) + list(range(1, count, 2))[::-1]


def along_ring(block):
    chips = chip_count()
    order = ring_order(chips)
    pairs = []
    for i in range(chips):
        here, after = order[i], order[(i + 1) % chips]
        pairs += [(2 * here, 2 * after), (2 * after + 1, 2 * here + 1)]
    return lax.ppermute(block, "fsdp", pairs)


def other_core(block):
    return lax.ppermute(block, "fsdp", [(i, i ^ 1) for i in range(2 * chip_count())])


def my_core():
    return lax.axis_index("fsdp") & 1


def source_chip(steps):
    chips = chip_count()
    chip = lax.shift_right_logical(lax.axis_index("fsdp"), 1)
    half = lax.shift_right_logical(chip, 1)
    place = jnp.where(chip & 1 == 0, half, chips - 1 - half)
    place = place + jnp.where(my_core() == 0, chips - steps, steps)
    place = jnp.where(place >= chips, place - chips, place)
    return jnp.where(place < (chips + 1) // 2, 2 * place, 2 * (chips - 1 - place) + 1)


def take_from(refs, number):
    return [refs.pop(0) for _ in range(number)]


def products(items, weight, running, side, finish, cost, name):
    body, extras, out_shape, cut, senders_only = finish or (None, [], None, None, False)
    streams, out_rows, features = weight.shape
    cut = cut or (0, out_rows)
    out_here, out_rows = slice(cut[0], cut[0] + cut[1]), cut[1]
    rows = features // lax.axis_size("fsdp")
    shards = [piece for _, _, pieces in items for piece in pieces]
    tokens = shards[0].shape[1]
    count = len(shards)
    first_group = running is None
    state = [] if first_group else list(running)
    padded = rows % 128 != 0
    width = 2 * rows if padded else rows
    scratch_shapes = [pltpu.VMEM((len(items) * width, tokens), bf16)] if padded else []

    def kernel(*refs):
        refs = list(refs)
        take = lambda n: take_from(refs, n)
        shard_refs = take(count)
        (weight_ref,) = take(1)
        state_refs = take(len(state))
        extra_refs = take(len(extras))
        outs = take(len(out_shape))

        def work():
            core = my_core()
            chip_of = {steps: source_chip(steps) for steps in sorted({item[0] for item in items})}
            if padded:
                (beside_ref,) = refs
                beside_ref[...] = jnp.zeros(beside_ref.shape, bf16)
            sides, right = [], []
            pieces_left = list(shard_refs)
            for k, (_, other, pieces) in enumerate(items):
                done = 0
                for piece_ref in take_from(pieces_left, len(pieces)):
                    more = min(piece_ref.shape[0], rows - done)
                    if padded:
                        at = k * width + jnp.where(core == other, 0, rows) + done
                        at = pl.multiple_of(at, math.gcd(rows, done or rows))
                        beside_ref[pl.ds(at, more)] = piece_ref[:more]
                    else:
                        right.append(piece_ref[:more])
                    if more < piece_ref.shape[0]:
                        sides.append(piece_ref[more:].astype(f32))
                    done += more
            right = beside_ref[...] if padded else jnp.concatenate(right, axis=0)
            side_sum = None
            if side:
                parts = sides + ([] if first_group else [state_refs[1][...]])
                side_sum = sum(parts[1:], parts[0])

            def total(stream, lanes=slice(None), out_here=out_here):
                left = []
                for steps, other, _ in items:
                    block = chip_of[steps]
                    if not padded:
                        block = 2 * block + (1 - core if other else core)
                    at = pl.ds(pl.multiple_of(block * width, width), width)
                    left.append(weight_ref[stream, out_here, at])
                product = dot(jnp.concatenate(left, axis=1), right[:, lanes])
                if first_group:
                    return product
                return state_refs[0][stream, out_here, lanes] + product

            if body is not None:
                body(total, side_sum, extra_refs, outs)
                return
            for stream in range(streams):
                outs[0][stream] = total(stream)
            if side:
                outs[1][...] = side_sum

        if senders_only:
            pl.when(lax.axis_index("ctx") < lax.axis_size("ctx") - 1)(work)
        else:
            work()

    aliases = {}
    if body is None:
        out_shape = [shape_of((streams, out_rows, tokens), f32)]
        if side:
            out_shape.append(shape_of((side_rows, tokens), f32))
        if not first_group:
            aliases = {count + 1 + i: i for i in range(len(state))}
    return pl.pallas_call(
        kernel,
        in_specs=[in_vmem] * (count + 1 + len(state) + len(extras)),
        out_specs=[in_vmem] * len(out_shape),
        out_shape=out_shape,
        scratch_shapes=scratch_shapes,
        input_output_aliases=aliases,
        compiler_params=params,
        cost_estimate=estimate(cost, 0),
        name=name,
    )(*shards, weight, *state, *extras)


def pass_on(near, far):
    rows = near.shape[0] - side_rows

    def kernel(near_ref, far_ref, out_ref):
        out_ref[:rows] = near_ref[:rows]
        below = pltpu.roll(far_ref[rows:].astype(f32), 2, 0)
        out_ref[rows:] = (near_ref[rows:].astype(f32) + below).astype(bf16)

    return pl.pallas_call(
        kernel,
        in_specs=[in_vmem, in_vmem],
        out_specs=in_vmem,
        out_shape=shape_of(near.shape, bf16),
        compiler_params=params,
        cost_estimate=estimate(0, 0),
        name="pass_on",
    )(near, far)


def gather_products(own, weight, beside, side, name):
    chips = chip_count()
    last_step = chips // 2

    def send(way, pieces, scope):
        sent = []
        for k, piece in enumerate(pieces):
            with jax.named_scope(f"{name}_{scope}_{k}"):
                sent.append(way(piece))
        return sent

    def joined(pieces):
        return [jnp.concatenate(pieces, axis=0)] if len(pieces) > 1 else pieces

    near, far = own, send(other_core, own, "core_own")
    items = [(0, 0, near), (0, 1, far)]
    sibling = far
    if side:
        far = [far[0][: far[0].shape[0] - side_rows]]
    running = None
    for step in range(1, last_step + 1):
        near = joined(send(along_ring, near, f"near_{step}"))
        arrived = near
        if running is not None:
            arrived, running = lax.optimization_barrier((near, running))
        elif beside:
            arrived, beside = lax.optimization_barrier((near, beside))
        theirs = send(other_core, arrived, f"core_near_{step}")
        pair = [(step, 0, arrived), (chips - step, 1, theirs)]
        if step < last_step:
            running = products(items + pair, weight, running, side, None, 0, f"{name}_{step}")
            if side and step == 1:
                near = [pass_on(near[0], sibling[0])]
            far = joined(send(along_ring, far, f"far_{step}"))
            theirs = send(other_core, far, f"core_far_{step}")
            items = [(step, 1, far), (chips - step, 0, theirs)]
        else:
            items.append(pair[0])
            running = products(items, weight, running, side, None, STAGGER, f"{name}_{step}")
            items = pair[1:]

    def last(finish, running):
        return products(items, weight, running, side, finish, 0, f"{name}_last")

    return last, running, beside


def smooth(projected, taps, count, halo):
    lane = lax.broadcasted_iota(jnp.int32, projected.shape, 1)
    out = taps[:, :1] * projected
    for tap in range(1, count):
        moved = pltpu.roll(projected, tap, 1)
        for place in range(tap):
            edge = 0.0
            if halo is not None:
                at = halo.shape[1] - tap + place
                edge = halo[:, at : at + 1]
            moved = jnp.where(lane == place, edge, moved)
        out = out + taps[:, tap : tap + 1] * moved
    return out


def channel_parts(channels):
    first = channels * 4 // 8 // 16 * 16
    return [(0, first), (first, channels - first)]


def norm_factor(side_sum, features):
    mean = jnp.sum(side_sum, axis=0, keepdims=True) * (1.0 / features)
    return lax.rsqrt(mean + epsilon)


def gate(projected, taps_ref, begin, write):
    count = taps_ref.shape[1]
    columns = [tap_columns(taps_ref[stream]) for stream in (1, 2)]
    rows = projected[0].shape[0]
    tile = math.gcd(rows, 64)
    for start in range(0, rows, tile):
        here = slice(start, start + tile)
        there = slice(begin + start, begin + start + tile)
        key, value = (
            smooth(wide[here].astype(f32), column[there], count, None)
            for wide, column in zip(projected, columns)
        )
        write(here, key, value)


def message_finish(features, w_short, tokens, part):
    streams, count, channels = w_short.shape
    parts = channel_parts(channels)
    begin, rows = parts[part]
    last = slice(tokens - block_len, tokens)

    def body(total, side_sum, extra_refs, outs):
        (taps_ref,), (message_ref,) = extra_refs, outs
        factor = norm_factor(side_sum, features)
        projected = [(total(stream) * factor).astype(bf16) for stream in (1, 2)]

        def write(here, key, value):
            message_ref[here] = (key * value).astype(bf16)

        gate(projected, taps_ref, begin, write)
        if part == 0:
            lines = []
            for stream in range(streams):
                end = (total(stream, last, slice(0, channels)) * factor[:, last]).astype(bf16)
                lines.append(end.astype(f32).T[block_len - count + 1 :])
            lines.append(jnp.zeros((side_rows - streams * (count - 1), channels), f32))
            message_ref[rows:] = jnp.zeros((side_rows, tokens), bf16)
            message_ref[rows:, :channels] = jnp.concatenate(lines, axis=0).astype(bf16)

    out_shape = [shape_of((rows + (side_rows if part == 0 else 0), tokens), bf16)]
    return body, [w_short], out_shape, parts[part], True


def projection_finish(features, w_short, tokens, part):
    streams, _, channels = w_short.shape
    parts = channel_parts(channels)
    begin, rows = parts[part]

    def body(total, side_sum, extra_refs, outs):
        (taps_ref,), (projected_ref, first_ref, gated_ref) = extra_refs, outs
        factor = norm_factor(side_sum, features)
        projected = [(total(stream) * factor).astype(bf16) for stream in range(streams)]
        for stream in range(streams):
            projected_ref[stream] = projected[stream]

        def write(here, key, value):
            first_ref[0, here] = key[:, :block_len]
            first_ref[1, here] = value[:, :block_len]
            gated_ref[here] = (key * value).astype(bf16)

        gate(projected[1:], taps_ref, begin, write)

    out_shape = [
        shape_of((streams, rows, tokens), bf16),
        shape_of((2, rows, block_len), f32),
        shape_of((rows, tokens), bf16),
    ]
    return body, [w_short], out_shape, parts[part], False


def halo_columns(message_ref, streams, count, channels, inside):
    side = message_ref[message_ref.shape[0] - side_rows :, :channels].astype(f32)
    side = jnp.where(inside, side, 0.0).T
    return [side[:, s * (count - 1) : (s + 1) * (count - 1)] for s in range(streams)]


def halo_edges(message_ref, taps, begin):
    streams, count, rows = taps.shape
    side = message_ref[message_ref.shape[0] - side_rows :, begin : begin + rows].astype(f32)
    lines = []
    for s in range(streams):
        for token in range(count - 1):
            line = jnp.zeros((1, rows), f32)
            for tap in range(token + 1, count):
                at = s * (count - 1) + count - 1 + token - tap
                line = line + taps[s, tap : tap + 1] * side[at : at + 1]
            lines.append(line)
    lines.append(jnp.zeros((-len(lines) % 8, rows), f32))
    columns = jnp.concatenate(lines, axis=0).T
    lane = lax.broadcasted_iota(jnp.int32, (rows, block_len), 1)
    edges = []
    for s in range(streams):
        edge = jnp.zeros((rows, block_len), f32)
        for token in range(count - 1):
            at = s * (count - 1) + token
            edge = jnp.where(lane == token, columns[:, at : at + 1], edge)
        edges.append(edge)
    return edges


def split_table(table):
    high = table.astype(bf16)
    return high, (table - high.astype(np.float64)).astype(bf16)


def dft_tables():
    size = 2 * block_len
    freq = np.arange(block_len) + 0.5
    angle = 2.0 * math.pi / size * np.arange(size)[:, None] * freq[None, :]
    high, low = split_table(np.concatenate([np.cos(angle), -np.sin(angle)], axis=1))
    block = np.concatenate([high[:block_len], low[:block_len]])
    segment = np.concatenate([high, low])
    back = angle[block_len:].T
    inverse = np.concatenate([np.cos(back), -np.sin(back)], axis=0) * (2.0 / size)
    high, low = split_table(inverse)
    return block, segment, np.concatenate([high, low], axis=1)


def spectrum_lanes(k):
    return slice(2 * k * block_len, 2 * (k + 1) * block_len)


def block_lanes(k):
    return slice(k * block_len, (k + 1) * block_len)


def filter_spectra(long_filter, table):
    channels, lags = long_filter.shape

    def kernel(filter_ref, table_ref, spectra_ref):
        before = jnp.zeros((channels, block_len), bf16)
        for k in range(lags // block_len):
            now = filter_ref[:, block_lanes(k)]
            segment = jnp.concatenate([before, now, before, now], axis=1)
            spectra_ref[:, spectrum_lanes(k)] = dot(segment, table_ref[...])
            before = now

    return pl.pallas_call(
        kernel,
        in_specs=[in_vmem, in_vmem],
        out_specs=in_vmem,
        out_shape=shape_of((channels, 2 * lags), f32),
        compiler_params=params,
        cost_estimate=estimate(6e9, 0),
        name="filter_spectra",
    )(long_filter, table)


def block_spectra(pieces, table_ref, spec_ref, first):
    rows = pieces[0].shape[0]
    stacked = jnp.concatenate(pieces, axis=0)
    spectra = dot(jnp.concatenate([stacked, stacked], axis=1), table_ref[...])
    for k in range(len(pieces)):
        spec_ref[:rows, spectrum_lanes(first + k)] = spectra[k * rows : (k + 1) * rows]


def multiply_spectra(source_ref, filters_ref, filter_start, pairs, before_ref, total_ref):
    used = [term for terms in pairs for term in terms]
    for start in range(0, total_ref.shape[0], 8):
        here = slice(start, start + 8)
        there = slice(filter_start + start, filter_start + start + 8)

        def parts(ref, rows, k):
            return ref[rows, block_lanes(2 * k)], ref[rows, block_lanes(2 * k + 1)]

        sources = {b: parts(source_ref, here, b) for b in sorted({b for b, _ in used})}
        filters = {d: parts(filters_ref, there, d) for d in sorted({d for _, d in used})}
        for a, terms in enumerate(pairs):
            real = imag = None
            if before_ref is not None:
                real, imag = parts(before_ref, here, a)
            for b, d in terms:
                gr, gi = sources[b]
                hr, hi = filters[d]
                more_real, more_imag = gr * hr - gi * hi, gr * hi + gi * hr
                real = more_real if real is None else real + more_real
                imag = more_imag if imag is None else imag + more_imag
            if real is None:
                real = imag = jnp.zeros((8, block_len), f32)
            total_ref[here, block_lanes(2 * a)] = real
            total_ref[here, block_lanes(2 * a + 1)] = imag


def mix(sum_ref, back_ref, query, gated, skip, out_ref):
    rows = out_ref.shape[0]
    spectra = [sum_ref[:, spectrum_lanes(a)] for a in range(len(query))]
    highs = [spectrum.astype(bf16) for spectrum in spectra]
    lows = [(s - high.astype(f32)).astype(bf16) for s, high in zip(spectra, highs)]
    both = dot(jnp.concatenate(highs, axis=0), back_ref[...])
    small = dot(jnp.concatenate(lows, axis=0), back_ref[:, :block_len])
    filtered = both[:, :block_len] + (both[:, block_len:] + small)
    for a in range(len(query)):
        here = filtered[a * rows : (a + 1) * rows]
        mixed = query[a] * (here + skip * gated[a].astype(f32))
        out_ref[:, block_lanes(a)] = mixed.astype(bf16)


def own_part(projected, alone, moved, taps, filters, table, inverse, skip):
    streams, _, tokens = projected[0].shape
    parts = channel_parts(taps.shape[2])
    number = len(parts)
    count = taps.shape[1]
    blocks = tokens // block_len
    first = 0 if moved else 1
    pairs = [[(b, a - b) for b in range(first, a + 1)] for a in range(blocks)]

    def kernel(*refs):
        refs = list(refs)
        take = lambda n: take_from(refs, n)
        projected_refs, message_refs = take(number), take(number)
        taps_ref, filters_ref, table_ref, back_ref, skip_ref = take(5)
        query_refs, total_refs = take(number), take(number)
        gated_refs = take(number)
        (spec_ref,) = refs
        columns = [tap_columns(taps_ref[s]) for s in range(streams)]
        if moved:
            inside = lax.axis_index("ctx") > 0
            halo = halo_columns(message_refs[0], streams, count, taps_ref.shape[2], inside)
        for part, (begin, rows) in enumerate(parts):
            tile = math.gcd(rows, 64)
            for start in range(0, rows, tile):
                here = slice(start, start + tile)
                there = slice(begin + start, begin + start + tile)
                projected_ref = projected_refs[part]

                def smoothed(s):
                    edge = halo[s][there] if moved else None
                    wide = projected_ref[s, here].astype(f32)
                    return smooth(wide, columns[s][there], count, edge)

                query_refs[part][here] = smoothed(0)
                if moved:
                    gated_refs[part][here] = (smoothed(1) * smoothed(2)).astype(bf16)
            source_ref = gated_refs[part] if moved else message_refs[part]
            pieces = [source_ref[:rows, block_lanes(b)] for b in range(first, blocks)]
            block_spectra(pieces, table_ref, spec_ref, first)
            multiply_spectra(spec_ref, filters_ref, begin, pairs, None, total_refs[part])
            if not moved:

                @pl.when(lax.axis_index("ctx") == 0)
                def _():
                    lanes = [block_lanes(a) for a in range(blocks)]
                    block_spectra([source_ref[:rows, lanes[0]]], table_ref, spec_ref, 0)
                    sum_ref = total_refs[part]
                    first_pairs = [[(0, a)] for a in range(blocks)]
                    multiply_spectra(spec_ref, filters_ref, begin, first_pairs, sum_ref, sum_ref)
                    query = [query_refs[part][:, at] for at in lanes]
                    gated = [source_ref[:rows, at] for at in lanes]
                    column_here = column(skip_ref[...])[begin : begin + rows]
                    mix(sum_ref, back_ref, query, gated, column_here, gated_refs[part])

    out_shape = [shape_of((rows, tokens), f32) for _, rows in parts]
    out_shape += [shape_of((rows, 2 * tokens), f32) for _, rows in parts]
    out_shape += [shape_of((rows, tokens), bf16) for _, rows in parts]
    inputs = [*projected, *(moved or alone), taps, filters, table, inverse, skip.reshape(1, -1)]
    outs = pl.pallas_call(
        kernel,
        in_specs=[in_vmem] * len(inputs),
        out_specs=[in_vmem] * len(out_shape),
        out_shape=out_shape,
        scratch_shapes=[pltpu.VMEM((max(rows for _, rows in parts), 2 * tokens), f32)],
        compiler_params=params,
        cost_estimate=estimate(0, 0),
        name="own_part",
    )(*inputs)
    gated = list(outs[2 * number :])
    return list(outs[:number]), list(outs[number : 2 * number]), gated


def far_part(turn, begin, moved, total, filters, table, last, own):
    rows, tokens = total.shape[0], moved.shape[1]
    blocks = tokens // block_len
    far_pairs = [[(b, turn * blocks + a - b) for b in range(blocks)] for a in range(blocks)]
    channels_here = slice(begin, begin + rows)

    def kernel(*refs):
        refs = list(refs)
        take = lambda n: take_from(refs, n)
        moved_ref, total_ref, filters_ref, table_ref = take(4)
        own_refs = take(4) if own else None
        spec_ref = refs.pop()
        sum_ref = refs.pop()
        if last:
            last_refs = take(4)
            (out_ref,) = refs

        def work(inside):
            pieces = [moved_ref[:rows, block_lanes(b)] for b in range(blocks)] if inside else []
            pairs = far_pairs if inside else [[] for _ in range(blocks)]
            if last:
                back_ref, query_ref, gated_ref, skip_ref = last_refs
                query, gated = (
                    [ref[:rows, block_lanes(a)] for a in range(blocks)]
                    for ref in (query_ref, gated_ref)
                )
            if own:
                first_ref, taps_ref, halo_ref, ready_ref = own_refs
                if not inside:
                    out_ref[...] = ready_ref[...]
                    return
                key, value = first_ref[0], first_ref[1]
                if inside:
                    edges = halo_edges(halo_ref, taps_ref[:, :, channels_here], begin)
                    query[0] = query[0] + edges[0]
                    key, value = key + edges[1], value + edges[2]
                gated[0] = (key * value).astype(bf16)
                pairs = [terms + [(len(pieces), a)] for a, terms in enumerate(pairs)]
                pieces.append(gated[0])
            if pieces:
                block_spectra(pieces, table_ref, spec_ref, 0)
            multiply_spectra(spec_ref, filters_ref, begin, pairs, total_ref, sum_ref)
            if not last:
                return
            mix(sum_ref, back_ref, query, gated, column(skip_ref[...])[channels_here], out_ref)

        inside = lax.axis_index("ctx") >= turn
        pl.when(inside)(lambda: work(True))
        pl.when(jnp.logical_not(inside))(lambda: work(False))

    args = [moved, total, filters, table]
    if own:
        args += list(own)
    scratch = [pltpu.VMEM((rows, 2 * (blocks + 1) * block_len), f32)]
    out_shape = shape_of((rows, 2 * tokens), f32)
    if last is not None:
        inverse, query, gated, skip = last
        args += [inverse, query, gated, skip.reshape(1, -1)]
        out_shape = shape_of((rows, tokens), bf16)
        scratch.append(pltpu.VMEM((rows, 2 * tokens), f32))
    return pl.pallas_call(
        kernel,
        in_specs=[in_vmem] * len(args),
        out_specs=in_vmem,
        out_shape=out_shape,
        scratch_shapes=scratch[::-1],
        compiler_params=params,
        cost_estimate=estimate(0, 0),
        name=f"far_part_{turn}_{begin}",
    )(*args)


def from_before(block):
    count = lax.axis_size("ctx")
    return lax.ppermute(block, "ctx", [(i, (i + 1) % count) for i in range(count)])


def output_finish(channels, tokens):
    def body(total, side_sum, extra_refs, outs):
        outs[0][...] = total(0).astype(bf16)

    return body, [], [shape_of((channels, tokens), bf16)], None, False


def shards(activations, norm_gain, w_in, w_short, long_filter, skip_gain, w_out):
    channels, tokens = activations.shape
    features = w_in.shape[2]
    w_short = w_short.transpose(0, 2, 1)
    turns = lax.axis_size("ctx")
    parts = channel_parts(channels)
    forward, segments, inverse = (jnp.asarray(t) for t in dft_tables())
    own = prepare(activations, norm_gain)

    filters = filter_spectra(long_filter, segments)
    last, running, (filters,) = gather_products([own], w_in, [filters], True, "projection")

    def message(part, running):
        (sent,) = last(message_finish(features, w_short, tokens, part), running)
        return from_before(sent)

    exact = turns > 2
    moving = [message(0, running)]
    results = [last(projection_finish(features, w_short, tokens, k), running) for k in range(2)]
    projected, first_blocks, gated = zip(*results)
    moving.append(message(1, running))
    query, totals, ready = own_part(
        projected, gated, moving if exact else None, w_short, filters, forward, inverse, skip_gain
    )
    if exact:
        gated = ready
        moving = [from_before(part) for part in gated]
    mixed = []
    for turn in range(1, turns):
        for k, (begin, _) in enumerate(parts):
            last = own_block = None
            if turn == turns - 1:
                last = (inverse, query[k], gated[k], skip_gain)
                if not exact:
                    own_block = (first_blocks[k], w_short, moving[0], ready[k])
            done = far_part(
                turn, begin, moving[k], totals[k], filters, forward, last, own_block
            )
            if last is None:
                totals[k] = done
                moving[k] = from_before(moving[k])
            else:
                mixed.append(done)

    last, running, _ = gather_products(mixed, w_out[None], [], False, "output")
    (result,) = last(output_finish(channels, tokens), running)
    return result


def solution(mesh):
    placed = (
        P("fsdp", "ctx"),
        P("fsdp"),
        P(None, "fsdp", None),
        P(None, "fsdp", None),
        P("fsdp", None),
        P("fsdp"),
        P("fsdp", None),
    )
    return jax.shard_map(
        shards, mesh=mesh, in_specs=placed, out_specs=P("fsdp", "ctx"), check_vma=False
    )
```
